32 devices in a mesh: dp: 4 (over y, x), seq: 8 (over z, core).
Axes of the slice: x: 2, y: 2, z: 4, core: 2. Of those that a mesh axis runs over, the one named last changes fastest.
Arguments:
- tokens: bfloat16 [4, 1024, 768], P('dp', 'seq'), may hold values from -6 to 6
- tie_index: int32 [4], P('dp'), may hold values from 0 to 1, as said below
- first_gain: bfloat16 [2, 768], P(None, ('dp', 'seq')), may hold values from 0.25 to 1.75
- first_shift: bfloat16 [2, 768], P(None, ('dp', 'seq')), may hold values from -4 to 4
- qkv_weight: bfloat16 [2, 768, 2304], P(None, ('dp', 'seq')), may hold values from -0.21875 to 0.21875
- qv_bias: bfloat16 [2, 1536], P(None, ('dp', 'seq')), may hold values from -6 to 6
- out_weight: bfloat16 [2, 768, 768], P(None, ('dp', 'seq')), may hold values from -3 to 3
- out_bias: bfloat16 [2, 768], P(None, ('dp', 'seq')), may hold values from -4 to 4
- second_gain: bfloat16 [2, 768], P(None, ('dp', 'seq')), may hold values from 0.25 to 1.75
- second_shift: bfloat16 [2, 768], P(None, ('dp', 'seq')), may hold values from -4 to 4
- fc_weight: bfloat16 [2, 768, 3072], P(None, ('dp', 'seq')), may hold values from -0.21875 to 0.21875
- fc_bias: bfloat16 [2, 3072], P(None, ('dp', 'seq')), may hold values from -6 to 6
- proj_weight: bfloat16 [2, 3072, 768], P(None, ('dp', 'seq')), may hold values from -0.109375 to 0.109375
- proj_bias: bfloat16 [2, 768], P(None, ('dp', 'seq')), may hold values from -4 to 4
- cotangent: bfloat16 [4, 1024, 768], P('dp', 'seq'), may hold values from -6 to 6
Outputs:
- layer_out: bfloat16 [4, 1024, 768], P('dp', 'seq')
- input_grad: bfloat16 [4, 1024, 768], P('dp', 'seq')
- grad_first_gain: float32 [2, 768], P(None, ('dp', 'seq'))
- grad_first_shift: float32 [2, 768], P(None, ('dp', 'seq'))
- grad_qkv_weight: float32 [2, 768, 2304], P(None, ('dp', 'seq'))
- grad_qv_bias: float32 [2, 1536], P(None, ('dp', 'seq'))
- grad_out_weight: float32 [2, 768, 768], P(None, ('dp', 'seq'))
- grad_out_bias: float32 [2, 768], P(None, ('dp', 'seq'))
- grad_second_gain: float32 [2, 768], P(None, ('dp', 'seq'))
- grad_second_shift: float32 [2, 768], P(None, ('dp', 'seq'))
- grad_fc_weight: float32 [2, 768, 3072], P(None, ('dp', 'seq'))
- grad_fc_bias: float32 [2, 3072], P(None, ('dp', 'seq'))
- grad_proj_weight: float32 [2, 3072, 768], P(None, ('dp', 'seq'))
- grad_proj_bias: float32 [2, 768], P(None, ('dp', 'seq'))
The draws below stay inside these ranges and needn't reach their ends.
Inputs may be any that keep to these rules, and one draw needn't show every extreme that they name: `tie_index`: each of the 2 shared blocks is picked by exactly 2 sequences.
All inputs are finite; a program needn't handle non-finite values.
Results may differ from the reference program's by a relative error of at most 0.017.
Values may be sent and summed in bfloat16 or wider, within the bound.
No kernel may reach another device: no remote copies, remote signals or barrier semaphores. Data moves between devices by JAX's collectives and lax.ppermute only.
A program may use at most 384 MiB of HBM per device.

```python
import math
import jax
import jax.numpy as jnp
from jax import lax

D = 768
HEADS = 12
HEAD_DIM = 64
FF = 3072
NTIE = 2
BLOCK = 256
L = 1024
SEQS = 4


def draw_tie_index(key, part):
    order = jax.random.permutation(key, SEQS)
    return (order % NTIE).astype(jnp.int32)


def shard_levels(own_key, shape, cuts, least, high):
    factor_of = 1.0
    for axis_at, shards_of in cuts:
        heights = jax.random.uniform(jax.random.fold_in(jax.random.fold_in(own_key, 6), axis_at), (shards_of,), jnp.float32, least / len(cuts), high / len(cuts))
        factor_of = factor_of * jnp.repeat(jnp.exp(heights), shape[axis_at] // shards_of).reshape((-1,) + (1,) * (len(shape) - 1 - axis_at))
    return factor_of


def scatter_about(stream_key, extent, spread, reach, cuts=(), held_as=jnp.bfloat16):
    entries = spread * jax.random.normal(stream_key, extent, jnp.float32)
    if cuts:
        entries = entries * shard_levels(stream_key, extent, cuts, -0.22, 0.18)
    return jnp.clip(entries, -reach, reach).astype(held_as)


def setup_inputs(seed: int = 0) -> dict:
    key_list = jax.random.split(jax.random.key(seed), 16)
    tokens = scatter_about(key_list[0], (SEQS, L, D), 1.0, 6.0, ((0, 4), (1, 8)))
    tie_index = draw_tie_index(jax.random.fold_in(key_list[15], 71), 0)
    first_gain = jnp.clip(1.0 + 0.15 * jax.random.normal(key_list[2], (NTIE, D), jnp.float32), 0.25, 1.75).astype(jnp.bfloat16)
    first_shift = scatter_about(key_list[3], (NTIE, D), 0.3, 4.0, ((1, 32),))
    qkv_weight = scatter_about(key_list[4], (NTIE, D, 3 * D), D ** -0.5, 0.21875, ((1, 32),))
    qv_bias = scatter_about(key_list[5], (NTIE, 2 * D), 0.5, 6.0, ((1, 32),))
    out_weight = scatter_about(key_list[6], (NTIE, D, D), 4 ** -0.5, 3.0, ((1, 32),))
    out_bias = scatter_about(key_list[7], (NTIE, D), 0.3, 4.0, ((1, 32),))
    second_gain = jnp.clip(1.0 + 0.15 * jax.random.normal(key_list[8], (NTIE, D), jnp.float32), 0.25, 1.75).astype(jnp.bfloat16)
    second_shift = scatter_about(key_list[9], (NTIE, D), 0.3, 4.0, ((1, 32),))
    fc_weight = scatter_about(key_list[10], (NTIE, D, FF), D ** -0.5, 0.21875, ((1, 32),))
    fc_bias = scatter_about(key_list[11], (NTIE, FF), 0.5, 6.0, ((1, 32),))
    proj_weight = scatter_about(key_list[12], (NTIE, FF, D), FF ** -0.5, 0.109375, ((1, 32),))
    proj_bias = scatter_about(key_list[13], (NTIE, D), 0.3, 4.0, ((1, 32),))
    cotangent = scatter_about(key_list[14], (SEQS, L, D), 1.0, 6.0, ((0, 4), (1, 8)))
    return dict(tokens=tokens, tie_index=tie_index, first_gain=first_gain, first_shift=first_shift, qkv_weight=qkv_weight, qv_bias=qv_bias, out_weight=out_weight, out_bias=out_bias, second_gain=second_gain, second_shift=second_shift, fc_weight=fc_weight, fc_bias=fc_bias, proj_weight=proj_weight, proj_bias=proj_bias, cotangent=cotangent)


@jax.custom_vjp
def low(v):
    return lax.optimization_barrier(v.astype(jnp.bfloat16)).astype(jnp.float32)

@jax.custom_vjp
def low_back(v):
    return v

def low_keep(v):
    return (low(v), None)

def low_pass(kept, grad):
    return (grad,)

def back_keep(v):
    return (v, None)

def back_low(kept, grad):
    return (low(grad),)
low.defvjp(low_keep, low_pass)
low_back.defvjp(back_keep, back_low)
epsilon = 1e-05
neg_large = -1e+30
precise = lax.Precision.HIGHEST

def norm_apply(values, norm_gain, norm_shift):
    row_mean = lax.optimization_barrier(jnp.mean(values, -1, keepdims=True))
    centred = values - row_mean
    row_var = lax.optimization_barrier(jnp.mean(centred * centred, -1, keepdims=True))
    return centred * lax.rsqrt(row_var + epsilon) * norm_gain + norm_shift

def gelu_tanh(values):
    return jax.nn.gelu(values, approximate=True)

def attend(query_rows, key_rows, value_rows):
    score_scale = 1.0 / math.sqrt(HEAD_DIM)
    row_span = math.gcd(L, 512)
    key_block = jnp.arange(L).astype(jnp.int32) // BLOCK

    def one_block(first_row):
        queries = lax.dynamic_slice_in_dim(query_rows, first_row, row_span, 0)
        scores = jnp.einsum('qhe,khe->hqk', queries, key_rows, precision=precise) * score_scale
        scores = low_back(scores)
        query_block = (first_row + jnp.arange(row_span).astype(jnp.int32)) // BLOCK
        allowed = key_block[None, :] <= query_block[:, None]
        scores = jnp.where(allowed[None], scores, neg_large)
        top_score = lax.optimization_barrier(jnp.max(scores, -1, keepdims=True))
        exponent = jnp.exp(scores - top_score)
        attn_probs = exponent / lax.optimization_barrier(jnp.sum(exponent, -1, keepdims=True))
        return jnp.einsum('hqk,khe->qhe', low(attn_probs), value_rows, precision=precise)
    starts = (jnp.arange(L // row_span) * row_span).astype(jnp.int32)
    outputs = lax.map(jax.checkpoint(one_block), starts)
    return outputs.reshape(L, HEADS * HEAD_DIM)

def one_sequence(inputs, picked):
    first_gain, first_shift, qkv_weight, qv_bias, out_weight, out_bias, second_gain, second_shift, fc_weight, fc_bias, proj_weight, proj_bias = picked
    model_width = HEADS * HEAD_DIM
    head_shape = (L, HEADS, HEAD_DIM)
    normed = low(norm_apply(inputs, first_gain, first_shift))
    qkv_rows = jnp.dot(normed, qkv_weight, precision=precise)
    queries = low(low_back(qkv_rows[:, :model_width] + qv_bias[:model_width]))
    key_rows = low(low_back(qkv_rows[:, model_width:2 * model_width]))
    value_rows = low(low_back(qkv_rows[:, 2 * model_width:] + qv_bias[model_width:]))
    attended = attend(queries.reshape(head_shape), key_rows.reshape(head_shape), value_rows.reshape(head_shape))
    attended = low(low_back(attended))
    middle = inputs + low_back(jnp.dot(attended, out_weight, precision=precise)) + out_bias
    normed_two = low(norm_apply(middle, second_gain, second_shift))
    hidden_pre = low_back(jnp.dot(normed_two, fc_weight, precision=precise) + fc_bias)
    hidden = low(gelu_tanh(hidden_pre))
    return middle + low_back(jnp.dot(hidden, proj_weight, precision=precise)) + proj_bias

def reference(tokens, tie_index, first_gain, first_shift, qkv_weight, qv_bias, out_weight, out_bias, second_gain, second_shift, fc_weight, fc_bias, proj_weight, proj_bias, cotangent):
    params = (first_gain, first_shift, qkv_weight, qv_bias, out_weight, out_bias, second_gain, second_shift, fc_weight, fc_bias, proj_weight, proj_bias)
    params = tuple((stacked.astype(jnp.float32) for stacked in params))

    def forward(token_rows, weights):

        def seq_step(carried, seq_item):
            seq_rows, chosen = seq_item
            picked = tuple((stacked[chosen] for stacked in weights))
            return (carried, jax.checkpoint(one_sequence)(seq_rows, picked))
        unused, outputs = lax.scan(seq_step, jnp.zeros((), jnp.float32), (token_rows, tie_index))
        return outputs
    result, pullback = jax.vjp(forward, tokens.astype(jnp.float32), params)
    input_grad, param_grads = pullback(cotangent.astype(jnp.float32))
    return (result.astype(jnp.bfloat16), input_grad.astype(jnp.bfloat16), param_grads[0], param_grads[1], param_grads[2], param_grads[3], param_grads[4], param_grads[5], param_grads[6], param_grads[7], param_grads[8], param_grads[9], param_grads[10], param_grads[11])
```

```python
import functools
import math

import jax
import jax.numpy as jnp
from jax import lax
from jax.experimental import pallas as pl
from jax.experimental.pallas import tpu as pltpu
from jax.sharding import PartitionSpec as P

HEADS = 12
HEAD_DIM = 64
BLOCK = 256

epsilon = 1e-05
bf16 = jnp.bfloat16
f32 = jnp.float32


def dot(a, b, ca, cb):
    return lax.dot_general(a, b, (((ca,), (cb,)), ((), ())), preferred_element_type=f32)


def norm_parts(values):
    row_mean = jnp.mean(values, -1, keepdims=True)
    centred = values - row_mean
    row_var = jnp.mean(centred * centred, -1, keepdims=True)
    scale = lax.rsqrt(row_var + epsilon)
    return centred * scale, scale


def norm_back(normal, scale, gain, grad):
    scaled = grad * gain
    return scale * (
        scaled
        - jnp.mean(scaled, -1, keepdims=True)
        - normal * jnp.mean(scaled * normal, -1, keepdims=True)
    )


def head_mask(rows, width, head):
    lane = lax.broadcasted_iota(jnp.int32, (rows, width), 1)
    return (lane >= head * HEAD_DIM) & (lane < (head + 1) * HEAD_DIM)


def attend_kernel(masked, rank_ref, q_ref, k_ref, v_ref, w_ref, *refs):
    bias_ref = refs[0] if masked else None
    a_ref, *out_refs = refs[1:] if masked else refs
    sums_ref = out_refs.pop()
    chunks, group, size, width = k_ref.shape
    for chunk in range(chunks):
        count = (chunk + 1) * group * size
        keys = k_ref[: chunk + 1].reshape(count, width)
        values = v_ref[: chunk + 1].reshape(count, width)
        values_t = values.T
        query = q_ref[chunk]
        parts = []
        for head in range(width // HEAD_DIM):
            part = jnp.where(head_mask(size, width, head), query, jnp.zeros_like(query))
            scores = dot(keys, part, 1, 1)
            if masked:
                early = count - group * size
                scores = jnp.concatenate([scores[:early], scores[early:] + bias_ref[...]], 0) if early else scores + bias_ref[...]
            top = jnp.max(scores, 0, keepdims=True)
            raised = jnp.exp(scores - top)
            total = jnp.sum(raised, 0, keepdims=True)
            mixed = dot(
                values_t[head * HEAD_DIM : (head + 1) * HEAD_DIM], raised.astype(bf16), 1, 0
            )
            parts.append(mixed / total)
        attended = jnp.concatenate(parts, 0).T.astype(bf16)
        a_ref[chunk] = attended
        sums_ref[chunk] = dot(attended, w_ref[...], 1, 0).astype(bf16)
    rank = rank_ref[0]
    for step, out_ref in enumerate(out_refs):
        out_ref[...] = sums_ref[lax.rem(rank + step, chunks)]


def attend_back_kernel(masked, q_ref, k_ref, v_ref, g_ref, *refs):
    bias_ref = refs[0] if masked else None
    dq_ref, dk_ref, dv_ref = refs[1:] if masked else refs
    chunks, group, size, width = k_ref.shape
    heads = width // HEAD_DIM
    score_scale = 1.0 / math.sqrt(HEAD_DIM)
    for chunk in range(chunks - 1, -1, -1):
        count = (chunk + 1) * group * size
        keys = k_ref[: chunk + 1].reshape(count, width)
        values = v_ref[: chunk + 1].reshape(count, width)
        keys_t = keys.T
        query = q_ref[chunk]
        grad = g_ref[chunk]
        parts, probs_all, grads_all, query_all, grad_all = [], [], [], [], []
        for head in range(heads):
            lanes = head_mask(size, width, head)
            query_part = jnp.where(lanes, query, jnp.zeros_like(query))
            grad_part = jnp.where(lanes, grad, jnp.zeros_like(grad))
            scores = dot(keys, query_part, 1, 1)
            if masked:
                early = count - group * size
                scores = jnp.concatenate([scores[:early], scores[early:] + bias_ref[...]], 0) if early else scores + bias_ref[...]
            top = jnp.max(scores, 0, keepdims=True)
            raised = jnp.exp(scores - top)
            probs = raised * (1.0 / jnp.sum(raised, 0, keepdims=True))
            grad_probs = dot(values, grad_part, 1, 1)
            delta = jnp.sum(probs * grad_probs, 0, keepdims=True)
            grad_scores = (probs * (grad_probs - delta)).astype(bf16)
            parts.append(
                dot(keys_t[head * HEAD_DIM : (head + 1) * HEAD_DIM], grad_scores, 1, 0)
            )
            probs_all.append(probs.astype(bf16))
            grads_all.append(grad_scores)
            query_all.append(query_part)
            grad_all.append(grad_part)
        dq_ref[chunk] = (jnp.concatenate(parts, 0).T * score_scale).astype(bf16)
        key_grad = dot(jnp.concatenate(grads_all, 1), jnp.concatenate(query_all, 0), 1, 0)
        value_grad = dot(jnp.concatenate(probs_all, 1), jnp.concatenate(grad_all, 0), 1, 0)
        key_grad = key_grad.reshape(chunk + 1, group, size, width)
        value_grad = value_grad.reshape(chunk + 1, group, size, width)
        if chunk == chunks - 1:
            dk_ref[...] = key_grad
            dv_ref[...] = value_grad
        else:
            dk_ref[: chunk + 1] = dk_ref[: chunk + 1] + key_grad
            dv_ref[: chunk + 1] = dv_ref[: chunk + 1] + value_grad


VMEM = pl.BlockSpec(memory_space=pltpu.VMEM)
SMEM = pl.BlockSpec(memory_space=pltpu.SMEM)
PARAMS = pltpu.CompilerParams(vmem_limit_bytes=56 * 1024 * 1024)


def attend(rank, query, keys, values, weight, bias):
    chunks, group, size, width = keys.shape
    model = weight.shape[1]
    extra = () if bias is None else (bias,)
    outs = pl.pallas_call(
        functools.partial(attend_kernel, bias is not None),
        out_shape=[jax.ShapeDtypeStruct((chunks, size, width), bf16)]
        + [jax.ShapeDtypeStruct((size, model), bf16)] * chunks,
        in_specs=[SMEM] + [VMEM] * (4 + len(extra)),
        out_specs=[VMEM] * (1 + chunks),
        scratch_shapes=[pltpu.VMEM((chunks, size, model), bf16)],
        compiler_params=PARAMS,
        name="attend",
    )(rank, query, keys, values, weight, *extra)
    return outs[0], outs[1:]


def attend_back(query, keys, values, grad, bias):
    chunks, group, size, width = keys.shape
    extra = () if bias is None else (bias,)
    return pl.pallas_call(
        functools.partial(attend_back_kernel, bias is not None),
        out_shape=[
            jax.ShapeDtypeStruct((chunks, size, width), bf16),
            jax.ShapeDtypeStruct(keys.shape, f32),
            jax.ShapeDtypeStruct(keys.shape, f32),
        ],
        in_specs=[VMEM] * (4 + len(extra)),
        out_specs=[VMEM] * 3,
        compiler_params=PARAMS,
        name="attend_back",
    )(query, keys, values, grad, *extra)


def per_device(
    n_dp,
    n_seq,
    tokens,
    tie_index,
    first_gain,
    first_shift,
    qkv_weight,
    qv_bias,
    out_weight,
    out_bias,
    second_gain,
    second_shift,
    fc_weight,
    fc_bias,
    proj_weight,
    proj_bias,
    cotangent,
):
    ranks, planes, group = n_dp, n_dp, n_seq // n_dp
    axes = ("dp", "seq")
    size, model = tokens.shape[1:]
    ties, rows = qkv_weight.shape[:2]
    inner = fc_weight.shape[2]
    width = model // ranks
    part = inner // ranks
    heads_here = HEADS // ranks
    score_scale = 1.0 / math.sqrt(HEAD_DIM)
    rank = lax.axis_index("dp")
    place = lax.axis_index("seq")
    plane, member = place // group, place % group

    def route(where):
        pairs = []
        for a in range(ranks):
            for b in range(planes):
                for c in range(group):
                    x, y, z = where(a, b, c)
                    pairs.append(
                        (a * n_seq + b * group + c, x * n_seq + y * group + z)
                    )
        return pairs

    swap = route(lambda a, b, c: (b, a, c))
    to_rank = [route(lambda a, b, c, k=k: ((a + k) % ranks, b, c)) for k in range(ranks)]
    to_plane = [route(lambda a, b, c, k=k: (a, (b + k) % planes, c)) for k in range(planes)]
    to_member = [route(lambda a, b, c, k=k: (a, b, (c + k) % group)) for k in range(group)]

    def send(values, pairs):
        return lax.ppermute(values, axes, pairs)

    def pick(stacked, index, axis=0):
        return lax.dynamic_index_in_dim(stacked, index, axis, keepdims=False)

    def turn(parts, start):
        count = len(parts)
        if count == 1:
            return jnp.stack(parts)
        if count == 2:
            first = jnp.where(start == 0, parts[0], parts[1])
            second = jnp.where(start == 0, parts[1], parts[0])
            return jnp.stack([first, second])
        stacked = jnp.stack(parts + parts)
        return lax.dynamic_slice_in_dim(stacked, (count - start) % count, count, 0)

    def from_ranks(pieces):
        return turn(
            [pick(pieces, rank)]
            + [
                send(pick(pieces, (rank + ranks - k) % ranks), to_rank[ranks - k])
                for k in range(1, ranks)
            ],
            rank,
        )

    def from_planes(piece_of):
        return [piece_of(plane)] + [
            send(piece_of((plane + planes - k) % planes), to_plane[planes - k])
            for k in range(1, planes)
        ]

    def from_members(piece):
        return [piece] + [send(piece, to_member[group - k]) for k in range(1, group)]

    tie_parts = [tie_index] + [send(tie_index, to_rank[ranks - k]) for k in range(1, ranks)]
    tie_rel = jnp.concatenate(tie_parts)
    tie_of = lambda seq: tie_rel[(seq + ranks - rank) % ranks]
    chosen = tie_of(plane)

    tokens_own = send(tokens[0], swap)
    grad_own = send(cotangent[0], swap)

    small = jnp.concatenate(
        [
            first_gain,
            first_shift,
            out_bias,
            second_gain,
            second_shift,
            proj_bias,
            qv_bias,
            fc_bias,
        ],
        1,
    )
    extra = 8
    small_rows = jnp.pad(small[:, None], ((0, 0), (0, extra - 1), (0, 3 * width - small.shape[1])))
    qkv_cols = qkv_weight.reshape(ties, rows, 3, ranks, width).transpose(3, 0, 1, 2, 4)
    qkv_cols = qkv_cols.reshape(ranks, ties, rows, 3 * width)
    qkv_cols = jnp.concatenate(
        [qkv_cols, jnp.broadcast_to(small_rows[None], (ranks,) + small_rows.shape)], 2
    )
    fc_cols = fc_weight.reshape(ties, rows, ranks, part).transpose(2, 0, 1, 3)
    qkv_rank = from_ranks(qkv_cols)
    fc_rank = from_ranks(fc_cols)

    def whole(piece_of):
        planes_here = turn(from_planes(piece_of), plane)
        return turn(from_members(planes_here), member)

    qkv_all = whole(lambda seq: pick(qkv_rank, tie_of(seq), 1)).transpose(2, 1, 0, 3, 4)
    w_qkv = qkv_all[..., :rows, :].reshape(model, 3 * width)
    small_all = qkv_all[..., rows, : 12 * rows].reshape(-1, 12 * rows)
    vectors = small_all[:, : 6 * rows].reshape(-1, 6, rows).transpose(1, 0, 2).reshape(6, model)
    vectors = vectors.astype(f32)
    gain_one, shift_one, bias_out, gain_two, shift_two, bias_proj = [
        vectors[k : k + 1] for k in range(6)
    ]
    bias_qv = small_all[:, 6 * rows : 8 * rows].reshape(2, ranks, width).astype(f32)
    bias_qv = pick(bias_qv, rank, 1)
    bias_fc = pick(small_all[:, 8 * rows :].reshape(ranks, 1, part), rank).astype(f32)

    out_all = whole(lambda seq: pick(out_weight, tie_of(seq)))
    w_out = out_all.transpose(1, 0, 2, 3).reshape(width, model)
    fc_all = whole(lambda seq: pick(fc_rank, tie_of(seq), 1)).transpose(2, 1, 0, 3, 4)
    w_fc = fc_all.reshape(model, part)
    proj_all = whole(lambda seq: pick(proj_weight, tie_of(seq)))
    w_proj = proj_all.transpose(1, 0, 2, 3).reshape(part, model)

    tokens_all = lax.all_gather(tokens_own, "dp", axis=0, tiled=True)
    normal_all, _ = norm_parts(tokens_all.astype(f32))
    normed = (normal_all * gain_one + shift_one).astype(bf16)
    mixed = dot(normed, w_qkv, 1, 0)
    query = (mixed[:, :width] + bias_qv[:1]).astype(bf16)
    key = mixed[:, width : 2 * width].astype(bf16)
    value = (mixed[:, 2 * width :] + bias_qv[1:]).astype(bf16)
    query = (query * jnp.asarray(score_scale, bf16)).reshape(ranks, size, width)
    pair = jnp.stack([key, value]).reshape(2, ranks, size, width)
    pairs = jnp.stack(from_members(pair), 2)
    keys, values = pairs[0], pairs[1]
    bias = None
    if group * size > BLOCK:
        owners = (member + jnp.arange(group)) % group
        seen = owners // (BLOCK // size) <= member // (BLOCK // size)
        bias = jnp.repeat(jnp.where(seen, 0.0, -1e30), size)[:, None].astype(f32)
        bias = jnp.broadcast_to(bias, (group * size, size))
    attended, sums = attend(rank.reshape(1).astype(jnp.int32), query, keys, values, w_out, bias)

    def spread(parts):
        total = parts[0].astype(f32)
        for k in range(1, ranks):
            total = total + send(parts[k], to_rank[k]).astype(f32)
        return total

    def by_step(values):
        stacked = values.reshape(ranks, size, model)
        return [pick(stacked, (rank + k) % ranks) for k in range(ranks)]

    middle = tokens_own.astype(f32) + spread(sums) + bias_out
    normal_two, scale_two = norm_parts(middle)
    normed_two_own = (normal_two * gain_two + shift_two).astype(bf16)
    normed_two = lax.all_gather(normed_two_own, "dp", axis=0, tiled=True)
    grad_all = lax.all_gather(grad_own, "dp", axis=0, tiled=True)
    hidden_pre = dot(normed_two, w_fc, 1, 0) + bias_fc
    root = math.sqrt(2.0 / math.pi)
    squared = hidden_pre * hidden_pre
    bent = jnp.tanh(root * hidden_pre * (1.0 + 0.044715 * squared))
    hidden = (0.5 * hidden_pre * (1.0 + bent)).astype(bf16)
    slope = 0.5 * (1.0 + bent) + 0.5 * hidden_pre * (1.0 - bent * bent) * root * (
        1.0 + 3.0 * 0.044715 * squared
    )
    layer_sums = dot(hidden, w_proj, 1, 0).astype(bf16)
    layer_own = (middle + spread(by_step(layer_sums)) + bias_proj).astype(bf16)
    layer_out = send(layer_own, swap)[None]

    grad_hidden = dot(grad_all, w_proj, 1, 1)
    grad_pre = (grad_hidden * slope).astype(bf16)
    second_sums = dot(grad_pre, w_fc, 1, 1)
    grad_second = spread(by_step(second_sums.astype(bf16)))
    upstream = grad_own.astype(f32)
    grad_middle = upstream + norm_back(normal_two, scale_two, gain_two, grad_second)
    middle_low_own = grad_middle.astype(bf16)
    middle_low = lax.all_gather(middle_low_own, "dp", axis=0, tiled=True)
    grad_attended = dot(middle_low, w_out, 1, 1).astype(bf16).reshape(ranks, size, width)
    grad_query, grad_keys, grad_values = attend_back(query, keys, values, grad_attended, bias)
    pair = jnp.stack([grad_keys, grad_values])
    total = pair[:, :, 0]
    for k in range(1, group):
        total = total + send(pair[:, :, k].astype(bf16), to_member[k]).astype(f32)
    total = total.astype(bf16).reshape(2, ranks * size, width)
    grad_query = grad_query.reshape(ranks * size, width)
    grad_mixed = jnp.concatenate([grad_query, total[0], total[1]], 1)
    first_sums = dot(grad_mixed, w_qkv, 1, 1)
    grad_first = spread(by_step(first_sums.astype(bf16)))
    normal_one, scale_one = norm_parts(tokens_own.astype(f32))
    input_own = (grad_middle + norm_back(normal_one, scale_one, gain_one, grad_first)).astype(bf16)
    input_grad = send(input_own, swap)[None]

    def over_members(pieces):
        axis = pieces.ndim - 3
        total = pick(pieces, member, axis)
        for k in range(1, group):
            total = total + send(pick(pieces, (member + k) % group, axis), to_member[k])
        return total

    def over_planes(pieces):
        parts = [pick(pieces, plane)] + [
            send(pick(pieces, (plane + k) % planes), to_plane[k]) for k in range(1, planes)
        ]
        sums_here = []
        for block in range(ties):
            total = 0.0
            for k in range(planes):
                source = (plane + planes - k) % planes
                total = total + jnp.where(tie_of(source) == block, parts[k].astype(f32), 0.0)
            sums_here.append(total)
        return jnp.stack(sums_here)

    by_owner = (ranks, planes, group)
    grad_w_proj = dot(hidden, grad_all, 0, 0).reshape(planes, group, -1, model)
    grad_proj_weight = over_planes(over_members(grad_w_proj).astype(bf16))
    grad_w_fc = dot(normed_two, grad_pre, 0, 0).reshape(by_owner + (rows, part))
    fc_owner = over_members(grad_w_fc).astype(bf16).transpose(1, 0, 2, 3)
    fc_back = from_ranks(over_planes(fc_owner).astype(bf16).transpose(1, 0, 2, 3))
    grad_fc_weight = fc_back.transpose(1, 2, 0, 3).reshape(ties, rows, inner).astype(f32)
    attended_flat = attended.reshape(ranks * size, width)
    grad_w_out = dot(attended_flat, middle_low, 0, 0).reshape(planes, group, rows, model)
    grad_out_weight = over_planes(over_members(grad_w_out).astype(bf16))

    second_normal = normed_two.astype(f32)
    own_sums = jnp.stack([grad_middle.sum(0), upstream.sum(0)])
    vector_grads = jnp.stack(
        [
            jnp.sum(first_sums * normal_all, 0),
            jnp.sum(first_sums, 0),
            own_sums[0],
            jnp.sum(grad_second * normal_two, 0),
            jnp.sum(grad_second, 0),
            own_sums[1],
        ]
    )
    mine = jnp.arange(ranks) == rank
    qv_sums = jnp.stack([grad_query.astype(f32).sum(0), total[1].astype(f32).sum(0)])
    qv_sums = jnp.where(mine[None, :, None], qv_sums[:, None], 0.0).reshape(-1, 2 * rows)
    fc_sums = grad_pre.astype(f32).sum(0)
    fc_sums = jnp.where(mine[:, None], fc_sums[None], 0.0).reshape(-1, 4 * rows)
    vector_grads = vector_grads.reshape(6, -1, rows).transpose(1, 0, 2).reshape(-1, 6 * rows)
    small_grads = jnp.concatenate([vector_grads, qv_sums, fc_sums], 1)
    small_grads = jnp.pad(
        small_grads.reshape(by_owner + (1, 12 * rows)),
        ((0, 0),) * 3 + ((0, extra - 1), (0, 3 * width - 12 * rows)),
    )
    grad_w_qkv = dot(normed, grad_mixed, 0, 0).reshape(by_owner + (rows, 3 * width))
    qkv_owner = over_members(jnp.concatenate([grad_w_qkv, small_grads], 3)).astype(bf16)
    qkv_back = over_planes(qkv_owner.transpose(1, 0, 2, 3)).astype(bf16)
    qkv_back = from_ranks(qkv_back.transpose(1, 0, 2, 3)).astype(f32)
    grad_qkv_weight = qkv_back[:, :, :rows].reshape(ranks, ties, rows, 3, width)
    grad_qkv_weight = grad_qkv_weight.transpose(1, 2, 3, 0, 4).reshape(ties, rows, 3 * model)
    small_back = qkv_back[:, :, rows, : 12 * rows].sum(0)
    vec = [small_back[:, k * rows : (k + 1) * rows] for k in range(6)]
    return (
        layer_out,
        input_grad,
        vec[0],
        vec[1],
        grad_qkv_weight,
        small_back[:, 6 * rows : 8 * rows],
        grad_out_weight,
        vec[2],
        vec[3],
        vec[4],
        grad_fc_weight,
        small_back[:, 8 * rows :],
        grad_proj_weight,
        vec[5],
    )


def solution(mesh):
    both = ("dp", "seq")
    token_spec = P("dp", "seq", None)
    vector = P(None, both)
    matrix = P(None, both, None)
    param_specs = (
        vector,
        vector,
        matrix,
        vector,
        matrix,
        vector,
        vector,
        vector,
        matrix,
        vector,
        matrix,
        vector,
    )
    return jax.shard_map(
        functools.partial(per_device, mesh.shape["dp"], mesh.shape["seq"]),
        mesh=mesh,
        in_specs=(token_spec, P("dp")) + param_specs + (token_spec,),
        out_specs=(token_spec, token_spec) + param_specs,
        check_vma=False,
    )
```

```python
import functools
import math

import jax
import jax.numpy as jnp
from jax import lax
from jax.experimental import pallas as pl
from jax.experimental.pallas import tpu as pltpu
from jax.sharding import PartitionSpec as P

HEADS = 12
HEAD_DIM = 64
BLOCK = 256


epsilon = 1e-05
neg_large = -1e30


def norm_apply(values, norm_gain, norm_shift):
    row_mean = jnp.mean(values, -1, keepdims=True)
    centred = values - row_mean
    row_var = jnp.mean(centred * centred, -1, keepdims=True)
    return centred * lax.rsqrt(row_var + epsilon) * norm_gain + norm_shift


def gelu_tanh(values):
    return jax.nn.gelu(values, approximate=True)


def select_all(gathered, chosen):
    return tuple(
        (lax.dynamic_index_in_dim(stacked, chosen, 0, keepdims=False) for stacked in gathered)
    )


def add_block(totals, update, chosen):
    current = lax.dynamic_index_in_dim(totals, chosen, 0, keepdims=True)
    return lax.dynamic_update_index_in_dim(totals, current + update[None], chosen, 0)


def split_three(values):
    upper_part = values.astype(jnp.bfloat16)
    rest_one = values - lax.optimization_barrier(upper_part).astype(jnp.float32)
    middle_part = rest_one.astype(jnp.bfloat16)
    lower_part = (rest_one - lax.optimization_barrier(middle_part).astype(jnp.float32)).astype(
        jnp.bfloat16
    )
    return (upper_part, middle_part, lower_part)


def to_heads(flat_rows, head_count):
    return flat_rows.reshape(
        flat_rows.shape[0], flat_rows.shape[1], head_count, flat_rows.shape[2] // head_count
    )


def allowed_mask(query_pos, key_pos, block_len):
    return (key_pos[None, :] // block_len <= query_pos[:, None] // block_len)[None, :, None, :]


def make_forward_step(query_heads, positions, block_len, score_scale):
    last_block = positions[-1] // block_len
    head_count = query_heads.shape[2]

    def fold_step(carried, shard_piece, start_row):
        key_piece, value_piece = shard_piece
        key_count = key_piece.shape[1]
        step_len = math.gcd(key_count, 512)

        def one_part(fold_state, offset):
            key_heads = to_heads(
                lax.dynamic_slice_in_dim(key_piece, offset, step_len, 1), head_count
            )
            value_heads = to_heads(
                lax.dynamic_slice_in_dim(value_piece, offset, step_len, 1), head_count
            )
            key_pos = offset + jnp.arange(step_len, dtype=jnp.int32)

            def update(state_in):
                top_old, total_old, sum_old = state_in
                scores = (
                    jnp.einsum(
                        "sqhe,skhe->sqhk",
                        query_heads,
                        key_heads,
                        preferred_element_type=jnp.float32,
                    )
                    * score_scale
                )
                allowed = allowed_mask(positions, key_pos, block_len)
                top_new = jnp.maximum(top_old, jnp.max(jnp.where(allowed, scores, neg_large), -1))
                exp_scores = jnp.where(allowed, jnp.exp(scores - top_new[..., None]), 0.0)
                rescale = jnp.exp(top_old - top_new)
                total_new = total_old * rescale + jnp.sum(exp_scores, -1)
                sum_new = sum_old * rescale[..., None] + jnp.einsum(
                    "sqhk,skhe->sqhe",
                    exp_scores.astype(jnp.bfloat16),
                    value_heads,
                    preferred_element_type=jnp.float32,
                )
                return (top_new, total_new, sum_new)

            return (
                lax.cond(
                    offset // block_len <= last_block, update, lambda state_in: state_in, fold_state
                ),
                None,
            )

        offsets = jnp.arange(key_count // step_len, dtype=jnp.int32) * step_len
        return lax.scan(one_part, carried, offsets)[0]

    return fold_step


def make_query_step(
    query_heads, grad_heads, log_total, delta_rows, positions, block_len, score_scale
):
    last_block = positions[-1] // block_len
    head_count = query_heads.shape[2]

    def fold_step(carried, shard_piece, start_row):
        key_piece, value_piece = shard_piece
        key_count = key_piece.shape[1]
        step_len = math.gcd(key_count, 512)

        def one_part(fold_state, offset):
            key_heads = to_heads(
                lax.dynamic_slice_in_dim(key_piece, offset, step_len, 1), head_count
            )
            value_heads = to_heads(
                lax.dynamic_slice_in_dim(value_piece, offset, step_len, 1), head_count
            )
            key_pos = offset + jnp.arange(step_len, dtype=jnp.int32)

            def update(state_in):
                scores = (
                    jnp.einsum(
                        "sqhe,skhe->sqhk",
                        query_heads,
                        key_heads,
                        preferred_element_type=jnp.float32,
                    )
                    * score_scale
                )
                allowed = allowed_mask(positions, key_pos, block_len)
                probs_all = jnp.where(allowed, jnp.exp(scores - log_total[..., None]), 0.0)
                grad_probs = jnp.einsum(
                    "sqhe,skhe->sqhk", grad_heads, value_heads, preferred_element_type=jnp.float32
                )
                grad_scores = (probs_all * (grad_probs - delta_rows[..., None])).astype(
                    jnp.bfloat16
                )
                return state_in + jnp.einsum(
                    "sqhk,skhe->sqhe", grad_scores, key_heads, preferred_element_type=jnp.float32
                )

            return (
                lax.cond(
                    offset // block_len <= last_block, update, lambda state_in: state_in, fold_state
                ),
                None,
            )

        offsets = jnp.arange(key_count // step_len, dtype=jnp.int32) * step_len
        return lax.scan(one_part, carried, offsets)[0]

    return fold_step


def make_key_step(key_heads, value_heads, positions, block_len, score_scale):
    first_block = positions[0] // block_len
    head_count = key_heads.shape[2]

    def fold_step(carried, shard_piece, start_row):
        query_piece, grad_piece, stats_piece = shard_piece
        seq_count, query_count, model_width = query_piece.shape
        step_len = math.gcd(query_count, 512)

        def one_part(fold_state, offset):
            query_part = to_heads(
                lax.dynamic_slice_in_dim(query_piece, offset, step_len, 1), head_count
            )
            grad_part = to_heads(
                lax.dynamic_slice_in_dim(grad_piece, offset, step_len, 1), head_count
            )
            stats_part = lax.dynamic_slice_in_dim(stats_piece, offset, step_len, 1).astype(
                jnp.float32
            )
            stats_part = stats_part.reshape(seq_count, step_len, 6, head_count)
            log_total = stats_part[:, :, 0] + stats_part[:, :, 1] + stats_part[:, :, 2]
            delta_rows = stats_part[:, :, 3] + stats_part[:, :, 4] + stats_part[:, :, 5]
            query_pos = offset + jnp.arange(step_len, dtype=jnp.int32)

            def update(state_in):
                key_grad, value_grad = state_in
                scores = (
                    jnp.einsum(
                        "sqhe,skhe->sqhk", query_part, key_heads, preferred_element_type=jnp.float32
                    )
                    * score_scale
                )
                allowed = allowed_mask(query_pos, positions, block_len)
                probs_all = jnp.where(allowed, jnp.exp(scores - log_total[..., None]), 0.0)
                grad_probs = jnp.einsum(
                    "sqhe,skhe->sqhk", grad_part, value_heads, preferred_element_type=jnp.float32
                )
                grad_scores = (probs_all * (grad_probs - delta_rows[..., None])).astype(
                    jnp.bfloat16
                )
                value_grad = value_grad + jnp.einsum(
                    "sqhk,sqhe->skhe",
                    probs_all.astype(jnp.bfloat16),
                    grad_part,
                    preferred_element_type=jnp.float32,
                )
                key_grad = key_grad + jnp.einsum(
                    "sqhk,sqhe->skhe", grad_scores, query_part, preferred_element_type=jnp.float32
                )
                return (key_grad, value_grad)

            last_query = (offset + step_len - 1) // block_len
            return (
                lax.cond(last_query >= first_block, update, lambda state_in: state_in, fold_state),
                None,
            )

        offsets = jnp.arange(query_count // step_len, dtype=jnp.int32) * step_len
        return lax.scan(one_part, carried, offsets)[0]

    return fold_step


def per_device(
    tokens,
    tie_index,
    first_gain,
    first_shift,
    qkv_weight,
    qv_bias,
    out_weight,
    out_bias,
    second_gain,
    second_shift,
    fc_weight,
    fc_bias,
    proj_weight,
    proj_bias,
    cotangent,
):
    gathered = (
        lax.all_gather(first_gain, ("dp", "seq"), axis=1, tiled=True),
        lax.all_gather(first_shift, ("dp", "seq"), axis=1, tiled=True),
        lax.all_gather(qkv_weight, ("dp", "seq"), axis=1, tiled=True),
        lax.all_gather(qv_bias, ("dp", "seq"), axis=1, tiled=True),
        lax.all_gather(out_weight, ("dp", "seq"), axis=1, tiled=True),
        lax.all_gather(out_bias, ("dp", "seq"), axis=1, tiled=True),
        lax.all_gather(second_gain, ("dp", "seq"), axis=1, tiled=True),
        lax.all_gather(second_shift, ("dp", "seq"), axis=1, tiled=True),
        lax.all_gather(fc_weight, ("dp", "seq"), axis=1, tiled=True),
        lax.all_gather(fc_bias, ("dp", "seq"), axis=1, tiled=True),
        lax.all_gather(proj_weight, ("dp", "seq"), axis=1, tiled=True),
        lax.all_gather(proj_bias, ("dp", "seq"), axis=1, tiled=True),
    )
    seq_count, tok_count, model_width = tokens.shape
    head_count = HEADS
    block_len = BLOCK
    score_scale = 1.0 / math.sqrt(HEAD_DIM)
    positions = lax.axis_index("seq") * tok_count + jnp.arange(tok_count, dtype=jnp.int32)
    member = 0
    gain_one, shift_one, w_qkv, bias_qv = select_all(gathered[0:4], tie_index[member])
    inputs = tokens[member].astype(jnp.float32)
    normed = norm_apply(inputs, gain_one, shift_one).astype(jnp.bfloat16)
    qkv_rows = jnp.dot(normed, w_qkv, preferred_element_type=jnp.float32)
    normed_list = [normed]
    query_list = [(qkv_rows[:, :model_width] + bias_qv[:model_width]).astype(jnp.bfloat16)]
    key_list = [qkv_rows[:, model_width : 2 * model_width].astype(jnp.bfloat16)]
    value_list = [(qkv_rows[:, 2 * model_width :] + bias_qv[model_width:]).astype(jnp.bfloat16)]
    query_all = jnp.stack(query_list)
    key_all = jnp.stack(key_list)
    value_all = jnp.stack(value_list)
    query_heads = to_heads(query_all, head_count)
    head_dim = query_heads.shape[3]
    stat_shape = (seq_count, tok_count, head_count)
    start_state = (
        jnp.full(stat_shape, neg_large, jnp.float32),
        jnp.zeros(stat_shape, jnp.float32),
        jnp.zeros(stat_shape + (head_dim,), jnp.float32),
    )
    forward_step = make_forward_step(query_heads, positions, block_len, score_scale)
    top_score, total_weight, weighted_sum = forward_step(
        start_state,
        (
            lax.all_gather(key_all, "seq", axis=1, tiled=True),
            lax.all_gather(value_all, "seq", axis=1, tiled=True),
        ),
        jnp.int32(0),
    )
    attn_heads = weighted_sum / total_weight[..., None]
    log_total = top_score + jnp.log(total_weight)
    attended = attn_heads.reshape(seq_count, tok_count, model_width).astype(jnp.bfloat16)
    member = 0
    w_out, bias_out, gain_two, shift_two, w_fc, bias_fc, w_proj, bias_proj = select_all(
        gathered[4:12], tie_index[member]
    )
    inputs = tokens[member].astype(jnp.float32)
    middle = (
        inputs + jnp.dot(attended[member], w_out, preferred_element_type=jnp.float32) + bias_out
    )
    normed_two = norm_apply(middle, gain_two, shift_two).astype(jnp.bfloat16)
    hidden_pre = jnp.dot(normed_two, w_fc, preferred_element_type=jnp.float32) + bias_fc
    hidden = gelu_tanh(hidden_pre).astype(jnp.bfloat16)
    layer_rows = [
        (middle + jnp.dot(hidden, w_proj, preferred_element_type=jnp.float32) + bias_proj).astype(
            jnp.bfloat16
        )
    ]
    saved_mlp = [(middle, normed_two, hidden_pre, hidden)]
    layer_out = jnp.stack(layer_rows)
    whole_back = (
        lax.all_gather(first_gain, ("dp", "seq"), axis=1, tiled=True),
        lax.all_gather(first_shift, ("dp", "seq"), axis=1, tiled=True),
        lax.all_gather(qkv_weight, ("dp", "seq"), axis=1, tiled=True),
        lax.all_gather(qv_bias, ("dp", "seq"), axis=1, tiled=True),
        lax.all_gather(out_weight, ("dp", "seq"), axis=1, tiled=True),
        lax.all_gather(out_bias, ("dp", "seq"), axis=1, tiled=True),
        lax.all_gather(second_gain, ("dp", "seq"), axis=1, tiled=True),
        lax.all_gather(second_shift, ("dp", "seq"), axis=1, tiled=True),
        lax.all_gather(fc_weight, ("dp", "seq"), axis=1, tiled=True),
        lax.all_gather(fc_bias, ("dp", "seq"), axis=1, tiled=True),
        lax.all_gather(proj_weight, ("dp", "seq"), axis=1, tiled=True),
        lax.all_gather(proj_bias, ("dp", "seq"), axis=1, tiled=True),
    )
    grad_totals = [jnp.zeros(stacked.shape, jnp.float32) for stacked in whole_back]
    member = 0
    chosen = tie_index[member]
    w_out, bias_out, gain_two, shift_two, w_fc, bias_fc, w_proj, bias_proj = select_all(
        whole_back[4:12], chosen
    )
    middle, normed_two, hidden_pre, hidden = saved_mlp[member]
    upstream = cotangent[member].astype(jnp.float32)
    upstream_low = upstream.astype(jnp.bfloat16)
    grad_hidden = jnp.einsum("td,fd->tf", upstream_low, w_proj, preferred_element_type=jnp.float32)
    gelu_pull = jax.vjp(gelu_tanh, hidden_pre)[1]
    grad_pre = gelu_pull(grad_hidden)[0].astype(jnp.bfloat16)
    grad_normed = jnp.einsum("tf,df->td", grad_pre, w_fc, preferred_element_type=jnp.float32)
    norm_pull = jax.vjp(
        norm_apply, middle, gain_two.astype(jnp.float32), shift_two.astype(jnp.float32)
    )[1]
    grad_middle, grad_gain, grad_shift = norm_pull(grad_normed)
    grad_middle = grad_middle + upstream
    middle_low = grad_middle.astype(jnp.bfloat16)
    attn_grads = [
        jnp.einsum("te,de->td", middle_low, w_out, preferred_element_type=jnp.float32).astype(
            jnp.bfloat16
        )
    ]
    middle_grads = [grad_middle]
    updates = (
        jnp.einsum("td,te->de", attended[member], middle_low, preferred_element_type=jnp.float32),
        jnp.sum(grad_middle, 0),
        grad_gain,
        grad_shift,
        jnp.einsum("td,tf->df", normed_two, grad_pre, preferred_element_type=jnp.float32),
        jnp.sum(grad_pre.astype(jnp.float32), 0),
        jnp.einsum("tf,td->fd", hidden, upstream_low, preferred_element_type=jnp.float32),
        jnp.sum(upstream, 0),
    )
    for slot_index, update in enumerate(updates):
        grad_totals[4 + slot_index] = add_block(grad_totals[4 + slot_index], update, chosen)
    grad_attn_all = jnp.stack(attn_grads)
    grad_heads = to_heads(grad_attn_all, head_count)
    delta_rows = jnp.sum(grad_heads.astype(jnp.float32) * attn_heads, -1)
    query_step = make_query_step(
        query_heads, grad_heads, log_total, delta_rows, positions, block_len, score_scale
    )
    zero_heads = jnp.zeros(stat_shape + (head_dim,), jnp.float32)
    grad_query = query_step(
        zero_heads,
        (
            lax.all_gather(key_all, "seq", axis=1, tiled=True),
            lax.all_gather(value_all, "seq", axis=1, tiled=True),
        ),
        jnp.int32(0),
    )
    row_stats = jnp.stack(split_three(log_total) + split_three(delta_rows), 2).reshape(
        seq_count, tok_count, 6 * head_count
    )
    key_step = make_key_step(
        to_heads(key_all, head_count),
        to_heads(value_all, head_count),
        positions,
        block_len,
        score_scale,
    )
    grad_key, grad_value = key_step(
        (zero_heads, zero_heads),
        (
            lax.all_gather(query_all, "seq", axis=1, tiled=True),
            lax.all_gather(grad_attn_all, "seq", axis=1, tiled=True),
            lax.all_gather(row_stats, "seq", axis=1, tiled=True),
        ),
        jnp.int32(0),
    )
    flat_shape = (seq_count, tok_count, model_width)
    grad_query = (grad_query * score_scale).reshape(flat_shape).astype(jnp.bfloat16)
    grad_key = (grad_key * score_scale).reshape(flat_shape).astype(jnp.bfloat16)
    grad_value = grad_value.reshape(flat_shape).astype(jnp.bfloat16)
    member = 0
    chosen = tie_index[member]
    gain_one, shift_one, w_qkv, bias_qv = select_all(whole_back[0:4], chosen)
    grad_mixed = jnp.concatenate([grad_query[member], grad_key[member], grad_value[member]], 1)
    grad_normed = jnp.einsum("te,de->td", grad_mixed, w_qkv, preferred_element_type=jnp.float32)
    norm_pull = jax.vjp(
        norm_apply,
        tokens[member].astype(jnp.float32),
        gain_one.astype(jnp.float32),
        shift_one.astype(jnp.float32),
    )[1]
    grad_inputs, grad_gain, grad_shift = norm_pull(grad_normed)
    input_rows = [(grad_inputs + middle_grads[member]).astype(jnp.bfloat16)]
    updates = (
        grad_gain,
        grad_shift,
        jnp.einsum(
            "td,te->de", normed_list[member], grad_mixed, preferred_element_type=jnp.float32
        ),
        jnp.concatenate(
            [
                jnp.sum(grad_query[member].astype(jnp.float32), 0),
                jnp.sum(grad_value[member].astype(jnp.float32), 0),
            ]
        ),
    )
    for slot_index, update in enumerate(updates):
        grad_totals[slot_index] = add_block(grad_totals[slot_index], update, chosen)
    input_grad = jnp.stack(input_rows)
    shard_grads = tuple(
        (
            lax.psum_scatter(grad_totals[0], ("dp", "seq"), scatter_dimension=1, tiled=True),
            lax.psum_scatter(grad_totals[1], ("dp", "seq"), scatter_dimension=1, tiled=True),
            lax.psum_scatter(grad_totals[2], ("dp", "seq"), scatter_dimension=1, tiled=True),
            lax.psum_scatter(grad_totals[3], ("dp", "seq"), scatter_dimension=1, tiled=True),
            lax.psum_scatter(grad_totals[4], ("dp", "seq"), scatter_dimension=1, tiled=True),
            lax.psum_scatter(grad_totals[5], ("dp", "seq"), scatter_dimension=1, tiled=True),
            lax.psum_scatter(grad_totals[6], ("dp", "seq"), scatter_dimension=1, tiled=True),
            lax.psum_scatter(grad_totals[7], ("dp", "seq"), scatter_dimension=1, tiled=True),
            lax.psum_scatter(grad_totals[8], ("dp", "seq"), scatter_dimension=1, tiled=True),
            lax.psum_scatter(grad_totals[9], ("dp", "seq"), scatter_dimension=1, tiled=True),
            lax.psum_scatter(grad_totals[10], ("dp", "seq"), scatter_dimension=1, tiled=True),
            lax.psum_scatter(grad_totals[11], ("dp", "seq"), scatter_dimension=1, tiled=True),
        )
    )
    return (layer_out, input_grad) + shard_grads


bf16 = jnp.bfloat16
f32 = jnp.float32
SMALL = 64
score_scale = 1.0 / math.sqrt(HEAD_DIM)
gelu_root = math.sqrt(2.0 / math.pi)
gelu_cube = 0.044715
SMEM = pl.BlockSpec(memory_space=pltpu.SMEM)


def dot(a, b, ca=1, cb=0):
    return lax.dot_general(a, b, (((ca,), (cb,)), ((), ())), preferred_element_type=f32)


def norm_parts(values):
    row_mean = jnp.mean(values, -1, keepdims=True)
    centred = values - row_mean
    row_var = jnp.mean(centred * centred, -1, keepdims=True)
    scale = lax.rsqrt(row_var + epsilon)
    return centred * scale, scale


def norm_back(normal, scale, gain, grad):
    scaled = grad * gain
    return scale * (
        scaled
        - jnp.mean(scaled, -1, keepdims=True)
        - normal * jnp.mean(scaled * normal, -1, keepdims=True)
    )


def head_mask(rows, width, head):
    lane = lax.broadcasted_iota(jnp.int32, (rows, width), 1)
    return (lane >= head * HEAD_DIM) & (lane < (head + 1) * HEAD_DIM)


class Held:
    def __init__(self, ref, copy):
        self.ref, self.copy = ref, copy
        self.shape, self.dtype = ref.shape, ref.dtype

    def __getitem__(self, at):
        if self.copy is not None:
            self.copy.wait()
            self.copy = None
        return self.ref[at]


class Made:
    def __init__(self, ref, copy):
        self.ref, self.copy = ref, copy
        self.shape, self.dtype = ref.shape, ref.dtype
        self.flushed = False

    def __getitem__(self, at):
        return self.ref[at]

    def __setitem__(self, at, value):
        self.ref[at] = value

    def flush(self):
        if not self.flushed:
            self.copy.start()
            self.flushed = True


COST = 1.0


def run(kernel, outs, *args, scalars=(), scratch=(), us=1.0, name=None):
    shapes = [jax.ShapeDtypeStruct(shape, dtype) for shape, dtype in outs]
    far = [k for k in range(len(args)) if k not in scalars]

    def body(*refs):
        ins, refs = list(refs[: len(args)]), refs[len(args) :]
        targets, refs = refs[: len(outs)], refs[len(outs) :]
        own, refs = refs[: len(scratch)], refs[len(scratch) :]
        held, refs = refs[: len(far)], refs[len(far) :]
        made, (in_sems, out_sems) = refs[: len(outs)], refs[len(outs) :]
        for n, k in enumerate(far):
            copy = pltpu.make_async_copy(ins[k], held[n], in_sems.at[n])
            copy.start()
            ins[k] = Held(held[n], copy)
        results = [
            Made(made[n], pltpu.make_async_copy(made[n], targets[n], out_sems.at[n]))
            for n in range(len(outs))
        ]
        kernel(*ins, *results, *own)
        for k in far:
            if ins[k].copy is not None:
                ins[k].copy.wait()
        for result in results:
            result.flush()
        for result in results:
            result.copy.wait()

    hbm = pl.BlockSpec(memory_space=pltpu.HBM)
    return pl.pallas_call(
        body,
        out_shape=shapes,
        in_specs=[SMEM if k in scalars else hbm for k in range(len(args))],
        out_specs=[hbm] * len(outs),
        scratch_shapes=list(scratch)
        + [pltpu.VMEM(args[k].shape, args[k].dtype) for k in far]
        + [pltpu.VMEM(out.shape, out.dtype) for out in shapes]
        + [
            pltpu.SemaphoreType.DMA((max(len(far), 1),)),
            pltpu.SemaphoreType.DMA((len(outs),)),
        ],
        compiler_params=pltpu.CompilerParams(vmem_limit_bytes=62 * 1024 * 1024),
        cost_estimate=pl.CostEstimate(
            flops=int(us * COST * 1e9), bytes_accessed=int(us * COST * 3.5e6), transcendentals=0
        ),
        name=name,
    )(*args)


def where_am_i(group):
    place = lax.axis_index("seq")
    return lax.axis_index("dp"), place // group, place % group


def ties_of(tie_refs):
    ranks = len(tie_refs)
    rank = lax.axis_index("dp")

    def tie_of(seq):
        step = lax.rem(seq + ranks - rank, ranks)
        tie = tie_refs[0][0]
        for k in range(1, ranks):
            tie = jnp.where(step == k, tie_refs[k][0], tie)
        return tie

    return tie_of


def flat_rows(value):
    return value.astype(f32).reshape(-1, value.shape[-1]).astype(value.dtype)


def pack_kernel(group, ranks, *refs):
    tie_of, refs = ties_of(refs[:ranks]), refs[ranks:]
    qkv_ref, out_w_ref, near_ref = refs[:3]
    vectors, out_ref, cols_refs = refs[3:11], refs[11], refs[12:]
    ties, rows, _ = qkv_ref.shape
    planes = ranks
    model = qkv_ref.shape[2] // 3
    width = model // ranks
    rank, plane, member = where_am_i(group)
    shape = (16, SMALL)
    eye = lax.broadcasted_iota(jnp.int32, shape, 0) == lax.broadcasted_iota(jnp.int32, shape, 1)
    eye = jnp.where(eye, 1.0, 0.0).astype(bf16)
    blocks = []
    for tie in range(ties):
        lines = []
        for ref in vectors:
            line = ref[tie : tie + 1].astype(f32)
            for at in range(line.shape[1] // rows):
                lines.append(line[:, at * rows : (at + 1) * rows])
        lines.append(jnp.zeros((16 - len(lines), rows), f32))
        small = dot(jnp.concatenate(lines, 0).astype(bf16), eye, 0, 0)
        blocks.append(small)
    for seq in range(planes):
        tie = tie_of(seq)
        small = blocks[0]
        for block in range(1, ties):
            small = jnp.where(tie == block, blocks[block], small)
        small = small.astype(bf16)
        qkv = qkv_ref[tie]
        for to in range(ranks):
            cols = [
                qkv[:, k * model + to * width : k * model + (to + 1) * width] for k in range(3)
            ]
            out_ref[to * planes + seq] = jnp.concatenate(cols + [small], 1)
    out_ref.flush()
    for step, ref in enumerate(cols_refs):
        tie = tie_of(lax.rem(plane + step, planes))
        here = out_w_ref[tie].astype(f32)
        there = near_ref[tie].astype(f32)
        first = jnp.where(member == 0, here, there)
        second = jnp.where(member == 0, there, here)
        ref[...] = jnp.concatenate([first, second], 0).astype(bf16)


def pack_late_kernel(ranks, *refs):
    tie_of = ties_of(refs[:ranks])
    fc_ref, proj_ref, fc_out_ref, proj_out_ref = refs[ranks:]
    planes = proj_out_ref.shape[0]
    part = fc_ref.shape[2] // ranks
    for seq in range(planes):
        fc = fc_ref[tie_of(seq)]
        for to in range(ranks):
            fc_out_ref[to * planes + seq] = fc[:, to * part : (to + 1) * part]
    fc_out_ref.flush()
    for seq in range(planes):
        proj_out_ref[seq] = proj_ref[tie_of(seq)]


def project_kernel(group, x_ref, *refs):
    w_refs, refs = refs[:group], refs[group:]
    sel_ref, bsel_ref, mask_ref, q_ref, kv_ref, h_ref, vec_ref, fcb_ref, w_ref = refs
    ranks, size, width = q_ref.shape
    part = fcb_ref.shape[1]
    normal, _ = norm_parts(x_ref[...].astype(f32))
    rows = w_ref.shape[0] // group
    for slot, ref in enumerate(w_refs):
        w_ref[slot * rows : (slot + 1) * rows] = flat_rows(ref[...])
    w_ref.flush()
    small = w_ref[:, 3 * width :]
    spread = dot(small, sel_ref[...], 0, 0)[:16]
    normed = (normal * spread[0:1] + spread[1:2]).astype(bf16)
    normed = dot(normed, sel_ref[...], 1, 1).astype(bf16)
    mixed = dot(normed, w_ref[:, : 3 * width])
    biases = jnp.sum(dot(small, bsel_ref[...], 0, 0)[:16] * mask_ref[...], 0, keepdims=True)
    bias = biases[:, part:]
    kv_ref[0] = mixed[:, width : 2 * width].astype(bf16).reshape(ranks, size, width)
    value = (mixed[:, 2 * width :] + bias[:, width:]).astype(bf16)
    kv_ref[1] = value.reshape(ranks, size, width)
    kv_ref.flush()
    query = (mixed[:, :width] + bias[:, :width]).astype(bf16) * jnp.asarray(score_scale, bf16)
    q_ref[...] = query.reshape(ranks, size, width)
    h_ref[...] = normed
    vec_ref[...] = spread[:8]
    fcb_ref[...] = jnp.broadcast_to(biases[:, :part], fcb_ref.shape)


def attend_kernel(group, q_ref, *refs):
    rank, plane, _ = where_am_i(group)
    kv_refs, refs = refs[:group], refs[group:]
    chunks, size, width = q_ref.shape
    w_refs, refs = refs[:chunks], refs[chunks:]
    a_ref, w_ref, sums_refs, sums_ref = refs[0], refs[1], refs[2:-1], refs[-1]
    for chunk in range(chunks):
        count = (chunk + 1) * size
        keys = jnp.concatenate([r[0, : chunk + 1].reshape(count, width) for r in kv_refs], 0)
        values = jnp.concatenate([r[1, : chunk + 1].reshape(count, width) for r in kv_refs], 0)
        values_t = values.T
        query = q_ref[chunk]
        parts = []
        for head in range(width // HEAD_DIM):
            part = jnp.where(head_mask(size, width, head), query, jnp.zeros_like(query))
            scores = dot(keys, part, 1, 1)
            top = jnp.max(scores, 0, keepdims=True)
            raised = jnp.exp(scores - top)
            total = jnp.sum(raised, 0, keepdims=True)
            mixed = dot(values_t[head * HEAD_DIM : (head + 1) * HEAD_DIM], raised.astype(bf16))
            parts.append(mixed / total)
        a_ref[chunk * size : (chunk + 1) * size] = jnp.concatenate(parts, 0).T.astype(bf16)
    a_ref.flush()
    step = w_ref.shape[0] // chunks
    for k, ref in enumerate(w_refs):
        start = pl.multiple_of(lax.rem(plane + chunks - k, chunks) * step, 16)
        w_ref[pl.ds(start, step)] = ref[...]
    sums = dot(a_ref[...], w_ref[...]).astype(bf16)
    sums_ref[...] = sums.reshape(sums_ref.shape)
    for k, ref in enumerate(sums_refs):
        ref[...] = sums_ref[lax.rem(rank + k, chunks)]
        ref.flush()


def join_kernel(ranks, *refs):
    parts, (x_ref, vec_ref, sel_ref, r_ref, h_ref) = refs[:ranks], refs[ranks:]
    total = x_ref[...].astype(f32) + vec_ref[2:3]
    for ref in parts:
        total = total + ref[...].astype(f32)
    r_ref[...] = total
    r_ref.flush()
    normal, _ = norm_parts(total)
    normed = (normal * vec_ref[3:4] + vec_ref[4:5]).astype(bf16)
    h_ref[...] = dot(normed, sel_ref[...], 1, 1).astype(bf16)


def mlp_kernel(group, ranks, h_ref, *refs):
    f_refs, refs = refs[:group], refs[group:]
    fcb_ref, refs = refs[0], refs[1:]
    g_refs, refs = refs[:ranks], refs[ranks:]
    p_refs, refs = refs[:group], refs[group:]
    sel_ref, refs = refs[0], refs[1:]
    dh_refs, refs = refs[:ranks], refs[ranks:]
    y_ref, g_ref, hid_ref, pre_ref, wf_ref, wp_ref, dh_ref = refs
    size = y_ref.shape[1]
    planes, hid_rows, model = p_refs[0].shape
    rank, _, member = where_am_i(group)
    rows = wf_ref.shape[0] // group
    for slot, ref in enumerate(f_refs):
        wf_ref[slot * rows : (slot + 1) * rows] = flat_rows(ref[...])
    value = dot(h_ref[...], wf_ref[...]) + fcb_ref[0:1]
    for slot, ref in enumerate(p_refs):
        for plane in range(planes):
            at = plane * group + lax.rem(member + slot, group)
            start = pl.multiple_of(at * hid_rows, 16)
            wp_ref[pl.ds(start, hid_rows)] = ref[plane]
    for k, ref in enumerate(g_refs):
        start = pl.multiple_of(lax.rem(rank + k, ranks) * size, size)
        g_ref[pl.ds(start, size)] = ref[...]
    g_ref.flush()
    grad = dot(g_ref[...], wp_ref[...], 1, 1)
    squared = value * value
    bent = jnp.tanh(gelu_root * value * (1.0 + gelu_cube * squared))
    half = 0.5 * (1.0 + bent)
    slope = half + (0.5 * gelu_root) * value * (1.0 - bent * bent) * (
        1.0 + 3.0 * gelu_cube * squared
    )
    pre_ref[...] = (grad * slope).astype(bf16)
    pre_ref.flush()
    below = dot(pre_ref[...], wf_ref[...], 1, 1).astype(bf16)
    dh_ref[...] = dot(below, sel_ref[...]).astype(bf16).reshape(ranks, size, model)
    for k, ref in enumerate(dh_refs):
        ref[...] = dh_ref[lax.rem(rank + k, ranks)]
        ref.flush()
    hid_ref[...] = (value * half).astype(bf16)
    hid_ref.flush()
    y_ref[...] = dot(hid_ref[...], wp_ref[...]).astype(bf16).reshape(ranks, size, model)


def mlp_grad_kernel(group, planes, h_ref, pre_ref, hid_ref, g_ref, *refs):
    out_refs, fcb_ref, scr_ref = refs[:group], refs[group], refs[group + 1]
    half = scr_ref.shape[0] // group
    whole = dot(h_ref[...], pre_ref[...], 0, 0)
    for slot, ref in enumerate(out_refs):
        ref[:half] = whole[slot * half : (slot + 1) * half].astype(ref.dtype)
    scr_ref[...] = dot(hid_ref[...], g_ref[...], 0, 0)
    member = where_am_i(group)[2]
    hid_rows = half // planes
    for slot in range(group - 1, -1, -1):
        ref = out_refs[slot]
        for plane in range(planes):
            at = plane * group + lax.rem(member + slot, group)
            start = pl.multiple_of(at * hid_rows, 16)
            to = half + plane * hid_rows
            ref[to : to + hid_rows] = scr_ref[pl.ds(start, hid_rows)].astype(ref.dtype)
        ref.flush()
    fcb_ref[...] = jnp.broadcast_to(
        jnp.sum(pre_ref[...].astype(f32), 0, keepdims=True), fcb_ref.shape
    )


def add_late_kernel(group, *refs):
    parts, (fc_ref, proj_ref) = refs[:group], refs[group:]
    total = parts[0][...]
    for ref in parts[1:]:
        total = total + ref[...].astype(f32)
    half = total.shape[0] // 2
    proj_ref[...] = total[half:].reshape(proj_ref.shape).astype(bf16)
    proj_ref.flush()
    fc_ref[...] = total[:half].reshape(fc_ref.shape).astype(bf16)


def join_back_kernel(ranks, *refs):
    parts, (r_ref, g_ref, vec_ref, dr_ref, low_ref, sums_ref) = refs[:ranks], refs[ranks:]
    normal, scale = norm_parts(r_ref[...])
    upstream = g_ref[...].astype(f32)
    grad = parts[0][...].astype(f32)
    for ref in parts[1:]:
        grad = grad + ref[...].astype(f32)
    total = upstream + norm_back(normal, scale, vec_ref[3:4], grad)
    low_ref[...] = total.astype(bf16)
    low_ref.flush()
    dr_ref[...] = total
    dr_ref.flush()
    sums_ref[...] = jnp.concatenate(
        [
            jnp.sum(total, 0, keepdims=True),
            jnp.sum(grad * normal, 0, keepdims=True),
            jnp.sum(grad, 0, keepdims=True),
            jnp.sum(upstream, 0, keepdims=True),
        ]
        + [jnp.zeros((4, total.shape[1]), f32)],
        0,
    )


def layer_kernel(parts_ref, r_ref, vec_ref, out_ref):
    total = r_ref[...] + vec_ref[5:6]
    for rank in range(parts_ref.shape[0]):
        total = total + parts_ref[rank].astype(f32)
    out_ref[...] = total.astype(bf16)


def attend_back_kernel(group, low_ref, wo_ref, q_ref, *refs):
    kv_refs, refs = refs[:group], refs[group:]
    a_ref, refs = refs[0], refs[1:]
    dkv_refs, dq_ref, dwo_refs, (scr_ref, wo_scr) = (
        refs[:group],
        refs[group],
        refs[group + 1 : -2],
        refs[-2:],
    )
    chunks, size, width = q_ref.shape
    heads = width // HEAD_DIM
    grad_all_rows = dot(low_ref[...], wo_ref[...], 1, 1).astype(bf16)
    for chunk in range(chunks - 1, -1, -1):
        count = (chunk + 1) * size
        keys = jnp.concatenate([r[0, : chunk + 1].reshape(count, width) for r in kv_refs], 0)
        values = jnp.concatenate([r[1, : chunk + 1].reshape(count, width) for r in kv_refs], 0)
        keys_t = keys.T
        query = q_ref[chunk]
        grad = grad_all_rows[chunk * size : (chunk + 1) * size]
        parts, probs_all, grads_all, query_all, grad_all = [], [], [], [], []
        for head in range(heads):
            lanes = head_mask(size, width, head)
            query_part = jnp.where(lanes, query, jnp.zeros_like(query))
            grad_part = jnp.where(lanes, grad, jnp.zeros_like(grad))
            scores = dot(keys, query_part, 1, 1)
            top = jnp.max(scores, 0, keepdims=True)
            raised = jnp.exp(scores - top)
            probs = raised * (1.0 / jnp.sum(raised, 0, keepdims=True))
            grad_probs = dot(values, grad_part, 1, 1)
            delta = jnp.sum(probs * grad_probs, 0, keepdims=True)
            grad_scores = (probs * (grad_probs - delta)).astype(bf16)
            parts.append(dot(keys_t[head * HEAD_DIM : (head + 1) * HEAD_DIM], grad_scores))
            probs_all.append(probs.astype(bf16))
            grads_all.append(grad_scores)
            query_all.append(query_part)
            grad_all.append(grad_part)
        dq_ref[chunk * size : (chunk + 1) * size] = (
            jnp.concatenate(parts, 0).T * score_scale
        ).astype(bf16)
        both = (
            dot(jnp.concatenate(grads_all, 1), jnp.concatenate(query_all, 0)),
            dot(jnp.concatenate(probs_all, 1), jnp.concatenate(grad_all, 0)),
        )
        for slot in range(group):
            for k in range(2):
                value = both[k][slot * count : (slot + 1) * count].reshape(chunk + 1, size, width)
                if chunk == chunks - 1:
                    scr_ref[slot, k] = value
                else:
                    scr_ref[slot, k, : chunk + 1] = scr_ref[slot, k, : chunk + 1] + value
    for slot in range(group - 1, -1, -1):
        dkv_refs[slot][...] = scr_ref[slot].astype(dkv_refs[slot].dtype)
        dkv_refs[slot].flush()
    dq_ref.flush()
    wo_scr[...] = dot(a_ref[...], low_ref[...], 0, 0).reshape(wo_scr.shape)
    for slot in range(group - 1, -1, -1):
        owner = lax.rem(where_am_i(group)[2] + slot, group)
        for plane in range(wo_scr.shape[0]):
            dwo_refs[slot][plane] = wo_scr[plane, owner].astype(dwo_refs[slot].dtype)


def first_kernel(group, ranks, dq_ref, *refs):
    dkv_refs, refs = refs[:group], refs[group:]
    w_ref, sel_ref, refs = refs[0], refs[1], refs[2:]
    dwo_refs, refs = refs[:group], refs[group:]
    proj_ref, refs = refs[0], refs[1:]
    dh_refs, (dh_ref, mix_ref, late_ref) = refs[:ranks], refs[ranks:]
    tokens, width = dq_ref.shape
    model = sel_ref.shape[0]
    size = tokens // ranks
    low = [dq_ref[...]]
    for k in range(2):
        total = dkv_refs[0][k]
        for ref in dkv_refs[1:]:
            total = total + ref[k].astype(f32)
        low.append(total.reshape(tokens, width).astype(bf16))
    mixed = jnp.concatenate(low, 1)
    mix_ref[...] = mixed
    mix_ref.flush()
    below = dot(mixed, w_ref[:, : 3 * width], 1, 1).astype(bf16)
    dh_ref[...] = dot(below, sel_ref[...]).astype(bf16).reshape(ranks, size, model)
    for k, ref in enumerate(dh_refs):
        ref[...] = dh_ref[lax.rem(where_am_i(group)[0] + k, ranks)]
        ref.flush()
    dh_ref.flush()
    total = dwo_refs[0][...]
    for ref in dwo_refs[1:]:
        total = total + ref[...].astype(f32)
    hid_rows = proj_ref.shape[1]
    rest = late_ref.shape[1] - hid_rows - total.shape[1]
    for plane in range(total.shape[0]):
        late_ref[plane, :hid_rows] = proj_ref[plane]
        late_ref[plane, hid_rows:] = jnp.concatenate(
            [total[plane], jnp.zeros((rest, model), f32)], 0
        ).astype(bf16)


def first_grad_kernel(
    group, h_ref, mix_ref, x_ref, dh_ref, sums_ref, fcb_ref, mask_ref, sel_ref, bsel_ref, *refs
):
    ranks, size, model = dh_ref.shape
    width = mix_ref.shape[1] // 3
    part = fcb_ref.shape[1]
    mixed = mix_ref[...]
    whole = dot(h_ref[...], mixed, 0, 0)
    normal, _ = norm_parts(x_ref[...].astype(f32))
    grad = dh_ref[...].reshape(ranks * size, model).astype(f32)
    vec = jnp.concatenate(
        [
            jnp.sum(grad * normal, 0, keepdims=True),
            jnp.sum(grad, 0, keepdims=True),
            sums_ref[0:4],
            jnp.zeros((2, model), f32),
        ],
        0,
    )
    cols = jnp.sum(mixed.astype(f32), 0, keepdims=True)
    both = jnp.concatenate([cols[:, :width], cols[:, 2 * width :]], 1)
    sums = jnp.concatenate([fcb_ref[0:1], both], 1) * mask_ref[...]
    small = dot(sel_ref[...], vec.astype(bf16), 1, 1)
    more = dot(bsel_ref[...], sums.astype(bf16), 1, 1)
    rest = jnp.zeros((model, SMALL - 24), f32)
    whole = jnp.concatenate([whole, small, more, rest], 1)
    rows = model // group
    for slot in range(group - 1, -1, -1):
        refs[slot][...] = whole[slot * rows : (slot + 1) * rows].astype(refs[slot].dtype)
        refs[slot].flush()


def add_early_kernel(group, *refs):
    parts, out_ref = refs[:group], refs[group]
    total = parts[0][...]
    for ref in parts[1:]:
        total = total + ref[...].astype(f32)
    out_ref[...] = total.reshape(out_ref.shape).astype(bf16)


def last_kernel(ranks, *refs):
    parts, (x_ref, vec_ref, dr_ref, out_ref) = refs[:ranks], refs[ranks:]
    normal, scale = norm_parts(x_ref[...].astype(f32))
    grad = parts[0][...].astype(f32)
    for ref in parts[1:]:
        grad = grad + ref[...].astype(f32)
    out_ref[...] = (dr_ref[...] + norm_back(normal, scale, vec_ref[0:1], grad)).astype(bf16)


def by_block(ties, parts, tie_of):
    totals = [jnp.zeros(parts[0].shape, f32) for _ in range(ties)]
    for seq, part in enumerate(parts):
        value = part.astype(f32)
        for block in range(ties):
            totals[block] = totals[block] + jnp.where(tie_of(seq) == block, value, 0.0)
    return totals


def final_late_kernel(ranks, *refs):
    tie_of = ties_of(refs[:ranks])
    fc_in, rest_in, fc_ref, proj_ref, out_ref = refs[ranks:]
    ties, _, inner = fc_ref.shape
    planes = rest_in.shape[0]
    hid_rows, rows = proj_ref.shape[1], out_ref.shape[1]
    part = inner // ranks
    for block, total in enumerate(by_block(ties, [rest_in[k] for k in range(planes)], tie_of)):
        proj_ref[block] = total[:hid_rows]
        out_ref[block] = total[hid_rows : hid_rows + rows]
    proj_ref.flush()
    for rank in range(ranks):
        parts = [fc_in[rank * planes + k] for k in range(planes)]
        for block, total in enumerate(by_block(ties, parts, tie_of)):
            fc_ref[block, :, rank * part : (rank + 1) * part] = total


def final_kernel(ranks, *refs):
    tie_of = ties_of(refs[:ranks])
    home_ref, qkv_ref, *small_refs = refs[ranks:]
    ties, rows, wide = qkv_ref.shape
    model = wide // 3
    planes = home_ref.shape[0] // ranks
    width = model // ranks
    sums = []
    for rank in range(ranks):
        parts = [home_ref[rank * planes + k] for k in range(planes)]
        sums.append(by_block(ties, parts, tie_of))
    eye = lax.broadcasted_iota(jnp.int32, (SMALL, SMALL), 0)
    eye = jnp.where(eye == lax.broadcasted_iota(jnp.int32, (SMALL, SMALL), 1), 1.0, 0.0)
    eye = eye.astype(bf16)
    for block in range(ties):
        values = [sums[rank][block] for rank in range(ranks)]
        qkv_ref[block] = jnp.concatenate(
            [value[:, k * width : (k + 1) * width] for k in range(3) for value in values], 1
        )
        small = values[0][:, 3 * width :]
        for value in values[1:]:
            small = small + value[:, 3 * width :]
        high = small.astype(bf16)
        low = (small - high.astype(f32)).astype(bf16)
        turned = dot(eye, high, 1, 1) + dot(eye, low, 1, 1)
        for k in range(6):
            small_refs[k][block : block + 1] = turned[k : k + 1]
        small_refs[6][block : block + 1] = jnp.concatenate(
            [turned[k : k + 1] for k in range(14, 16)], 1
        )
        small_refs[7][block : block + 1] = jnp.concatenate(
            [turned[k : k + 1] for k in range(16, 20)], 1
        )


def fast_device(
    n_dp,
    n_seq,
    tokens,
    tie_index,
    first_gain,
    first_shift,
    qkv_weight,
    qv_bias,
    out_weight,
    out_bias,
    second_gain,
    second_shift,
    fc_weight,
    fc_bias,
    proj_weight,
    proj_bias,
    cotangent,
):
    ranks, planes, group = n_dp, n_dp, n_seq // n_dp
    axes = ("dp", "seq")
    size, model = tokens.shape[1:]
    ties, rows = qkv_weight.shape[:2]
    hid_rows = proj_weight.shape[1]
    inner = fc_weight.shape[2]
    width = model // ranks
    part = inner // ranks
    count = ranks * size
    lanes = 3 * width + SMALL
    squads = ranks * planes
    rank = lax.axis_index("dp")
    place = lax.axis_index("seq")
    plane, member = place // group, place % group

    def route(where):
        pairs = []
        for a in range(ranks):
            for b in range(planes):
                for c in range(group):
                    x, y, z = where(a, b, c)
                    pairs.append((a * n_seq + b * group + c, x * n_seq + y * group + z))
        return pairs

    swap = route(lambda a, b, c: (b, a, c))
    to_rank = [route(lambda a, b, c, k=k: ((a + k) % ranks, b, c)) for k in range(ranks)]
    to_plane = [route(lambda a, b, c, k=k: (a, (b + k) % planes, c)) for k in range(planes)]
    to_member = [route(lambda a, b, c, k=k: (a, b, (c + k) % group)) for k in range(group)]
    same_member = [[b * group + c for b in range(planes)] for c in range(group)]
    squad = [
        [a * n_seq + b * group + c for a in range(ranks) for b in range(planes)]
        for c in range(group)
    ]

    def send(values, pairs):
        return lax.ppermute(values, axes, pairs)

    def from_members(piece):
        return [piece] + [send(piece, to_member[group - k]) for k in range(1, group)]

    def over_members(parts):
        return [parts[0]] + [send(parts[k], to_member[k]) for k in range(1, group)]

    def over_planes(pieces):
        return lax.all_to_all(pieces, "seq", 0, 0, axis_index_groups=same_member)

    def over_squad(pieces):
        return lax.all_to_all(pieces, axes, 0, 0, axis_index_groups=squad)

    def scatter(parts):
        return [parts[0]] + [send(parts[k], to_rank[k]) for k in range(1, ranks)]

    def gate(value, *before):
        return lax.optimization_barrier((value, before))[0]

    ties_seen = [tie_index] + [send(tie_index, to_rank[ranks - k]) for k in range(1, ranks)]
    scalar_ties = tuple(range(ranks))
    near = send(out_weight, to_member[1])
    tokens_own = send(tokens[0], swap)
    grad_own = send(cotangent[0], swap)

    early, *out_cols = run(
        functools.partial(pack_kernel, group, ranks),
        [((squads, rows, lanes), bf16)] + [((group * rows, model), bf16)] * planes,
        *ties_seen,
        qkv_weight,
        out_weight,
        near,
        first_gain,
        first_shift,
        out_bias,
        second_gain,
        second_shift,
        proj_bias,
        qv_bias,
        fc_bias,
        scalars=scalar_ties,
        us=2.0,
        name="pack",
    )
    early = over_squad(early)
    out_cols = [out_cols[0]] + [send(out_cols[k], to_plane[k]) for k in range(1, planes)]

    def arrival(owner, row):
        a, b, c = owner // n_seq, (owner % n_seq) // group, owner % group
        slot = (c + group - member) % group
        return (slot * squads + a * planes + b) * rows + row

    flat = jnp.arange(model)
    at_model = arrival(flat // rows, flat % rows)
    unit = jnp.arange(part) + rank * part
    at_fc = arrival(unit // (4 * rows), unit % rows)
    flat_qv = jnp.arange(2 * width)
    unit_qv = (flat_qv // width) * model + rank * width + flat_qv % width
    at_qv = arrival(unit_qv // (2 * rows), unit_qv % rows)
    at_bias = jnp.concatenate([at_fc, at_qv])
    lanes_of = jnp.concatenate(
        [
            (jnp.arange(part) % (4 * rows)) // rows + 8,
            (unit_qv % (2 * rows)) // rows + 6,
        ]
    )
    sel = (jnp.arange(model)[:, None] == at_model[None, :]).astype(bf16)
    bsel = (jnp.arange(model)[:, None] == at_bias[None, :]).astype(bf16)
    row_mask = (jnp.arange(16)[:, None] == lanes_of[None, :]).astype(f32)

    late_fc, late_proj = run(
        functools.partial(pack_late_kernel, ranks),
        [((squads, rows, part), bf16), ((planes, hid_rows, model), bf16)],
        *ties_seen,
        fc_weight,
        proj_weight,
        scalars=scalar_ties,
        us=2.0,
        name="pack_late",
    )
    tokens_all = lax.all_gather(tokens_own, "dp", axis=0, tiled=True)
    early = gate(early, tokens_all, grad_own, sel, bsel, row_mask, late_fc, out_cols)
    grads_seen = [grad_own] + [send(grad_own, to_rank[ranks - k]) for k in range(1, ranks)]
    late_fc = over_squad(gate(late_fc, early))
    early = from_members(early)
    own = ((size, model), bf16)
    q, kv, h_one, vec, fcb, w_early = run(
        functools.partial(project_kernel, group),
        [
            ((ranks, size, width), bf16),
            ((2, ranks, size, width), bf16),
            ((count, model), bf16),
            ((8, model), f32),
            ((8, part), f32),
            ((model, lanes), bf16),
        ],
        tokens_all,
        *early,
        sel,
        bsel,
        row_mask,
        us=5.0,
        name="project",
    )
    kv = from_members(kv)
    attended, w_out, *sums = run(
        functools.partial(attend_kernel, group),
        [((count, width), bf16), ((width, model), bf16)] + [own] * ranks,
        q,
        *kv,
        *out_cols,
        scratch=[pltpu.VMEM((ranks, size, model), bf16)],
        us=6.0,
        name="attend",
    )
    late_proj = over_planes(gate(late_proj, attended))
    middle, h_own = run(
        functools.partial(join_kernel, ranks),
        [((size, model), f32), own],
        *scatter(sums),
        tokens_own,
        gate(vec, grads_seen),
        sel,
        us=2.0,
        name="join",
    )
    late_proj = from_members(gate(late_proj, h_own))
    late_fc = from_members(gate(late_fc, h_own))
    h_two = lax.all_gather(h_own, "dp", axis=0, tiled=True)
    rest = run(
        functools.partial(mlp_kernel, group, ranks),
        [own] * ranks
        + [((ranks, size, model), bf16), ((count, model), bf16)]
        + [((count, part), bf16)] * 2,
        h_two,
        *late_fc,
        fcb,
        *grads_seen,
        *late_proj,
        sel,
        scratch=[
            pltpu.VMEM((model, part), bf16),
            pltpu.VMEM((part, model), bf16),
            pltpu.VMEM((ranks, size, model), bf16),
        ],
        us=7.0,
        name="mlp",
    )
    below, (layer_parts, grad_all, hidden, grad_pre) = rest[:ranks], rest[ranks:]
    below = scatter(below)
    half = 2 * (model // group)
    *late, fc_sums = run(
        functools.partial(mlp_grad_kernel, group, planes),
        [((half, model), f32)]
        + [((half, model), bf16)] * (group - 1)
        + [((8, part), f32)],
        h_two,
        grad_pre,
        hidden,
        grad_all,
        scratch=[pltpu.VMEM((part, model), f32)],
        us=4.0,
        name="mlp_grad",
    )
    late = over_members(late)
    grad_middle, low_own, own_sums = run(
        functools.partial(join_back_kernel, ranks),
        [((size, model), f32), own, ((8, model), f32)],
        *below,
        middle,
        grad_own,
        vec,
        us=30.0,
        name="join_back",
    )
    late_fc, late_proj = run(
        functools.partial(add_late_kernel, group),
        [((squads, rows, part), bf16), ((planes, hid_rows, model), bf16)],
        *gate(late, low_own),
        us=2.0,
        name="add_late",
    )
    low = lax.all_gather(gate(low_own, late_fc), "dp", axis=0, tiled=True)
    late_fc = over_squad(late_fc)
    layer_parts = lax.all_to_all(gate(layer_parts, low, late_fc), "dp", 0, 0)
    (layer_own,) = run(
        layer_kernel,
        [own],
        layer_parts,
        middle,
        vec,
        us=1.0,
        name="layer",
    )
    layer_out = send(layer_own, swap)[None]
    rest = run(
        functools.partial(attend_back_kernel, group),
        [((2, ranks, size, width), f32)]
        + [((2, ranks, size, width), bf16)] * (group - 1)
        + [((count, width), bf16)]
        + [((planes, rows, model), f32)]
        + [((planes, rows, model), bf16)] * (group - 1),
        low,
        w_out,
        q,
        *kv,
        attended,
        scratch=[
            pltpu.VMEM((group, 2, ranks, size, width), f32),
            pltpu.VMEM((planes, group, rows, model), f32),
        ],
        us=10.0,
        name="attend_back",
    )
    dkv, dq, dw_out = rest[:group], rest[group], rest[group + 1 :]
    dkv = over_members(dkv)
    dw_out = over_members(dw_out)
    late_rows = hid_rows + (rows + 15) // 16 * 16
    rest = run(
        functools.partial(first_kernel, group, ranks),
        [own] * ranks
        + [
            ((ranks, size, model), bf16),
            ((count, 3 * width), bf16),
            ((planes, late_rows, model), bf16),
        ],
        dq,
        *dkv,
        gate(w_early, layer_own),
        sel,
        *dw_out,
        late_proj,
        us=4.0,
        name="first",
    )
    first_parts, (first_all, mixed, late_rest) = rest[:ranks], rest[ranks:]
    grad_first = scatter(first_parts)
    late_rest = over_planes(gate(late_rest, layer_parts))
    early = run(
        functools.partial(first_grad_kernel, group),
        [((model // group, lanes), f32)]
        + [((model // group, lanes), bf16)] * (group - 1),
        h_one,
        mixed,
        tokens_all,
        first_all,
        own_sums,
        fc_sums,
        row_mask,
        sel,
        bsel,
        us=5.0,
        name="first_grad",
    )
    early = over_members(early)
    (input_own,) = run(
        functools.partial(last_kernel, ranks),
        [own],
        *grad_first,
        tokens_own,
        vec,
        grad_middle,
        us=30.0,
        name="last",
    )
    (early,) = run(
        functools.partial(add_early_kernel, group),
        [((squads, rows, lanes), bf16)],
        *gate(early, input_own, layer_out),
        us=1.0,
        name="add_early",
    )
    input_grad = send(input_own, swap)[None]
    early = over_squad(early)
    grad_fc_weight, grad_proj_weight, grad_out_weight = run(
        functools.partial(final_late_kernel, ranks),
        [((ties, rows, inner), f32), ((ties, hid_rows, model), f32), ((ties, rows, model), f32)],
        *ties_seen,
        late_fc,
        gate(late_rest, input_own),
        scalars=scalar_ties,
        us=3.0,
        name="final_late",
    )
    grad_qkv_weight, *small = run(
        functools.partial(final_kernel, ranks),
        [((ties, rows, 3 * model), f32)]
        + [((ties, rows), f32)] * 6
        + [((ties, 2 * rows), f32), ((ties, 4 * rows), f32)],
        *ties_seen,
        gate(early, grad_fc_weight),
        scalars=scalar_ties,
        us=1.0,
        name="final",
    )
    return (
        layer_out,
        input_grad,
        small[0],
        small[1],
        grad_qkv_weight,
        small[6],
        grad_out_weight,
        small[2],
        small[3],
        small[4],
        grad_fc_weight,
        small[7],
        grad_proj_weight,
        small[5],
    )


def pick_device(n_dp, n_seq, *args):
    tokens, qkv_weight, proj_weight = args[0], args[4], args[12]
    size, rows, hid_rows = tokens.shape[1], qkv_weight.shape[1], proj_weight.shape[1]
    group = n_seq // n_dp
    whole_tiles = rows % 8 == 0 and (group * rows) % 16 == 0 and hid_rows % 16 == 0
    one_block = tokens.shape[0] == 1 and group == 2 and size * group == BLOCK
    if whole_tiles and one_block:
        return fast_device(n_dp, n_seq, *args)
    return per_device(*args)


def solution(mesh):
    in_specs = (
        P("dp", "seq", None),
        P("dp"),
        P(None, ("dp", "seq")),
        P(None, ("dp", "seq")),
        P(None, ("dp", "seq"), None),
        P(None, ("dp", "seq")),
        P(None, ("dp", "seq"), None),
        P(None, ("dp", "seq")),
        P(None, ("dp", "seq")),
        P(None, ("dp", "seq")),
        P(None, ("dp", "seq"), None),
        P(None, ("dp", "seq")),
        P(None, ("dp", "seq"), None),
        P(None, ("dp", "seq")),
        P("dp", "seq", None),
    )
    out_specs = (
        P("dp", "seq", None),
        P("dp", "seq", None),
        P(None, ("dp", "seq")),
        P(None, ("dp", "seq")),
        P(None, ("dp", "seq"), None),
        P(None, ("dp", "seq")),
        P(None, ("dp", "seq"), None),
        P(None, ("dp", "seq")),
        P(None, ("dp", "seq")),
        P(None, ("dp", "seq")),
        P(None, ("dp", "seq"), None),
        P(None, ("dp", "seq")),
        P(None, ("dp", "seq"), None),
        P(None, ("dp", "seq")),
    )
    return jax.shard_map(
        functools.partial(pick_device, mesh.shape["dp"], mesh.shape["seq"]),
        mesh=mesh,
        in_specs=in_specs,
        out_specs=out_specs,
        check_vma=False,
    )
```

```python
import functools
import math

import jax
import jax.numpy as jnp
from jax import lax
from jax.experimental import pallas as pl
from jax.experimental.pallas import tpu as pltpu
from jax.sharding import PartitionSpec as P

HEADS = 12
HEAD_DIM = 64
BLOCK = 256


epsilon = 1e-05
neg_large = -1e30


def norm_apply(values, norm_gain, norm_shift):
    row_mean = jnp.mean(values, -1, keepdims=True)
    centred = values - row_mean
    row_var = jnp.mean(centred * centred, -1, keepdims=True)
    return centred * lax.rsqrt(row_var + epsilon) * norm_gain + norm_shift


def gelu_tanh(values):
    return jax.nn.gelu(values, approximate=True)


def select_all(gathered, chosen):
    return tuple(
        (lax.dynamic_index_in_dim(stacked, chosen, 0, keepdims=False) for stacked in gathered)
    )


def add_block(totals, update, chosen):
    current = lax.dynamic_index_in_dim(totals, chosen, 0, keepdims=True)
    return lax.dynamic_update_index_in_dim(totals, current + update[None], chosen, 0)


def split_three(values):
    upper_part = values.astype(jnp.bfloat16)
    rest_one = values - lax.optimization_barrier(upper_part).astype(jnp.float32)
    middle_part = rest_one.astype(jnp.bfloat16)
    lower_part = (rest_one - lax.optimization_barrier(middle_part).astype(jnp.float32)).astype(
        jnp.bfloat16
    )
    return (upper_part, middle_part, lower_part)


def to_heads(flat_rows, head_count):
    return flat_rows.reshape(
        flat_rows.shape[0], flat_rows.shape[1], head_count, flat_rows.shape[2] // head_count
    )


def allowed_mask(query_pos, key_pos, block_len):
    return (key_pos[None, :] // block_len <= query_pos[:, None] // block_len)[None, :, None, :]


def make_forward_step(query_heads, positions, block_len, score_scale):
    last_block = positions[-1] // block_len
    head_count = query_heads.shape[2]

    def fold_step(carried, shard_piece, start_row):
        key_piece, value_piece = shard_piece
        key_count = key_piece.shape[1]
        step_len = math.gcd(key_count, 512)

        def one_part(fold_state, offset):
            key_heads = to_heads(
                lax.dynamic_slice_in_dim(key_piece, offset, step_len, 1), head_count
            )
            value_heads = to_heads(
                lax.dynamic_slice_in_dim(value_piece, offset, step_len, 1), head_count
            )
            key_pos = offset + jnp.arange(step_len, dtype=jnp.int32)

            def update(state_in):
                top_old, total_old, sum_old = state_in
                scores = (
                    jnp.einsum(
                        "sqhe,skhe->sqhk",
                        query_heads,
                        key_heads,
                        preferred_element_type=jnp.float32,
                    )
                    * score_scale
                )
                allowed = allowed_mask(positions, key_pos, block_len)
                top_new = jnp.maximum(top_old, jnp.max(jnp.where(allowed, scores, neg_large), -1))
                exp_scores = jnp.where(allowed, jnp.exp(scores - top_new[..., None]), 0.0)
                rescale = jnp.exp(top_old - top_new)
                total_new = total_old * rescale + jnp.sum(exp_scores, -1)
                sum_new = sum_old * rescale[..., None] + jnp.einsum(
                    "sqhk,skhe->sqhe",
                    exp_scores.astype(jnp.bfloat16),
                    value_heads,
                    preferred_element_type=jnp.float32,
                )
                return (top_new, total_new, sum_new)

            return (
                lax.cond(
                    offset // block_len <= last_block, update, lambda state_in: state_in, fold_state
                ),
                None,
            )

        offsets = jnp.arange(key_count // step_len, dtype=jnp.int32) * step_len
        return lax.scan(one_part, carried, offsets)[0]

    return fold_step


def make_query_step(
    query_heads, grad_heads, log_total, delta_rows, positions, block_len, score_scale
):
    last_block = positions[-1] // block_len
    head_count = query_heads.shape[2]

    def fold_step(carried, shard_piece, start_row):
        key_piece, value_piece = shard_piece
        key_count = key_piece.shape[1]
        step_len = math.gcd(key_count, 512)

        def one_part(fold_state, offset):
            key_heads = to_heads(
                lax.dynamic_slice_in_dim(key_piece, offset, step_len, 1), head_count
            )
            value_heads = to_heads(
                lax.dynamic_slice_in_dim(value_piece, offset, step_len, 1), head_count
            )
            key_pos = offset + jnp.arange(step_len, dtype=jnp.int32)

            def update(state_in):
                scores = (
                    jnp.einsum(
                        "sqhe,skhe->sqhk",
                        query_heads,
                        key_heads,
                        preferred_element_type=jnp.float32,
                    )
                    * score_scale
                )
                allowed = allowed_mask(positions, key_pos, block_len)
                probs_all = jnp.where(allowed, jnp.exp(scores - log_total[..., None]), 0.0)
                grad_probs = jnp.einsum(
                    "sqhe,skhe->sqhk", grad_heads, value_heads, preferred_element_type=jnp.float32
                )
                grad_scores = (probs_all * (grad_probs - delta_rows[..., None])).astype(
                    jnp.bfloat16
                )
                return state_in + jnp.einsum(
                    "sqhk,skhe->sqhe", grad_scores, key_heads, preferred_element_type=jnp.float32
                )

            return (
                lax.cond(
                    offset // block_len <= last_block, update, lambda state_in: state_in, fold_state
                ),
                None,
            )

        offsets = jnp.arange(key_count // step_len, dtype=jnp.int32) * step_len
        return lax.scan(one_part, carried, offsets)[0]

    return fold_step


def make_key_step(key_heads, value_heads, positions, block_len, score_scale):
    first_block = positions[0] // block_len
    head_count = key_heads.shape[2]

    def fold_step(carried, shard_piece, start_row):
        query_piece, grad_piece, stats_piece = shard_piece
        seq_count, query_count, model_width = query_piece.shape
        step_len = math.gcd(query_count, 512)

        def one_part(fold_state, offset):
            query_part = to_heads(
                lax.dynamic_slice_in_dim(query_piece, offset, step_len, 1), head_count
            )
            grad_part = to_heads(
                lax.dynamic_slice_in_dim(grad_piece, offset, step_len, 1), head_count
            )
            stats_part = lax.dynamic_slice_in_dim(stats_piece, offset, step_len, 1).astype(
                jnp.float32
            )
            stats_part = stats_part.reshape(seq_count, step_len, 6, head_count)
            log_total = stats_part[:, :, 0] + stats_part[:, :, 1] + stats_part[:, :, 2]
            delta_rows = stats_part[:, :, 3] + stats_part[:, :, 4] + stats_part[:, :, 5]
            query_pos = offset + jnp.arange(step_len, dtype=jnp.int32)

            def update(state_in):
                key_grad, value_grad = state_in
                scores = (
                    jnp.einsum(
                        "sqhe,skhe->sqhk", query_part, key_heads, preferred_element_type=jnp.float32
                    )
                    * score_scale
                )
                allowed = allowed_mask(query_pos, positions, block_len)
                probs_all = jnp.where(allowed, jnp.exp(scores - log_total[..., None]), 0.0)
                grad_probs = jnp.einsum(
                    "sqhe,skhe->sqhk", grad_part, value_heads, preferred_element_type=jnp.float32
                )
                grad_scores = (probs_all * (grad_probs - delta_rows[..., None])).astype(
                    jnp.bfloat16
                )
                value_grad = value_grad + jnp.einsum(
                    "sqhk,sqhe->skhe",
                    probs_all.astype(jnp.bfloat16),
                    grad_part,
                    preferred_element_type=jnp.float32,
                )
                key_grad = key_grad + jnp.einsum(
                    "sqhk,sqhe->skhe", grad_scores, query_part, preferred_element_type=jnp.float32
                )
                return (key_grad, value_grad)

            last_query = (offset + step_len - 1) // block_len
            return (
                lax.cond(last_query >= first_block, update, lambda state_in: state_in, fold_state),
                None,
            )

        offsets = jnp.arange(query_count // step_len, dtype=jnp.int32) * step_len
        return lax.scan(one_part, carried, offsets)[0]

    return fold_step


def per_device(
    tokens,
    tie_index,
    first_gain,
    first_shift,
    qkv_weight,
    qv_bias,
    out_weight,
    out_bias,
    second_gain,
    second_shift,
    fc_weight,
    fc_bias,
    proj_weight,
    proj_bias,
    cotangent,
):
    gathered = (
        lax.all_gather(first_gain, ("dp", "seq"), axis=1, tiled=True),
        lax.all_gather(first_shift, ("dp", "seq"), axis=1, tiled=True),
        lax.all_gather(qkv_weight, ("dp", "seq"), axis=1, tiled=True),
        lax.all_gather(qv_bias, ("dp", "seq"), axis=1, tiled=True),
        lax.all_gather(out_weight, ("dp", "seq"), axis=1, tiled=True),
        lax.all_gather(out_bias, ("dp", "seq"), axis=1, tiled=True),
        lax.all_gather(second_gain, ("dp", "seq"), axis=1, tiled=True),
        lax.all_gather(second_shift, ("dp", "seq"), axis=1, tiled=True),
        lax.all_gather(fc_weight, ("dp", "seq"), axis=1, tiled=True),
        lax.all_gather(fc_bias, ("dp", "seq"), axis=1, tiled=True),
        lax.all_gather(proj_weight, ("dp", "seq"), axis=1, tiled=True),
        lax.all_gather(proj_bias, ("dp", "seq"), axis=1, tiled=True),
    )
    seq_count, tok_count, model_width = tokens.shape
    head_count = HEADS
    block_len = BLOCK
    score_scale = 1.0 / math.sqrt(HEAD_DIM)
    positions = lax.axis_index("seq") * tok_count + jnp.arange(tok_count, dtype=jnp.int32)
    member = 0
    gain_one, shift_one, w_qkv, bias_qv = select_all(gathered[0:4], tie_index[member])
    inputs = tokens[member].astype(jnp.float32)
    normed = norm_apply(inputs, gain_one, shift_one).astype(jnp.bfloat16)
    qkv_rows = jnp.dot(normed, w_qkv, preferred_element_type=jnp.float32)
    normed_list = [normed]
    query_list = [(qkv_rows[:, :model_width] + bias_qv[:model_width]).astype(jnp.bfloat16)]
    key_list = [qkv_rows[:, model_width : 2 * model_width].astype(jnp.bfloat16)]
    value_list = [(qkv_rows[:, 2 * model_width :] + bias_qv[model_width:]).astype(jnp.bfloat16)]
    query_all = jnp.stack(query_list)
    key_all = jnp.stack(key_list)
    value_all = jnp.stack(value_list)
    query_heads = to_heads(query_all, head_count)
    head_dim = query_heads.shape[3]
    stat_shape = (seq_count, tok_count, head_count)
    start_state = (
        jnp.full(stat_shape, neg_large, jnp.float32),
        jnp.zeros(stat_shape, jnp.float32),
        jnp.zeros(stat_shape + (head_dim,), jnp.float32),
    )
    forward_step = make_forward_step(query_heads, positions, block_len, score_scale)
    top_score, total_weight, weighted_sum = forward_step(
        start_state,
        (
            lax.all_gather(key_all, "seq", axis=1, tiled=True),
            lax.all_gather(value_all, "seq", axis=1, tiled=True),
        ),
        jnp.int32(0),
    )
    attn_heads = weighted_sum / total_weight[..., None]
    log_total = top_score + jnp.log(total_weight)
    attended = attn_heads.reshape(seq_count, tok_count, model_width).astype(jnp.bfloat16)
    member = 0
    w_out, bias_out, gain_two, shift_two, w_fc, bias_fc, w_proj, bias_proj = select_all(
        gathered[4:12], tie_index[member]
    )
    inputs = tokens[member].astype(jnp.float32)
    middle = (
        inputs + jnp.dot(attended[member], w_out, preferred_element_type=jnp.float32) + bias_out
    )
    normed_two = norm_apply(middle, gain_two, shift_two).astype(jnp.bfloat16)
    hidden_pre = jnp.dot(normed_two, w_fc, preferred_element_type=jnp.float32) + bias_fc
    hidden = gelu_tanh(hidden_pre).astype(jnp.bfloat16)
    layer_rows = [
        (middle + jnp.dot(hidden, w_proj, preferred_element_type=jnp.float32) + bias_proj).astype(
            jnp.bfloat16
        )
    ]
    saved_mlp = [(middle, normed_two, hidden_pre, hidden)]
    layer_out = jnp.stack(layer_rows)
    whole_back = (
        lax.all_gather(first_gain, ("dp", "seq"), axis=1, tiled=True),
        lax.all_gather(first_shift, ("dp", "seq"), axis=1, tiled=True),
        lax.all_gather(qkv_weight, ("dp", "seq"), axis=1, tiled=True),
        lax.all_gather(qv_bias, ("dp", "seq"), axis=1, tiled=True),
        lax.all_gather(out_weight, ("dp", "seq"), axis=1, tiled=True),
        lax.all_gather(out_bias, ("dp", "seq"), axis=1, tiled=True),
        lax.all_gather(second_gain, ("dp", "seq"), axis=1, tiled=True),
        lax.all_gather(second_shift, ("dp", "seq"), axis=1, tiled=True),
        lax.all_gather(fc_weight, ("dp", "seq"), axis=1, tiled=True),
        lax.all_gather(fc_bias, ("dp", "seq"), axis=1, tiled=True),
        lax.all_gather(proj_weight, ("dp", "seq"), axis=1, tiled=True),
        lax.all_gather(proj_bias, ("dp", "seq"), axis=1, tiled=True),
    )
    grad_totals = [jnp.zeros(stacked.shape, jnp.float32) for stacked in whole_back]
    member = 0
    chosen = tie_index[member]
    w_out, bias_out, gain_two, shift_two, w_fc, bias_fc, w_proj, bias_proj = select_all(
        whole_back[4:12], chosen
    )
    middle, normed_two, hidden_pre, hidden = saved_mlp[member]
    upstream = cotangent[member].astype(jnp.float32)
    upstream_low = upstream.astype(jnp.bfloat16)
    grad_hidden = jnp.einsum("td,fd->tf", upstream_low, w_proj, preferred_element_type=jnp.float32)
    gelu_pull = jax.vjp(gelu_tanh, hidden_pre)[1]
    grad_pre = gelu_pull(grad_hidden)[0].astype(jnp.bfloat16)
    grad_normed = jnp.einsum("tf,df->td", grad_pre, w_fc, preferred_element_type=jnp.float32)
    norm_pull = jax.vjp(
        norm_apply, middle, gain_two.astype(jnp.float32), shift_two.astype(jnp.float32)
    )[1]
    grad_middle, grad_gain, grad_shift = norm_pull(grad_normed)
    grad_middle = grad_middle + upstream
    middle_low = grad_middle.astype(jnp.bfloat16)
    attn_grads = [
        jnp.einsum("te,de->td", middle_low, w_out, preferred_element_type=jnp.float32).astype(
            jnp.bfloat16
        )
    ]
    middle_grads = [grad_middle]
    updates = (
        jnp.einsum("td,te->de", attended[member], middle_low, preferred_element_type=jnp.float32),
        jnp.sum(grad_middle, 0),
        grad_gain,
        grad_shift,
        jnp.einsum("td,tf->df", normed_two, grad_pre, preferred_element_type=jnp.float32),
        jnp.sum(grad_pre.astype(jnp.float32), 0),
        jnp.einsum("tf,td->fd", hidden, upstream_low, preferred_element_type=jnp.float32),
        jnp.sum(upstream, 0),
    )
    for slot_index, update in enumerate(updates):
        grad_totals[4 + slot_index] = add_block(grad_totals[4 + slot_index], update, chosen)
    grad_attn_all = jnp.stack(attn_grads)
    grad_heads = to_heads(grad_attn_all, head_count)
    delta_rows = jnp.sum(grad_heads.astype(jnp.float32) * attn_heads, -1)
    query_step = make_query_step(
        query_heads, grad_heads, log_total, delta_rows, positions, block_len, score_scale
    )
    zero_heads = jnp.zeros(stat_shape + (head_dim,), jnp.float32)
    grad_query = query_step(
        zero_heads,
        (
            lax.all_gather(key_all, "seq", axis=1, tiled=True),
            lax.all_gather(value_all, "seq", axis=1, tiled=True),
        ),
        jnp.int32(0),
    )
    row_stats = jnp.stack(split_three(log_total) + split_three(delta_rows), 2).reshape(
        seq_count, tok_count, 6 * head_count
    )
    key_step = make_key_step(
        to_heads(key_all, head_count),
        to_heads(value_all, head_count),
        positions,
        block_len,
        score_scale,
    )
    grad_key, grad_value = key_step(
        (zero_heads, zero_heads),
        (
            lax.all_gather(query_all, "seq", axis=1, tiled=True),
            lax.all_gather(grad_attn_all, "seq", axis=1, tiled=True),
            lax.all_gather(row_stats, "seq", axis=1, tiled=True),
        ),
        jnp.int32(0),
    )
    flat_shape = (seq_count, tok_count, model_width)
    grad_query = (grad_query * score_scale).reshape(flat_shape).astype(jnp.bfloat16)
    grad_key = (grad_key * score_scale).reshape(flat_shape).astype(jnp.bfloat16)
    grad_value = grad_value.reshape(flat_shape).astype(jnp.bfloat16)
    member = 0
    chosen = tie_index[member]
    gain_one, shift_one, w_qkv, bias_qv = select_all(whole_back[0:4], chosen)
    grad_mixed = jnp.concatenate([grad_query[member], grad_key[member], grad_value[member]], 1)
    grad_normed = jnp.einsum("te,de->td", grad_mixed, w_qkv, preferred_element_type=jnp.float32)
    norm_pull = jax.vjp(
        norm_apply,
        tokens[member].astype(jnp.float32),
        gain_one.astype(jnp.float32),
        shift_one.astype(jnp.float32),
    )[1]
    grad_inputs, grad_gain, grad_shift = norm_pull(grad_normed)
    input_rows = [(grad_inputs + middle_grads[member]).astype(jnp.bfloat16)]
    updates = (
        grad_gain,
        grad_shift,
        jnp.einsum(
            "td,te->de", normed_list[member], grad_mixed, preferred_element_type=jnp.float32
        ),
        jnp.concatenate(
            [
                jnp.sum(grad_query[member].astype(jnp.float32), 0),
                jnp.sum(grad_value[member].astype(jnp.float32), 0),
            ]
        ),
    )
    for slot_index, update in enumerate(updates):
        grad_totals[slot_index] = add_block(grad_totals[slot_index], update, chosen)
    input_grad = jnp.stack(input_rows)
    shard_grads = tuple(
        (
            lax.psum_scatter(grad_totals[0], ("dp", "seq"), scatter_dimension=1, tiled=True),
            lax.psum_scatter(grad_totals[1], ("dp", "seq"), scatter_dimension=1, tiled=True),
            lax.psum_scatter(grad_totals[2], ("dp", "seq"), scatter_dimension=1, tiled=True),
            lax.psum_scatter(grad_totals[3], ("dp", "seq"), scatter_dimension=1, tiled=True),
            lax.psum_scatter(grad_totals[4], ("dp", "seq"), scatter_dimension=1, tiled=True),
            lax.psum_scatter(grad_totals[5], ("dp", "seq"), scatter_dimension=1, tiled=True),
            lax.psum_scatter(grad_totals[6], ("dp", "seq"), scatter_dimension=1, tiled=True),
            lax.psum_scatter(grad_totals[7], ("dp", "seq"), scatter_dimension=1, tiled=True),
            lax.psum_scatter(grad_totals[8], ("dp", "seq"), scatter_dimension=1, tiled=True),
            lax.psum_scatter(grad_totals[9], ("dp", "seq"), scatter_dimension=1, tiled=True),
            lax.psum_scatter(grad_totals[10], ("dp", "seq"), scatter_dimension=1, tiled=True),
            lax.psum_scatter(grad_totals[11], ("dp", "seq"), scatter_dimension=1, tiled=True),
        )
    )
    return (layer_out, input_grad) + shard_grads


bf16 = jnp.bfloat16
f32 = jnp.float32
SMALL = 64
score_scale = 1.0 / math.sqrt(HEAD_DIM)
gelu_root = math.sqrt(2.0 / math.pi)
gelu_cube = 0.044715
SMEM = pl.BlockSpec(memory_space=pltpu.SMEM)
VMEM = pl.BlockSpec(memory_space=pltpu.VMEM)


def dot(a, b, ca=1, cb=0):
    return lax.dot_general(a, b, (((ca,), (cb,)), ((), ())), preferred_element_type=f32)


def norm_parts(values):
    row_mean = jnp.mean(values, -1, keepdims=True)
    centred = values - row_mean
    row_var = jnp.mean(centred * centred, -1, keepdims=True)
    scale = lax.rsqrt(row_var + epsilon)
    return centred * scale, scale


def norm_back(normal, scale, gain, grad):
    scaled = grad * gain
    return scale * (
        scaled
        - jnp.mean(scaled, -1, keepdims=True)
        - normal * jnp.mean(scaled * normal, -1, keepdims=True)
    )


def head_mask(rows, width, head):
    lane = lax.broadcasted_iota(jnp.int32, (rows, width), 1)
    return (lane >= head * HEAD_DIM) & (lane < (head + 1) * HEAD_DIM)


class Held:
    def __init__(self, ref, copy):
        self.ref, self.copy = ref, copy
        self.shape, self.dtype = ref.shape, ref.dtype

    def __getitem__(self, at):
        if self.copy is not None:
            self.copy.wait()
            self.copy = None
        return self.ref[at]


class Made:
    def __init__(self, ref, copy):
        self.ref, self.copy = ref, copy
        self.shape, self.dtype = ref.shape, ref.dtype
        self.flushed = False

    def __getitem__(self, at):
        return self.ref[at]

    def __setitem__(self, at, value):
        self.ref[at] = value

    def flush(self):
        if not self.flushed:
            self.copy.start()
            self.flushed = True


COST = 1.0


def run(kernel, outs, *args, scalars=(), scratch=(), us=1.0, room=60, name=None):
    shapes = [jax.ShapeDtypeStruct(shape, dtype) for shape, dtype in outs]
    far = [k for k in range(len(args)) if k not in scalars]

    def body(*refs):
        ins, refs = list(refs[: len(args)]), refs[len(args) :]
        targets, refs = refs[: len(outs)], refs[len(outs) :]
        own, refs = refs[: len(scratch)], refs[len(scratch) :]
        held, refs = refs[: len(far)], refs[len(far) :]
        made, (in_sems, out_sems) = refs[: len(outs)], refs[len(outs) :]
        for n, k in enumerate(far):
            copy = pltpu.make_async_copy(ins[k], held[n], in_sems.at[n])
            copy.start()
            ins[k] = Held(held[n], copy)
        results = [
            Made(made[n], pltpu.make_async_copy(made[n], targets[n], out_sems.at[n]))
            for n in range(len(outs))
        ]
        kernel(*ins, *results, *own)
        for k in far:
            if ins[k].copy is not None:
                ins[k].copy.wait()
        for result in results:
            result.flush()
        for result in results:
            result.copy.wait()

    hbm = pl.BlockSpec(memory_space=pl.ANY)
    return pl.pallas_call(
        body,
        out_shape=shapes,
        in_specs=[SMEM if k in scalars else hbm for k in range(len(args))],
        out_specs=[hbm] * len(outs),
        scratch_shapes=list(scratch)
        + [pltpu.VMEM(args[k].shape, args[k].dtype) for k in far]
        + [pltpu.VMEM(out.shape, out.dtype) for out in shapes]
        + [
            pltpu.SemaphoreType.DMA((max(len(far), 1),)),
            pltpu.SemaphoreType.DMA((len(outs),)),
        ],
        compiler_params=pltpu.CompilerParams(vmem_limit_bytes=room * 1024 * 1024),
        cost_estimate=pl.CostEstimate(
            flops=int(us * COST * 1e9), bytes_accessed=int(us * COST * 3.5e6), transcendentals=0
        ),
        name=name,
    )(*args)


def by_head(values):
    size, width = values.shape
    blank = jnp.zeros_like(values)
    return jnp.concatenate(
        [
            jnp.where(head_mask(size, width, head), values, blank)
            for head in range(width // HEAD_DIM)
        ],
        0,
    )


def where_am_i(group):
    place = lax.axis_index("seq")
    return lax.axis_index("dp"), place // group, place % group


def ties_of(tie_refs):
    ranks = len(tie_refs)
    rank = lax.axis_index("dp")

    def tie_of(seq):
        step = lax.rem(seq + ranks - rank, ranks)
        tie = tie_refs[0][0]
        for k in range(1, ranks):
            tie = jnp.where(step == k, tie_refs[k][0], tie)
        return tie

    return tie_of


def one_hot(at_ref, rows):
    at = at_ref[...]
    row = lax.broadcasted_iota(jnp.int32, (rows, at.shape[1]), 0)
    return jnp.where(row == at, 1.0, 0.0).astype(bf16)


def flat_rows(value):
    return value.astype(f32).reshape(-1, value.shape[-1]).astype(value.dtype)


def pack_kernel(group, ranks, *refs):
    refs, scr_ref = refs[:-1], refs[-1]
    tie_of, refs = ties_of(refs[:ranks]), refs[ranks:]
    qkv_ref, out_w_ref, vectors, out_ref, cols_ref = refs[0], refs[1], refs[2:10], refs[10], refs[11]
    ties, rows, _ = qkv_ref.shape
    planes = ranks
    model = qkv_ref.shape[2] // 3
    width = model // ranks
    shape = (16, SMALL)
    eye = lax.broadcasted_iota(jnp.int32, shape, 0) == lax.broadcasted_iota(jnp.int32, shape, 1)
    eye = jnp.where(eye, 1.0, 0.0).astype(bf16)
    for tie in range(ties):
        lines = []
        for ref in vectors:
            line = ref[tie : tie + 1].astype(f32)
            for at in range(line.shape[1] // rows):
                lines.append(line[:, at * rows : (at + 1) * rows])
        lines.append(jnp.zeros((16 - len(lines), rows), f32))
        small = dot(jnp.concatenate(lines, 0).astype(bf16), eye, 0, 0).astype(bf16)
        qkv = qkv_ref[tie]
        for to in range(ranks):
            cols = [
                qkv[:, k * model + to * width : k * model + (to + 1) * width] for k in range(3)
            ]
            scr_ref[tie, to] = jnp.concatenate(cols + [small], 1)
    for seq in range(planes):
        tie = tie_of(seq)
        for to in range(ranks):
            out_ref[to * planes + seq] = scr_ref[tie, to]
    out_ref.flush()
    blank = jnp.zeros((cols_ref.shape[1] - rows, model), f32)
    for seq in range(planes):
        cols = jnp.concatenate([out_w_ref[tie_of(seq)].astype(f32), blank], 0)
        cols_ref[seq] = cols.astype(bf16)


def pack_late_kernel(ranks, *refs):
    tie_of = ties_of(refs[:ranks])
    fc_ref, proj_ref, fc_out_ref, proj_out_ref = refs[ranks:]
    planes = proj_out_ref.shape[0]
    part = fc_ref.shape[2] // ranks
    for seq in range(planes):
        fc = fc_ref[tie_of(seq)]
        for to in range(ranks):
            fc_out_ref[to * planes + seq] = fc[:, to * part : (to + 1) * part]
    fc_out_ref.flush()
    for seq in range(planes):
        proj_out_ref[seq] = proj_ref[tie_of(seq)]


def project_kernel(group, x_ref, *refs):
    w_refs, refs = refs[:group], refs[group:]
    sel_ref, bsel_ref, mask_ref, q_ref, kv_ref, h_ref, vec_ref, fcb_ref, w_ref = refs
    ranks, size, width = q_ref.shape
    part = fcb_ref.shape[1]
    model = x_ref.shape[1]
    sel = one_hot(sel_ref, model)
    bsel = one_hot(bsel_ref, model)
    normal, _ = norm_parts(x_ref[...].astype(f32))
    rows = w_ref.shape[0] // group
    for slot, ref in enumerate(w_refs):
        w_ref[slot * rows : (slot + 1) * rows] = flat_rows(ref[...])
    w_ref.flush()
    small = w_ref[:, 3 * width :]
    spread = dot(small, sel, 0, 0)[:16]
    normed = (normal * spread[0:1] + spread[1:2]).astype(bf16)
    normed = dot(normed, sel, 1, 1).astype(bf16)
    mixed = dot(normed, w_ref[:, : 3 * width])
    biases = jnp.sum(dot(small, bsel, 0, 0)[:16] * mask_ref[...], 0, keepdims=True)
    bias = biases[:, part:]
    kv_ref[0] = mixed[:, width : 2 * width].astype(bf16).reshape(ranks, size, width)
    value = (mixed[:, 2 * width :] + bias[:, width:]).astype(bf16)
    kv_ref[1] = value.reshape(ranks, size, width)
    kv_ref.flush()
    query = (mixed[:, :width] + bias[:, :width]).astype(bf16) * jnp.asarray(score_scale, bf16)
    q_ref[...] = query.reshape(ranks, size, width)
    h_ref[...] = normed
    vec_ref[...] = spread[:8]
    fcb_ref[...] = jnp.broadcast_to(biases[:, :part], fcb_ref.shape)


def attend_kernel(group, rows, q_ref, *refs):
    kv_refs, refs = refs[:group], refs[group:]
    cols_refs, refs = refs[:group], refs[group:]
    a_ref, lse_ref, w_ref, sums_refs, (whole_ref, sums_ref) = *refs[:3], refs[3:-2], refs[-2:]
    rank, _, member = where_am_i(group)
    chunks, size, width = q_ref.shape
    for chunk in range(chunks):
        count = (chunk + 1) * size
        keys = jnp.concatenate([r[0, : chunk + 1].reshape(count, width) for r in kv_refs], 0)
        values = jnp.concatenate([r[1, : chunk + 1].reshape(count, width) for r in kv_refs], 0)
        values_t = values.T
        scores = dot(keys, by_head(q_ref[chunk]), 1, 1)
        top = jnp.max(scores, 0, keepdims=True)
        raised = jnp.exp(scores - top)
        total = jnp.sum(raised, 0, keepdims=True)
        lse_ref[chunk : chunk + 1] = top + jnp.log(total)
        mixed = dot(values_t, raised.astype(bf16)) / total
        parts = [
            mixed[head * HEAD_DIM : (head + 1) * HEAD_DIM, head * size : (head + 1) * size]
            for head in range(width // HEAD_DIM)
        ]
        a_ref[chunk * size : (chunk + 1) * size] = jnp.concatenate(parts, 0).T.astype(bf16)
    a_ref.flush()
    lse_ref.flush()
    for plane in range(cols_refs[0].shape[0]):
        pieces = [ref[plane].astype(f32)[:rows] for ref in cols_refs]
        for owner in range(group):
            piece = pieces[0]
            for slot in range(1, group):
                here = lax.rem(member + slot, group) == owner
                piece = jnp.where(here, pieces[slot], piece)
            at = (plane * group + owner) * rows
            whole_ref[at : at + rows] = piece
    w_ref[...] = whole_ref[...].astype(bf16)
    sums_ref[...] = dot(a_ref[...], w_ref[...]).astype(bf16).reshape(sums_ref.shape)
    for k, ref in enumerate(sums_refs):
        ref[...] = sums_ref[lax.rem(rank + k, chunks)]
        ref.flush()


def join_kernel(ranks, *refs):
    parts, (x_ref, vec_ref, sel_ref, r_ref, h_ref) = refs[:ranks], refs[ranks:]
    total = x_ref[...].astype(f32) + vec_ref[2:3]
    for ref in parts:
        total = total + ref[...].astype(f32)
    r_ref[...] = total
    r_ref.flush()
    normal, _ = norm_parts(total)
    normed = (normal * vec_ref[3:4] + vec_ref[4:5]).astype(bf16)
    h_ref[...] = dot(normed, one_hot(sel_ref, normed.shape[1]), 1, 1).astype(bf16)


def mlp_kernel(group, ranks, h_ref, *refs):
    f_refs, refs = refs[:group], refs[group:]
    fcb_ref, refs = refs[0], refs[1:]
    g_refs, refs = refs[:ranks], refs[ranks:]
    p_refs, refs = refs[:group], refs[group:]
    sel_ref, refs = refs[0], refs[1:]
    dh_refs, refs = refs[:ranks], refs[ranks:]
    y_ref, g_ref, hid_ref, pre_ref, wf_ref, wp_ref, dh_ref = refs
    size = y_ref.shape[1]
    planes, _, model = p_refs[0].shape
    hid_rows = wp_ref.shape[0] // (planes * group)
    rank, _, member = where_am_i(group)
    rows = wf_ref.shape[0] // group
    for slot, ref in enumerate(f_refs):
        wf_ref[slot * rows : (slot + 1) * rows] = flat_rows(ref[...])
    value = dot(h_ref[...], wf_ref[...]) + fcb_ref[0:1]
    for slot, ref in enumerate(p_refs):
        for plane in range(planes):
            at = plane * group + lax.rem(member + slot, group)
            start = pl.multiple_of(at * hid_rows, 16)
            wp_ref[pl.ds(start, hid_rows)] = ref[plane, :hid_rows]
    for k, ref in enumerate(g_refs):
        start = pl.multiple_of(lax.rem(rank + k, ranks) * size, size)
        g_ref[pl.ds(start, size)] = ref[...]
    g_ref.flush()
    grad = dot(g_ref[...], wp_ref[...], 1, 1)
    squared = value * value
    bent = jnp.tanh(gelu_root * value * (1.0 + gelu_cube * squared))
    half = 0.5 * (1.0 + bent)
    slope = half + (0.5 * gelu_root) * value * (1.0 - bent * bent) * (
        1.0 + 3.0 * gelu_cube * squared
    )
    pre_ref[...] = (grad * slope).astype(bf16)
    pre_ref.flush()
    below = dot(pre_ref[...], wf_ref[...], 1, 1).astype(bf16)
    dh_ref[...] = dot(below, one_hot(sel_ref, model)).astype(bf16).reshape(ranks, size, model)
    for k, ref in enumerate(dh_refs):
        ref[...] = dh_ref[lax.rem(rank + k, ranks)]
        ref.flush()
    hid_ref[...] = (value * half).astype(bf16)
    hid_ref.flush()
    y_ref[...] = dot(hid_ref[...], wp_ref[...]).astype(bf16).reshape(ranks, size, model)


def mlp_grad_kernel(group, planes, h_ref, pre_ref, hid_ref, g_ref, *refs):
    out_refs, fcb_ref, scr_ref = refs[:group], refs[group], refs[group + 1]
    half = scr_ref.shape[0] // group
    whole = dot(h_ref[...], pre_ref[...], 0, 0)
    for slot, ref in enumerate(out_refs):
        ref[:half] = whole[slot * half : (slot + 1) * half].astype(ref.dtype)
    scr_ref[...] = dot(hid_ref[...], g_ref[...], 0, 0)
    member = where_am_i(group)[2]
    hid_rows = half // planes
    for slot in range(group - 1, -1, -1):
        ref = out_refs[slot]
        for plane in range(planes):
            at = plane * group + lax.rem(member + slot, group)
            start = pl.multiple_of(at * hid_rows, 16)
            to = half + plane * hid_rows
            ref[to : to + hid_rows] = scr_ref[pl.ds(start, hid_rows)].astype(ref.dtype)
        ref.flush()
    fcb_ref[...] = jnp.broadcast_to(
        jnp.sum(pre_ref[...].astype(f32), 0, keepdims=True), fcb_ref.shape
    )


def add_late_kernel(group, *refs):
    parts, (fc_ref, proj_ref) = refs[:group], refs[group:]
    total = parts[0][...]
    for ref in parts[1:]:
        total = total + ref[...].astype(f32)
    half = total.shape[0] // 2
    proj_ref[...] = total[half:].reshape(proj_ref.shape).astype(bf16)
    proj_ref.flush()
    fc_ref[...] = total[:half].reshape(fc_ref.shape).astype(bf16)


def join_back_kernel(ranks, *refs):
    parts, (r_ref, g_ref, vec_ref, dr_ref, low_ref, sums_ref) = refs[:ranks], refs[ranks:]
    normal, scale = norm_parts(r_ref[...])
    upstream = g_ref[...].astype(f32)
    grad = parts[0][...].astype(f32)
    for ref in parts[1:]:
        grad = grad + ref[...].astype(f32)
    total = upstream + norm_back(normal, scale, vec_ref[3:4], grad)
    low_ref[...] = total.astype(bf16)
    low_ref.flush()
    dr_ref[...] = total
    dr_ref.flush()
    sums_ref[...] = jnp.concatenate(
        [
            jnp.sum(total, 0, keepdims=True),
            jnp.sum(grad * normal, 0, keepdims=True),
            jnp.sum(grad, 0, keepdims=True),
            jnp.sum(upstream, 0, keepdims=True),
        ]
        + [jnp.zeros((4, total.shape[1]), f32)],
        0,
    )


def layer_kernel(parts_ref, r_ref, vec_ref, out_ref):
    total = r_ref[...] + vec_ref[5:6]
    for rank in range(parts_ref.shape[0]):
        total = total + parts_ref[rank].astype(f32)
    out_ref[...] = total.astype(bf16)


def attend_back_kernel(group, low_ref, wo_ref, q_ref, *refs):
    kv_refs, refs = refs[:group], refs[group:]
    lse_ref, a_ref, refs = refs[0], refs[1], refs[2:]
    dkv_refs, dq_ref, dwo_refs, (scr_ref, wo_scr) = (
        refs[:group],
        refs[group],
        refs[group + 1 : -2],
        refs[-2:],
    )
    chunks, size, width = q_ref.shape
    heads = width // HEAD_DIM
    grad_all_rows = dot(low_ref[...], wo_ref[...], 1, 1).astype(bf16)
    for chunk in range(chunks - 1, -1, -1):
        count = (chunk + 1) * size
        keys = jnp.concatenate([r[0, : chunk + 1].reshape(count, width) for r in kv_refs], 0)
        values = jnp.concatenate([r[1, : chunk + 1].reshape(count, width) for r in kv_refs], 0)
        keys_t = keys.T
        query = by_head(q_ref[chunk])
        grad = by_head(grad_all_rows[chunk * size : (chunk + 1) * size])
        probs = jnp.exp(dot(keys, query, 1, 1) - lse_ref[chunk : chunk + 1])
        grad_probs = dot(values, grad, 1, 1)
        delta = jnp.sum(probs * grad_probs, 0, keepdims=True)
        grad_scores = (probs * (grad_probs - delta)).astype(bf16)
        turned = dot(keys_t, grad_scores)
        parts = [
            turned[head * HEAD_DIM : (head + 1) * HEAD_DIM, head * size : (head + 1) * size]
            for head in range(heads)
        ]
        dq_ref[chunk * size : (chunk + 1) * size] = (
            jnp.concatenate(parts, 0).T * score_scale
        ).astype(bf16)
        both = (dot(grad_scores, query), dot(probs.astype(bf16), grad))
        for slot in range(group):
            for k in range(2):
                value = both[k][slot * count : (slot + 1) * count].reshape(chunk + 1, size, width)
                if chunk == chunks - 1:
                    scr_ref[slot, k] = value
                else:
                    scr_ref[slot, k, : chunk + 1] = scr_ref[slot, k, : chunk + 1] + value
    for slot in range(group - 1, -1, -1):
        dkv_refs[slot][...] = scr_ref[slot].astype(dkv_refs[slot].dtype)
        dkv_refs[slot].flush()
    dq_ref.flush()
    wo_scr[...] = dot(a_ref[...], low_ref[...], 0, 0).reshape(wo_scr.shape)
    for slot in range(group - 1, -1, -1):
        owner = lax.rem(where_am_i(group)[2] + slot, group)
        for plane in range(wo_scr.shape[0]):
            dwo_refs[slot][plane] = wo_scr[plane, owner].astype(dwo_refs[slot].dtype)


def first_kernel(group, ranks, dq_ref, *refs):
    dkv_refs, refs = refs[:group], refs[group:]
    w_ref, sel_ref, refs = refs[0], refs[1], refs[2:]
    dwo_refs, refs = refs[:group], refs[group:]
    proj_ref, refs = refs[0], refs[1:]
    dh_refs, (dh_ref, mix_ref, late_ref) = refs[:ranks], refs[ranks:]
    tokens, width = dq_ref.shape
    model = sel_ref.shape[1]
    size = tokens // ranks
    low = [dq_ref[...]]
    for k in range(2):
        total = dkv_refs[0][k]
        for ref in dkv_refs[1:]:
            total = total + ref[k].astype(f32)
        low.append(total.reshape(tokens, width).astype(bf16))
    mixed = jnp.concatenate(low, 1)
    mix_ref[...] = mixed
    mix_ref.flush()
    below = dot(mixed, w_ref[:, : 3 * width], 1, 1).astype(bf16)
    dh_ref[...] = dot(below, one_hot(sel_ref, model)).astype(bf16).reshape(ranks, size, model)
    for k, ref in enumerate(dh_refs):
        ref[...] = dh_ref[lax.rem(where_am_i(group)[0] + k, ranks)]
        ref.flush()
    dh_ref.flush()
    total = dwo_refs[0][...]
    for ref in dwo_refs[1:]:
        total = total + ref[...].astype(f32)
    hid_rows = proj_ref.shape[1]
    rest = late_ref.shape[1] - hid_rows - total.shape[1]
    for plane in range(total.shape[0]):
        late_ref[plane, :hid_rows] = proj_ref[plane]
        late_ref[plane, hid_rows:] = jnp.concatenate(
            [total[plane], jnp.zeros((rest, model), f32)], 0
        ).astype(bf16)


def first_grad_kernel(
    group, h_ref, mix_ref, x_ref, dh_ref, sums_ref, fcb_ref, mask_ref, sel_ref, bsel_ref, *refs
):
    ranks, size, model = dh_ref.shape
    width = mix_ref.shape[1] // 3
    part = fcb_ref.shape[1]
    mixed = mix_ref[...]
    whole = dot(h_ref[...], mixed, 0, 0)
    normal, _ = norm_parts(x_ref[...].astype(f32))
    grad = dh_ref[...].reshape(ranks * size, model).astype(f32)
    vec = jnp.concatenate(
        [
            jnp.sum(grad * normal, 0, keepdims=True),
            jnp.sum(grad, 0, keepdims=True),
            sums_ref[0:4],
            jnp.zeros((2, model), f32),
        ],
        0,
    )
    cols = jnp.sum(mixed.astype(f32), 0, keepdims=True)
    both = jnp.concatenate([cols[:, :width], cols[:, 2 * width :]], 1)
    sums = jnp.concatenate([fcb_ref[0:1], both], 1) * mask_ref[...]
    small = dot(one_hot(sel_ref, model), vec.astype(bf16), 1, 1)
    more = dot(one_hot(bsel_ref, model), sums.astype(bf16), 1, 1)
    rest = jnp.zeros((model, SMALL - 24), f32)
    whole = jnp.concatenate([whole, small, more, rest], 1)
    rows = model // group
    for slot in range(group - 1, -1, -1):
        refs[slot][...] = whole[slot * rows : (slot + 1) * rows].astype(refs[slot].dtype)
        refs[slot].flush()


def add_early_kernel(group, *refs):
    parts, out_ref = refs[:group], refs[group]
    total = parts[0][...]
    for ref in parts[1:]:
        total = total + ref[...].astype(f32)
    out_ref[...] = total.reshape(out_ref.shape).astype(bf16)


def last_kernel(ranks, *refs):
    parts, (x_ref, vec_ref, dr_ref, out_ref) = refs[:ranks], refs[ranks:]
    normal, scale = norm_parts(x_ref[...].astype(f32))
    grad = parts[0][...].astype(f32)
    for ref in parts[1:]:
        grad = grad + ref[...].astype(f32)
    out_ref[...] = (dr_ref[...] + norm_back(normal, scale, vec_ref[0:1], grad)).astype(bf16)


def by_block(ties, parts, tie_of):
    totals = [jnp.zeros(parts[0].shape, f32) for _ in range(ties)]
    for seq, part in enumerate(parts):
        value = part.astype(f32)
        for block in range(ties):
            totals[block] = totals[block] + jnp.where(tie_of(seq) == block, value, 0.0)
    return totals


def final_late_kernel(ranks, *refs):
    tie_of = ties_of(refs[:ranks])
    fc_in, rest_in, fc_ref, proj_ref, out_ref = refs[ranks:]
    ties, _, inner = fc_ref.shape
    planes = rest_in.shape[0]
    hid_rows, rows = proj_ref.shape[1], out_ref.shape[1]
    part = inner // ranks
    for block, total in enumerate(by_block(ties, [rest_in[k] for k in range(planes)], tie_of)):
        proj_ref[block] = total[:hid_rows]
        out_ref[block] = total[hid_rows : hid_rows + rows]
    proj_ref.flush()
    for rank in range(ranks):
        parts = [fc_in[rank * planes + k] for k in range(planes)]
        for block, total in enumerate(by_block(ties, parts, tie_of)):
            fc_ref[block, :, rank * part : (rank + 1) * part] = total


def final_kernel(ranks, *refs):
    tie_of = ties_of(refs[:ranks])
    home_ref, qkv_ref, *small_refs = refs[ranks:]
    ties, rows, wide = qkv_ref.shape
    model = wide // 3
    planes = home_ref.shape[0] // ranks
    width = model // ranks
    sums = []
    for rank in range(ranks):
        parts = [home_ref[rank * planes + k] for k in range(planes)]
        sums.append(by_block(ties, parts, tie_of))
    eye = lax.broadcasted_iota(jnp.int32, (SMALL, SMALL), 0)
    eye = jnp.where(eye == lax.broadcasted_iota(jnp.int32, (SMALL, SMALL), 1), 1.0, 0.0)
    eye = eye.astype(bf16)
    for block in range(ties):
        values = [sums[rank][block] for rank in range(ranks)]
        qkv_ref[block] = jnp.concatenate(
            [value[:, k * width : (k + 1) * width] for k in range(3) for value in values], 1
        )
        small = values[0][:, 3 * width :]
        for value in values[1:]:
            small = small + value[:, 3 * width :]
        high = small.astype(bf16)
        low = (small - high.astype(f32)).astype(bf16)
        turned = dot(eye, high, 1, 1) + dot(eye, low, 1, 1)
        for k in range(6):
            small_refs[k][block : block + 1] = turned[k : k + 1]
        small_refs[6][block : block + 1] = jnp.concatenate(
            [turned[k : k + 1] for k in range(14, 16)], 1
        )
        small_refs[7][block : block + 1] = jnp.concatenate(
            [turned[k : k + 1] for k in range(16, 20)], 1
        )


def fast_device(
    n_dp,
    n_seq,
    tokens,
    tie_index,
    first_gain,
    first_shift,
    qkv_weight,
    qv_bias,
    out_weight,
    out_bias,
    second_gain,
    second_shift,
    fc_weight,
    fc_bias,
    proj_weight,
    proj_bias,
    cotangent,
):
    ranks, planes, group = n_dp, n_dp, n_seq // n_dp
    axes = ("dp", "seq")
    size, model = tokens.shape[1:]
    ties, rows = qkv_weight.shape[:2]
    hid_rows = proj_weight.shape[1]
    inner = fc_weight.shape[2]
    width = model // ranks
    part = inner // ranks
    count = ranks * size
    lanes = 3 * width + SMALL
    heads_here = width // HEAD_DIM
    squads = ranks * planes
    rank = lax.axis_index("dp")
    place = lax.axis_index("seq")
    plane, member = place // group, place % group

    def route(where):
        pairs = []
        for a in range(ranks):
            for b in range(planes):
                for c in range(group):
                    x, y, z = where(a, b, c)
                    pairs.append((a * n_seq + b * group + c, x * n_seq + y * group + z))
        return pairs

    swap = route(lambda a, b, c: (b, a, c))
    to_rank = [route(lambda a, b, c, k=k: ((a + k) % ranks, b, c)) for k in range(ranks)]
    to_plane = [route(lambda a, b, c, k=k: (a, (b + k) % planes, c)) for k in range(planes)]
    to_member = [route(lambda a, b, c, k=k: (a, b, (c + k) % group)) for k in range(group)]
    same_member = [[b * group + c for b in range(planes)] for c in range(group)]
    squad = [
        [a * n_seq + b * group + c for a in range(ranks) for b in range(planes)]
        for c in range(group)
    ]

    def send(values, pairs):
        return lax.ppermute(values, axes, pairs)

    def from_members(piece):
        return [piece] + [send(piece, to_member[group - k]) for k in range(1, group)]

    def over_members(parts):
        return [parts[0]] + [send(parts[k], to_member[k]) for k in range(1, group)]

    def over_planes(pieces):
        return lax.all_to_all(pieces, "seq", 0, 0, axis_index_groups=same_member)

    def over_squad(pieces):
        return lax.all_to_all(pieces, axes, 0, 0, axis_index_groups=squad)

    def scatter(parts):
        return [parts[0]] + [send(parts[k], to_rank[k]) for k in range(1, ranks)]

    def gate(value, *before):
        return lax.optimization_barrier((value, before))[0]

    ties_seen = [tie_index] + [send(tie_index, to_rank[ranks - k]) for k in range(1, ranks)]
    scalar_ties = tuple(range(ranks))
    tokens_own = send(tokens[0], swap)

    cols_rows = (rows + 15) // 16 * 16
    early, cols = run(
        functools.partial(pack_kernel, group, ranks),
        [((squads, rows, lanes), bf16), ((planes, cols_rows, model), bf16)],
        *ties_seen,
        qkv_weight,
        out_weight,
        first_gain,
        first_shift,
        out_bias,
        second_gain,
        second_shift,
        proj_bias,
        qv_bias,
        fc_bias,
        scalars=scalar_ties,
        scratch=[pltpu.VMEM((ties, ranks, rows, lanes), bf16)],
        us=2.0,
        name="pack",
    )
    packed = early
    early = over_squad(early)

    def arrival(owner, row):
        a, b, c = owner // n_seq, (owner % n_seq) // group, owner % group
        slot = (c + group - member) % group
        return (slot * squads + a * planes + b) * rows + row

    flat = jnp.arange(model)
    at_model = arrival(flat // rows, flat % rows)
    unit = jnp.arange(part) + rank * part
    at_fc = arrival(unit // (4 * rows), unit % rows)
    flat_qv = jnp.arange(2 * width)
    unit_qv = (flat_qv // width) * model + rank * width + flat_qv % width
    at_qv = arrival(unit_qv // (2 * rows), unit_qv % rows)
    at_bias = jnp.concatenate([at_fc, at_qv])
    lanes_of = jnp.concatenate(
        [
            (jnp.arange(part) % (4 * rows)) // rows + 8,
            (unit_qv % (2 * rows)) // rows + 6,
        ]
    )
    sel = at_model[None].astype(jnp.int32)
    bsel = at_bias[None].astype(jnp.int32)
    row_mask = (jnp.arange(16)[:, None] == lanes_of[None, :]).astype(f32)

    tokens_all = lax.all_gather(tokens_own, "dp", axis=0, tiled=True)
    early = gate(early, tokens_all, sel, bsel, row_mask)
    cols = over_planes(gate(cols, early))
    late_rows = hid_rows + cols_rows
    early = from_members(early)
    own = ((size, model), bf16)
    q, kv, h_one, vec, fcb, w_early = run(
        functools.partial(project_kernel, group),
        [
            ((ranks, size, width), bf16),
            ((2, ranks, size, width), bf16),
            ((count, model), bf16),
            ((8, model), f32),
            ((8, part), f32),
            ((model, lanes), bf16),
        ],
        tokens_all,
        *early,
        sel,
        bsel,
        row_mask,
        room=20,
        us=5.0,
        name="project",
    )
    grad_own = send(gate(cotangent[0], tokens_all), swap)
    late_fc, late_proj = run(
        functools.partial(pack_late_kernel, ranks),
        [((squads, rows, part), bf16), ((planes, hid_rows, model), bf16)],
        *ties_seen,
        gate(fc_weight, q),
        proj_weight,
        scalars=scalar_ties,
        us=2.0,
        name="pack_late",
    )
    cols = from_members(gate(cols, q))
    late_fc = over_squad(gate(late_fc, grad_own, cols))
    kv = from_members(gate(kv, grad_own))
    grads_seen = [grad_own] + [send(grad_own, to_rank[ranks - k]) for k in range(1, ranks)]
    attended, lse, w_out, *sums = run(
        functools.partial(attend_kernel, group, rows),
        [((count, width), bf16), ((8, heads_here * size), f32), ((width, model), bf16)] + [own] * ranks,
        q,
        *kv,
        *cols,
        scratch=[pltpu.VMEM((width, model), f32), pltpu.VMEM((ranks, size, model), bf16)],
        us=6.0,
        name="attend",
    )
    sums = scatter(sums)
    late_fc = gate(late_fc, attended, grads_seen)
    late_proj = over_planes(gate(late_proj, late_fc))
    late_fc = from_members(late_fc)
    middle, h_own = run(
        functools.partial(join_kernel, ranks),
        [((size, model), f32), own],
        *sums,
        tokens_own,
        gate(vec, grads_seen),
        sel,
        room=16,
        us=2.0,
        name="join",
    )
    late_proj = from_members(gate(late_proj, h_own))
    h_two = lax.all_gather(h_own, "dp", axis=0, tiled=True)
    rest = run(
        functools.partial(mlp_kernel, group, ranks),
        [own] * ranks
        + [((ranks, size, model), bf16), ((count, model), bf16)]
        + [((count, part), bf16)] * 2,
        h_two,
        *late_fc,
        fcb,
        *grads_seen,
        *late_proj,
        sel,
        scratch=[
            pltpu.VMEM((model, part), bf16),
            pltpu.VMEM((part, model), bf16),
            pltpu.VMEM((ranks, size, model), bf16),
        ],
        us=7.0,
        name="mlp",
    )
    below, (layer_parts, grad_all, hidden, grad_pre) = rest[:ranks], rest[ranks:]
    below = scatter(below)
    half = 2 * (model // group)
    *late, fc_sums = run(
        functools.partial(mlp_grad_kernel, group, planes),
        [((half, model), f32)]
        + [((half, model), bf16)] * (group - 1)
        + [((8, part), f32)],
        h_two,
        grad_pre,
        hidden,
        grad_all,
        scratch=[pltpu.VMEM((part, model), f32)],
        us=4.0,
        name="mlp_grad",
    )
    late = over_members(late)
    grad_middle, low_own, own_sums = run(
        functools.partial(join_back_kernel, ranks),
        [((size, model), f32), own, ((8, model), f32)],
        *below,
        middle,
        grad_own,
        vec,
        room=16,
        us=30.0,
        name="join_back",
    )
    late = gate(late, low_own)
    late_fc, late_proj = run(
        functools.partial(add_late_kernel, group),
        [((squads, rows, part), bf16), ((planes, hid_rows, model), bf16)],
        *late,
        room=16,
        us=2.0,
        name="add_late",
    )
    low = lax.all_gather(gate(low_own, late_fc), "dp", axis=0, tiled=True)
    late_fc = over_squad(late_fc)
    layer_parts = lax.all_to_all(gate(layer_parts, low, late_fc), "dp", 0, 0)
    (layer_own,) = run(
        layer_kernel,
        [own],
        layer_parts,
        middle,
        vec,
        room=16,
        us=1.0,
        name="layer",
    )
    layer_out = send(layer_own, swap)
    rest = run(
        functools.partial(attend_back_kernel, group),
        [((2, ranks, size, width), f32)]
        + [((2, ranks, size, width), bf16)] * (group - 1)
        + [((count, width), bf16)]
        + [((planes, rows, model), f32)]
        + [((planes, rows, model), bf16)] * (group - 1),
        low,
        w_out,
        q,
        *kv,
        lse,
        attended,
        scratch=[
            pltpu.VMEM((group, 2, ranks, size, width), f32),
            pltpu.VMEM((planes, group, rows, model), f32),
        ],
        us=10.0,
        name="attend_back",
    )
    dkv, dq, dw_out = rest[:group], rest[group], rest[group + 1 :]
    dkv = over_members(dkv)
    dw_out = over_members(dw_out)
    rest = run(
        functools.partial(first_kernel, group, ranks),
        [own] * ranks
        + [
            ((ranks, size, model), bf16),
            ((count, 3 * width), bf16),
            ((planes, late_rows, model), bf16),
        ],
        dq,
        *dkv,
        gate(w_early, layer_own),
        sel,
        *dw_out,
        late_proj,
        us=4.0,
        name="first",
    )
    first_parts, (first_all, mixed, late_rest) = rest[:ranks], rest[ranks:]
    grad_first = scatter(first_parts)
    late_rest = over_planes(gate(late_rest, layer_parts))
    early = run(
        functools.partial(first_grad_kernel, group),
        [((model // group, lanes), f32)]
        + [((model // group, lanes), bf16)] * (group - 1),
        h_one,
        mixed,
        tokens_all,
        first_all,
        own_sums,
        fc_sums,
        row_mask,
        sel,
        bsel,
        us=5.0,
        name="first_grad",
    )
    early = over_members(early)
    (input_own,) = run(
        functools.partial(last_kernel, ranks),
        [own],
        *grad_first,
        tokens_own,
        vec,
        grad_middle,
        room=16,
        us=30.0,
        name="last",
    )
    early = gate(early, input_own, layer_out)
    (early,) = run(
        functools.partial(add_early_kernel, group),
        [((squads, rows, lanes), bf16)],
        *early,
        room=16,
        us=1.0,
        name="add_early",
    )
    input_grad = send(input_own, swap)
    early = over_squad(early)
    grad_fc_weight, grad_proj_weight, grad_out_weight = run(
        functools.partial(final_late_kernel, ranks),
        [((ties, rows, inner), f32), ((ties, hid_rows, model), f32), ((ties, rows, model), f32)],
        *ties_seen,
        late_fc,
        gate(late_rest, input_own),
        scalars=scalar_ties,
        us=3.0,
        name="final_late",
    )
    early = gate(early, grad_fc_weight)
    grad_qkv_weight, *small = run(
        functools.partial(final_kernel, ranks),
        [((ties, rows, 3 * model), f32)]
        + [((ties, rows), f32)] * 6
        + [((ties, 2 * rows), f32), ((ties, 4 * rows), f32)],
        *ties_seen,
        early,
        scalars=scalar_ties,
        room=16,
        us=1.0,
        name="final",
    )
    layer_out, input_grad = gate((layer_out, input_grad), grad_qkv_weight)
    return (
        layer_out[None],
        input_grad[None],
        small[0],
        small[1],
        grad_qkv_weight,
        small[6],
        grad_out_weight,
        small[2],
        small[3],
        small[4],
        grad_fc_weight,
        small[7],
        grad_proj_weight,
        small[5],
    )


def pick_device(n_dp, n_seq, *args):
    tokens, qkv_weight, proj_weight = args[0], args[4], args[12]
    size, rows, hid_rows = tokens.shape[1], qkv_weight.shape[1], proj_weight.shape[1]
    group = n_seq // n_dp
    whole_tiles = rows % 8 == 0 and (group * rows) % 16 == 0 and hid_rows % 16 == 0
    one_block = tokens.shape[0] == 1 and group == 2 and size * group == BLOCK
    if whole_tiles and one_block:
        return fast_device(n_dp, n_seq, *args)
    return per_device(*args)


def solution(mesh):
    in_specs = (
        P("dp", "seq", None),
        P("dp"),
        P(None, ("dp", "seq")),
        P(None, ("dp", "seq")),
        P(None, ("dp", "seq"), None),
        P(None, ("dp", "seq")),
        P(None, ("dp", "seq"), None),
        P(None, ("dp", "seq")),
        P(None, ("dp", "seq")),
        P(None, ("dp", "seq")),
        P(None, ("dp", "seq"), None),
        P(None, ("dp", "seq")),
        P(None, ("dp", "seq"), None),
        P(None, ("dp", "seq")),
        P("dp", "seq", None),
    )
    out_specs = (
        P("dp", "seq", None),
        P("dp", "seq", None),
        P(None, ("dp", "seq")),
        P(None, ("dp", "seq")),
        P(None, ("dp", "seq"), None),
        P(None, ("dp", "seq")),
        P(None, ("dp", "seq"), None),
        P(None, ("dp", "seq")),
        P(None, ("dp", "seq")),
        P(None, ("dp", "seq")),
        P(None, ("dp", "seq"), None),
        P(None, ("dp", "seq")),
        P(None, ("dp", "seq"), None),
        P(None, ("dp", "seq")),
    )
    return jax.shard_map(
        functools.partial(pick_device, mesh.shape["dp"], mesh.shape["seq"]),
        mesh=mesh,
        in_specs=in_specs,
        out_specs=out_specs,
        check_vma=False,
    )
```

```python
import functools
import math

import jax
import jax.numpy as jnp
from jax import lax
from jax.experimental import pallas as pl
from jax.experimental.pallas import tpu as pltpu
from jax.sharding import PartitionSpec as P

HEADS = 12
HEAD_DIM = 64
BLOCK = 256


epsilon = 1e-05
neg_large = -1e30


def norm_apply(values, norm_gain, norm_shift):
    row_mean = jnp.mean(values, -1, keepdims=True)
    centred = values - row_mean
    row_var = jnp.mean(centred * centred, -1, keepdims=True)
    return centred * lax.rsqrt(row_var + epsilon) * norm_gain + norm_shift


def gelu_tanh(values):
    return jax.nn.gelu(values, approximate=True)


def select_all(gathered, chosen):
    return tuple(
        (lax.dynamic_index_in_dim(stacked, chosen, 0, keepdims=False) for stacked in gathered)
    )


def add_block(totals, update, chosen):
    current = lax.dynamic_index_in_dim(totals, chosen, 0, keepdims=True)
    return lax.dynamic_update_index_in_dim(totals, current + update[None], chosen, 0)


def split_three(values):
    upper_part = values.astype(jnp.bfloat16)
    rest_one = values - lax.optimization_barrier(upper_part).astype(jnp.float32)
    middle_part = rest_one.astype(jnp.bfloat16)
    lower_part = (rest_one - lax.optimization_barrier(middle_part).astype(jnp.float32)).astype(
        jnp.bfloat16
    )
    return (upper_part, middle_part, lower_part)


def to_heads(flat_rows, head_count):
    return flat_rows.reshape(
        flat_rows.shape[0], flat_rows.shape[1], head_count, flat_rows.shape[2] // head_count
    )


def allowed_mask(query_pos, key_pos, block_len):
    return (key_pos[None, :] // block_len <= query_pos[:, None] // block_len)[None, :, None, :]


def make_forward_step(query_heads, positions, block_len, score_scale):
    last_block = positions[-1] // block_len
    head_count = query_heads.shape[2]

    def fold_step(carried, shard_piece, start_row):
        key_piece, value_piece = shard_piece
        key_count = key_piece.shape[1]
        step_len = math.gcd(key_count, 512)

        def one_part(fold_state, offset):
            key_heads = to_heads(
                lax.dynamic_slice_in_dim(key_piece, offset, step_len, 1), head_count
            )
            value_heads = to_heads(
                lax.dynamic_slice_in_dim(value_piece, offset, step_len, 1), head_count
            )
            key_pos = offset + jnp.arange(step_len, dtype=jnp.int32)

            def update(state_in):
                top_old, total_old, sum_old = state_in
                scores = (
                    jnp.einsum(
                        "sqhe,skhe->sqhk",
                        query_heads,
                        key_heads,
                        preferred_element_type=jnp.float32,
                    )
                    * score_scale
                )
                allowed = allowed_mask(positions, key_pos, block_len)
                top_new = jnp.maximum(top_old, jnp.max(jnp.where(allowed, scores, neg_large), -1))
                exp_scores = jnp.where(allowed, jnp.exp(scores - top_new[..., None]), 0.0)
                rescale = jnp.exp(top_old - top_new)
                total_new = total_old * rescale + jnp.sum(exp_scores, -1)
                sum_new = sum_old * rescale[..., None] + jnp.einsum(
                    "sqhk,skhe->sqhe",
                    exp_scores.astype(jnp.bfloat16),
                    value_heads,
                    preferred_element_type=jnp.float32,
                )
                return (top_new, total_new, sum_new)

            return (
                lax.cond(
                    offset // block_len <= last_block, update, lambda state_in: state_in, fold_state
                ),
                None,
            )

        offsets = jnp.arange(key_count // step_len, dtype=jnp.int32) * step_len
        return lax.scan(one_part, carried, offsets)[0]

    return fold_step


def make_query_step(
    query_heads, grad_heads, log_total, delta_rows, positions, block_len, score_scale
):
    last_block = positions[-1] // block_len
    head_count = query_heads.shape[2]

    def fold_step(carried, shard_piece, start_row):
        key_piece, value_piece = shard_piece
        key_count = key_piece.shape[1]
        step_len = math.gcd(key_count, 512)

        def one_part(fold_state, offset):
            key_heads = to_heads(
                lax.dynamic_slice_in_dim(key_piece, offset, step_len, 1), head_count
            )
            value_heads = to_heads(
                lax.dynamic_slice_in_dim(value_piece, offset, step_len, 1), head_count
            )
            key_pos = offset + jnp.arange(step_len, dtype=jnp.int32)

            def update(state_in):
                scores = (
                    jnp.einsum(
                        "sqhe,skhe->sqhk",
                        query_heads,
                        key_heads,
                        preferred_element_type=jnp.float32,
                    )
                    * score_scale
                )
                allowed = allowed_mask(positions, key_pos, block_len)
                probs_all = jnp.where(allowed, jnp.exp(scores - log_total[..., None]), 0.0)
                grad_probs = jnp.einsum(
                    "sqhe,skhe->sqhk", grad_heads, value_heads, preferred_element_type=jnp.float32
                )
                grad_scores = (probs_all * (grad_probs - delta_rows[..., None])).astype(
                    jnp.bfloat16
                )
                return state_in + jnp.einsum(
                    "sqhk,skhe->sqhe", grad_scores, key_heads, preferred_element_type=jnp.float32
                )

            return (
                lax.cond(
                    offset // block_len <= last_block, update, lambda state_in: state_in, fold_state
                ),
                None,
            )

        offsets = jnp.arange(key_count // step_len, dtype=jnp.int32) * step_len
        return lax.scan(one_part, carried, offsets)[0]

    return fold_step


def make_key_step(key_heads, value_heads, positions, block_len, score_scale):
    first_block = positions[0] // block_len
    head_count = key_heads.shape[2]

    def fold_step(carried, shard_piece, start_row):
        query_piece, grad_piece, stats_piece = shard_piece
        seq_count, query_count, model_width = query_piece.shape
        step_len = math.gcd(query_count, 512)

        def one_part(fold_state, offset):
            query_part = to_heads(
                lax.dynamic_slice_in_dim(query_piece, offset, step_len, 1), head_count
            )
            grad_part = to_heads(
                lax.dynamic_slice_in_dim(grad_piece, offset, step_len, 1), head_count
            )
            stats_part = lax.dynamic_slice_in_dim(stats_piece, offset, step_len, 1).astype(
                jnp.float32
            )
            stats_part = stats_part.reshape(seq_count, step_len, 6, head_count)
            log_total = stats_part[:, :, 0] + stats_part[:, :, 1] + stats_part[:, :, 2]
            delta_rows = stats_part[:, :, 3] + stats_part[:, :, 4] + stats_part[:, :, 5]
            query_pos = offset + jnp.arange(step_len, dtype=jnp.int32)

            def update(state_in):
                key_grad, value_grad = state_in
                scores = (
                    jnp.einsum(
                        "sqhe,skhe->sqhk", query_part, key_heads, preferred_element_type=jnp.float32
                    )
                    * score_scale
                )
                allowed = allowed_mask(query_pos, positions, block_len)
                probs_all = jnp.where(allowed, jnp.exp(scores - log_total[..., None]), 0.0)
                grad_probs = jnp.einsum(
                    "sqhe,skhe->sqhk", grad_part, value_heads, preferred_element_type=jnp.float32
                )
                grad_scores = (probs_all * (grad_probs - delta_rows[..., None])).astype(
                    jnp.bfloat16
                )
                value_grad = value_grad + jnp.einsum(
                    "sqhk,sqhe->skhe",
                    probs_all.astype(jnp.bfloat16),
                    grad_part,
                    preferred_element_type=jnp.float32,
                )
                key_grad = key_grad + jnp.einsum(
                    "sqhk,sqhe->skhe", grad_scores, query_part, preferred_element_type=jnp.float32
                )
                return (key_grad, value_grad)

            last_query = (offset + step_len - 1) // block_len
            return (
                lax.cond(last_query >= first_block, update, lambda state_in: state_in, fold_state),
                None,
            )

        offsets = jnp.arange(query_count // step_len, dtype=jnp.int32) * step_len
        return lax.scan(one_part, carried, offsets)[0]

    return fold_step


def per_device(
    tokens,
    tie_index,
    first_gain,
    first_shift,
    qkv_weight,
    qv_bias,
    out_weight,
    out_bias,
    second_gain,
    second_shift,
    fc_weight,
    fc_bias,
    proj_weight,
    proj_bias,
    cotangent,
):
    gathered = (
        lax.all_gather(first_gain, ("dp", "seq"), axis=1, tiled=True),
        lax.all_gather(first_shift, ("dp", "seq"), axis=1, tiled=True),
        lax.all_gather(qkv_weight, ("dp", "seq"), axis=1, tiled=True),
        lax.all_gather(qv_bias, ("dp", "seq"), axis=1, tiled=True),
        lax.all_gather(out_weight, ("dp", "seq"), axis=1, tiled=True),
        lax.all_gather(out_bias, ("dp", "seq"), axis=1, tiled=True),
        lax.all_gather(second_gain, ("dp", "seq"), axis=1, tiled=True),
        lax.all_gather(second_shift, ("dp", "seq"), axis=1, tiled=True),
        lax.all_gather(fc_weight, ("dp", "seq"), axis=1, tiled=True),
        lax.all_gather(fc_bias, ("dp", "seq"), axis=1, tiled=True),
        lax.all_gather(proj_weight, ("dp", "seq"), axis=1, tiled=True),
        lax.all_gather(proj_bias, ("dp", "seq"), axis=1, tiled=True),
    )
    seq_count, tok_count, model_width = tokens.shape
    head_count = HEADS
    block_len = BLOCK
    score_scale = 1.0 / math.sqrt(HEAD_DIM)
    positions = lax.axis_index("seq") * tok_count + jnp.arange(tok_count, dtype=jnp.int32)
    member = 0
    gain_one, shift_one, w_qkv, bias_qv = select_all(gathered[0:4], tie_index[member])
    inputs = tokens[member].astype(jnp.float32)
    normed = norm_apply(inputs, gain_one, shift_one).astype(jnp.bfloat16)
    qkv_rows = jnp.dot(normed, w_qkv, preferred_element_type=jnp.float32)
    normed_list = [normed]
    query_list = [(qkv_rows[:, :model_width] + bias_qv[:model_width]).astype(jnp.bfloat16)]
    key_list = [qkv_rows[:, model_width : 2 * model_width].astype(jnp.bfloat16)]
    value_list = [(qkv_rows[:, 2 * model_width :] + bias_qv[model_width:]).astype(jnp.bfloat16)]
    query_all = jnp.stack(query_list)
    key_all = jnp.stack(key_list)
    value_all = jnp.stack(value_list)
    query_heads = to_heads(query_all, head_count)
    head_dim = query_heads.shape[3]
    stat_shape = (seq_count, tok_count, head_count)
    start_state = (
        jnp.full(stat_shape, neg_large, jnp.float32),
        jnp.zeros(stat_shape, jnp.float32),
        jnp.zeros(stat_shape + (head_dim,), jnp.float32),
    )
    forward_step = make_forward_step(query_heads, positions, block_len, score_scale)
    top_score, total_weight, weighted_sum = forward_step(
        start_state,
        (
            lax.all_gather(key_all, "seq", axis=1, tiled=True),
            lax.all_gather(value_all, "seq", axis=1, tiled=True),
        ),
        jnp.int32(0),
    )
    attn_heads = weighted_sum / total_weight[..., None]
    log_total = top_score + jnp.log(total_weight)
    attended = attn_heads.reshape(seq_count, tok_count, model_width).astype(jnp.bfloat16)
    member = 0
    w_out, bias_out, gain_two, shift_two, w_fc, bias_fc, w_proj, bias_proj = select_all(
        gathered[4:12], tie_index[member]
    )
    inputs = tokens[member].astype(jnp.float32)
    middle = (
        inputs + jnp.dot(attended[member], w_out, preferred_element_type=jnp.float32) + bias_out
    )
    normed_two = norm_apply(middle, gain_two, shift_two).astype(jnp.bfloat16)
    hidden_pre = jnp.dot(normed_two, w_fc, preferred_element_type=jnp.float32) + bias_fc
    hidden = gelu_tanh(hidden_pre).astype(jnp.bfloat16)
    layer_rows = [
        (middle + jnp.dot(hidden, w_proj, preferred_element_type=jnp.float32) + bias_proj).astype(
            jnp.bfloat16
        )
    ]
    saved_mlp = [(middle, normed_two, hidden_pre, hidden)]
    layer_out = jnp.stack(layer_rows)
    whole_back = (
        lax.all_gather(first_gain, ("dp", "seq"), axis=1, tiled=True),
        lax.all_gather(first_shift, ("dp", "seq"), axis=1, tiled=True),
        lax.all_gather(qkv_weight, ("dp", "seq"), axis=1, tiled=True),
        lax.all_gather(qv_bias, ("dp", "seq"), axis=1, tiled=True),
        lax.all_gather(out_weight, ("dp", "seq"), axis=1, tiled=True),
        lax.all_gather(out_bias, ("dp", "seq"), axis=1, tiled=True),
        lax.all_gather(second_gain, ("dp", "seq"), axis=1, tiled=True),
        lax.all_gather(second_shift, ("dp", "seq"), axis=1, tiled=True),
        lax.all_gather(fc_weight, ("dp", "seq"), axis=1, tiled=True),
        lax.all_gather(fc_bias, ("dp", "seq"), axis=1, tiled=True),
        lax.all_gather(proj_weight, ("dp", "seq"), axis=1, tiled=True),
        lax.all_gather(proj_bias, ("dp", "seq"), axis=1, tiled=True),
    )
    grad_totals = [jnp.zeros(stacked.shape, jnp.float32) for stacked in whole_back]
    member = 0
    chosen = tie_index[member]
    w_out, bias_out, gain_two, shift_two, w_fc, bias_fc, w_proj, bias_proj = select_all(
        whole_back[4:12], chosen
    )
    middle, normed_two, hidden_pre, hidden = saved_mlp[member]
    upstream = cotangent[member].astype(jnp.float32)
    upstream_low = upstream.astype(jnp.bfloat16)
    grad_hidden = jnp.einsum("td,fd->tf", upstream_low, w_proj, preferred_element_type=jnp.float32)
    gelu_pull = jax.vjp(gelu_tanh, hidden_pre)[1]
    grad_pre = gelu_pull(grad_hidden)[0].astype(jnp.bfloat16)
    grad_normed = jnp.einsum("tf,df->td", grad_pre, w_fc, preferred_element_type=jnp.float32)
    norm_pull = jax.vjp(
        norm_apply, middle, gain_two.astype(jnp.float32), shift_two.astype(jnp.float32)
    )[1]
    grad_middle, grad_gain, grad_shift = norm_pull(grad_normed)
    grad_middle = grad_middle + upstream
    middle_low = grad_middle.astype(jnp.bfloat16)
    attn_grads = [
        jnp.einsum("te,de->td", middle_low, w_out, preferred_element_type=jnp.float32).astype(
            jnp.bfloat16
        )
    ]
    middle_grads = [grad_middle]
    updates = (
        jnp.einsum("td,te->de", attended[member], middle_low, preferred_element_type=jnp.float32),
        jnp.sum(grad_middle, 0),
        grad_gain,
        grad_shift,
        jnp.einsum("td,tf->df", normed_two, grad_pre, preferred_element_type=jnp.float32),
        jnp.sum(grad_pre.astype(jnp.float32), 0),
        jnp.einsum("tf,td->fd", hidden, upstream_low, preferred_element_type=jnp.float32),
        jnp.sum(upstream, 0),
    )
    for slot_index, update in enumerate(updates):
        grad_totals[4 + slot_index] = add_block(grad_totals[4 + slot_index], update, chosen)
    grad_attn_all = jnp.stack(attn_grads)
    grad_heads = to_heads(grad_attn_all, head_count)
    delta_rows = jnp.sum(grad_heads.astype(jnp.float32) * attn_heads, -1)
    query_step = make_query_step(
        query_heads, grad_heads, log_total, delta_rows, positions, block_len, score_scale
    )
    zero_heads = jnp.zeros(stat_shape + (head_dim,), jnp.float32)
    grad_query = query_step(
        zero_heads,
        (
            lax.all_gather(key_all, "seq", axis=1, tiled=True),
            lax.all_gather(value_all, "seq", axis=1, tiled=True),
        ),
        jnp.int32(0),
    )
    row_stats = jnp.stack(split_three(log_total) + split_three(delta_rows), 2).reshape(
        seq_count, tok_count, 6 * head_count
    )
    key_step = make_key_step(
        to_heads(key_all, head_count),
        to_heads(value_all, head_count),
        positions,
        block_len,
        score_scale,
    )
    grad_key, grad_value = key_step(
        (zero_heads, zero_heads),
        (
            lax.all_gather(query_all, "seq", axis=1, tiled=True),
            lax.all_gather(grad_attn_all, "seq", axis=1, tiled=True),
            lax.all_gather(row_stats, "seq", axis=1, tiled=True),
        ),
        jnp.int32(0),
    )
    flat_shape = (seq_count, tok_count, model_width)
    grad_query = (grad_query * score_scale).reshape(flat_shape).astype(jnp.bfloat16)
    grad_key = (grad_key * score_scale).reshape(flat_shape).astype(jnp.bfloat16)
    grad_value = grad_value.reshape(flat_shape).astype(jnp.bfloat16)
    member = 0
    chosen = tie_index[member]
    gain_one, shift_one, w_qkv, bias_qv = select_all(whole_back[0:4], chosen)
    grad_mixed = jnp.concatenate([grad_query[member], grad_key[member], grad_value[member]], 1)
    grad_normed = jnp.einsum("te,de->td", grad_mixed, w_qkv, preferred_element_type=jnp.float32)
    norm_pull = jax.vjp(
        norm_apply,
        tokens[member].astype(jnp.float32),
        gain_one.astype(jnp.float32),
        shift_one.astype(jnp.float32),
    )[1]
    grad_inputs, grad_gain, grad_shift = norm_pull(grad_normed)
    input_rows = [(grad_inputs + middle_grads[member]).astype(jnp.bfloat16)]
    updates = (
        grad_gain,
        grad_shift,
        jnp.einsum(
            "td,te->de", normed_list[member], grad_mixed, preferred_element_type=jnp.float32
        ),
        jnp.concatenate(
            [
                jnp.sum(grad_query[member].astype(jnp.float32), 0),
                jnp.sum(grad_value[member].astype(jnp.float32), 0),
            ]
        ),
    )
    for slot_index, update in enumerate(updates):
        grad_totals[slot_index] = add_block(grad_totals[slot_index], update, chosen)
    input_grad = jnp.stack(input_rows)
    shard_grads = tuple(
        (
            lax.psum_scatter(grad_totals[0], ("dp", "seq"), scatter_dimension=1, tiled=True),
            lax.psum_scatter(grad_totals[1], ("dp", "seq"), scatter_dimension=1, tiled=True),
            lax.psum_scatter(grad_totals[2], ("dp", "seq"), scatter_dimension=1, tiled=True),
            lax.psum_scatter(grad_totals[3], ("dp", "seq"), scatter_dimension=1, tiled=True),
            lax.psum_scatter(grad_totals[4], ("dp", "seq"), scatter_dimension=1, tiled=True),
            lax.psum_scatter(grad_totals[5], ("dp", "seq"), scatter_dimension=1, tiled=True),
            lax.psum_scatter(grad_totals[6], ("dp", "seq"), scatter_dimension=1, tiled=True),
            lax.psum_scatter(grad_totals[7], ("dp", "seq"), scatter_dimension=1, tiled=True),
            lax.psum_scatter(grad_totals[8], ("dp", "seq"), scatter_dimension=1, tiled=True),
            lax.psum_scatter(grad_totals[9], ("dp", "seq"), scatter_dimension=1, tiled=True),
            lax.psum_scatter(grad_totals[10], ("dp", "seq"), scatter_dimension=1, tiled=True),
            lax.psum_scatter(grad_totals[11], ("dp", "seq"), scatter_dimension=1, tiled=True),
        )
    )
    return (layer_out, input_grad) + shard_grads


bf16 = jnp.bfloat16
f32 = jnp.float32
SMALL = 64
score_scale = 1.0 / math.sqrt(HEAD_DIM)
gelu_root = math.sqrt(2.0 / math.pi)
gelu_cube = 0.044715
SMEM = pl.BlockSpec(memory_space=pltpu.SMEM)
VMEM = pl.BlockSpec(memory_space=pltpu.VMEM)


def dot(a, b, ca=1, cb=0):
    return lax.dot_general(a, b, (((ca,), (cb,)), ((), ())), preferred_element_type=f32)


def norm_parts(values):
    row_mean = jnp.mean(values, -1, keepdims=True)
    centred = values - row_mean
    row_var = jnp.mean(centred * centred, -1, keepdims=True)
    scale = lax.rsqrt(row_var + epsilon)
    return centred * scale, scale


def norm_back(normal, scale, gain, grad):
    scaled = grad * gain
    return scale * (
        scaled
        - jnp.mean(scaled, -1, keepdims=True)
        - normal * jnp.mean(scaled * normal, -1, keepdims=True)
    )


def head_mask(rows, width, head):
    lane = lax.broadcasted_iota(jnp.int32, (rows, width), 1)
    return (lane >= head * HEAD_DIM) & (lane < (head + 1) * HEAD_DIM)


class Held:
    def __init__(self, ref, copy):
        self.ref, self.copy = ref, copy
        self.shape, self.dtype = ref.shape, ref.dtype

    def __getitem__(self, at):
        if self.copy is not None:
            self.copy.wait()
            self.copy = None
        return self.ref[at]


class Made:
    def __init__(self, ref, copy):
        self.ref, self.copy = ref, copy
        self.shape, self.dtype = ref.shape, ref.dtype
        self.flushed = False

    def __getitem__(self, at):
        return self.ref[at]

    def __setitem__(self, at, value):
        self.ref[at] = value

    def flush(self):
        if not self.flushed:
            self.copy.start()
            self.flushed = True


COST = 1.0


def run(kernel, outs, *args, scalars=(), scratch=(), us=1.0, room=60, name=None):
    shapes = [jax.ShapeDtypeStruct(shape, dtype) for shape, dtype in outs]
    far = [k for k in range(len(args)) if k not in scalars]

    def body(*refs):
        ins, refs = list(refs[: len(args)]), refs[len(args) :]
        targets, refs = refs[: len(outs)], refs[len(outs) :]
        own, refs = refs[: len(scratch)], refs[len(scratch) :]
        held, refs = refs[: len(far)], refs[len(far) :]
        made, (in_sems, out_sems) = refs[: len(outs)], refs[len(outs) :]
        for n, k in enumerate(far):
            copy = pltpu.make_async_copy(ins[k], held[n], in_sems.at[n])
            copy.start()
            ins[k] = Held(held[n], copy)
        results = [
            Made(made[n], pltpu.make_async_copy(made[n], targets[n], out_sems.at[n]))
            for n in range(len(outs))
        ]
        kernel(*ins, *results, *own)
        for k in far:
            if ins[k].copy is not None:
                ins[k].copy.wait()
        for result in results:
            result.flush()
        for result in results:
            result.copy.wait()

    hbm = pl.BlockSpec(memory_space=pl.ANY)
    return pl.pallas_call(
        body,
        out_shape=shapes,
        in_specs=[SMEM if k in scalars else hbm for k in range(len(args))],
        out_specs=[hbm] * len(outs),
        scratch_shapes=list(scratch)
        + [pltpu.VMEM(args[k].shape, args[k].dtype) for k in far]
        + [pltpu.VMEM(out.shape, out.dtype) for out in shapes]
        + [
            pltpu.SemaphoreType.DMA((max(len(far), 1),)),
            pltpu.SemaphoreType.DMA((len(outs),)),
        ],
        compiler_params=pltpu.CompilerParams(vmem_limit_bytes=room * 1024 * 1024),
        cost_estimate=pl.CostEstimate(
            flops=int(us * COST * 1e9), bytes_accessed=int(us * COST * 3.5e6), transcendentals=0
        ),
        name=name,
    )(*args)


def by_head(values):
    size, width = values.shape
    blank = jnp.zeros_like(values)
    return jnp.concatenate(
        [
            jnp.where(head_mask(size, width, head), values, blank)
            for head in range(width // HEAD_DIM)
        ],
        0,
    )


def where_am_i(group):
    place = lax.axis_index("seq")
    return lax.axis_index("dp"), place // group, place % group


def ties_of(tie_refs):
    ranks = len(tie_refs)
    rank = lax.axis_index("dp")

    def tie_of(seq):
        step = lax.rem(seq + ranks - rank, ranks)
        tie = tie_refs[0][0]
        for k in range(1, ranks):
            tie = jnp.where(step == k, tie_refs[k][0], tie)
        return tie

    return tie_of


def one_hot(at_ref, rows):
    at = at_ref[...]
    row = lax.broadcasted_iota(jnp.int32, (rows, at.shape[1]), 0)
    return jnp.where(row == at, 1.0, 0.0).astype(bf16)


def flat_rows(value):
    return value.astype(f32).reshape(-1, value.shape[-1]).astype(value.dtype)


def pack_kernel(group, ranks, *refs):
    refs, scr_ref = refs[:-1], refs[-1]
    tie_of, refs = ties_of(refs[:ranks]), refs[ranks:]
    qkv_ref, out_w_ref, vectors, out_ref, cols_ref = refs[0], refs[1], refs[2:10], refs[10], refs[11]
    ties, rows, _ = qkv_ref.shape
    planes = ranks
    model = qkv_ref.shape[2] // 3
    width = model // ranks
    shape = (16, SMALL)
    eye = lax.broadcasted_iota(jnp.int32, shape, 0) == lax.broadcasted_iota(jnp.int32, shape, 1)
    eye = jnp.where(eye, 1.0, 0.0).astype(bf16)
    for tie in range(ties):
        lines = []
        for ref in vectors:
            line = ref[tie : tie + 1].astype(f32)
            for at in range(line.shape[1] // rows):
                lines.append(line[:, at * rows : (at + 1) * rows])
        lines.append(jnp.zeros((16 - len(lines), rows), f32))
        small = dot(jnp.concatenate(lines, 0).astype(bf16), eye, 0, 0).astype(bf16)
        qkv = qkv_ref[tie]
        for to in range(ranks):
            cols = [
                qkv[:, k * model + to * width : k * model + (to + 1) * width] for k in range(3)
            ]
            scr_ref[tie, to] = jnp.concatenate(cols + [small], 1)
    for seq in range(planes):
        tie = tie_of(seq)
        for to in range(ranks):
            out_ref[to * planes + seq] = scr_ref[tie, to]
    out_ref.flush()
    blank = jnp.zeros((cols_ref.shape[1] - rows, model), f32)
    for seq in range(planes):
        cols = jnp.concatenate([out_w_ref[tie_of(seq)].astype(f32), blank], 0)
        cols_ref[seq] = cols.astype(bf16)


def pack_late_kernel(ranks, *refs):
    tie_of = ties_of(refs[:ranks])
    fc_ref, proj_ref, fc_out_ref, proj_out_ref = refs[ranks:]
    planes = proj_out_ref.shape[0]
    part = fc_ref.shape[2] // ranks
    for seq in range(planes):
        fc = fc_ref[tie_of(seq)]
        for to in range(ranks):
            fc_out_ref[to * planes + seq] = fc[:, to * part : (to + 1) * part]
    fc_out_ref.flush()
    for seq in range(planes):
        proj_out_ref[seq] = proj_ref[tie_of(seq)]


def project_kernel(group, x_ref, *refs):
    w_refs, refs = refs[:group], refs[group:]
    sel_ref, bsel_ref, mask_ref, q_ref, kv_ref, h_ref, vec_ref, fcb_ref, w_ref = refs
    ranks, size, width = q_ref.shape
    part = fcb_ref.shape[1]
    model = x_ref.shape[1]
    sel = one_hot(sel_ref, model)
    bsel = one_hot(bsel_ref, model)
    normal, _ = norm_parts(x_ref[...].astype(f32))
    rows = w_ref.shape[0] // group
    for slot, ref in enumerate(w_refs):
        w_ref[slot * rows : (slot + 1) * rows] = flat_rows(ref[...])
    w_ref.flush()
    small = w_ref[:, 3 * width :]
    spread = dot(small, sel, 0, 0)[:16]
    normed = (normal * spread[0:1] + spread[1:2]).astype(bf16)
    normed = dot(normed, sel, 1, 1).astype(bf16)
    mixed = dot(normed, w_ref[:, : 3 * width])
    biases = jnp.sum(dot(small, bsel, 0, 0)[:16] * mask_ref[...], 0, keepdims=True)
    bias = biases[:, part:]
    kv_ref[0] = mixed[:, width : 2 * width].astype(bf16).reshape(ranks, size, width)
    value = (mixed[:, 2 * width :] + bias[:, width:]).astype(bf16)
    kv_ref[1] = value.reshape(ranks, size, width)
    kv_ref.flush()
    query = (mixed[:, :width] + bias[:, :width]).astype(bf16) * jnp.asarray(score_scale, bf16)
    q_ref[...] = query.reshape(ranks, size, width)
    h_ref[...] = normed
    vec_ref[...] = spread[:8]
    fcb_ref[...] = jnp.broadcast_to(biases[:, :part], fcb_ref.shape)


def attend_kernel(group, rows, q_ref, *refs):
    kv_refs, refs = refs[:group], refs[group:]
    cols_refs, refs = refs[:group], refs[group:]
    a_ref, lse_ref, w_ref, sums_refs, (whole_ref, sums_ref) = *refs[:3], refs[3:-2], refs[-2:]
    rank, _, member = where_am_i(group)
    chunks, size, width = q_ref.shape
    for chunk in range(chunks):
        count = (chunk + 1) * size
        keys = jnp.concatenate([r[0, : chunk + 1].reshape(count, width) for r in kv_refs], 0)
        values = jnp.concatenate([r[1, : chunk + 1].reshape(count, width) for r in kv_refs], 0)
        values_t = values.T
        scores = dot(keys, by_head(q_ref[chunk]), 1, 1)
        top = jnp.max(scores, 0, keepdims=True)
        raised = jnp.exp(scores - top)
        total = jnp.sum(raised, 0, keepdims=True)
        lse_ref[chunk : chunk + 1] = top + jnp.log(total)
        mixed = dot(values_t, raised.astype(bf16)) / total
        parts = [
            mixed[head * HEAD_DIM : (head + 1) * HEAD_DIM, head * size : (head + 1) * size]
            for head in range(width // HEAD_DIM)
        ]
        a_ref[chunk * size : (chunk + 1) * size] = jnp.concatenate(parts, 0).T.astype(bf16)
    a_ref.flush()
    lse_ref.flush()
    for plane in range(cols_refs[0].shape[0]):
        pieces = [ref[plane].astype(f32)[:rows] for ref in cols_refs]
        for owner in range(group):
            piece = pieces[0]
            for slot in range(1, group):
                here = lax.rem(member + slot, group) == owner
                piece = jnp.where(here, pieces[slot], piece)
            at = (plane * group + owner) * rows
            whole_ref[at : at + rows] = piece
    w_ref[...] = whole_ref[...].astype(bf16)
    sums_ref[...] = dot(a_ref[...], w_ref[...]).astype(bf16).reshape(sums_ref.shape)
    for k, ref in enumerate(sums_refs):
        ref[...] = sums_ref[lax.rem(rank + k, chunks)]
        ref.flush()


def join_kernel(ranks, *refs):
    parts, (x_ref, vec_ref, sel_ref, r_ref, h_ref) = refs[:ranks], refs[ranks:]
    total = x_ref[...].astype(f32) + vec_ref[2:3]
    for ref in parts:
        total = total + ref[...].astype(f32)
    r_ref[...] = total
    r_ref.flush()
    normal, _ = norm_parts(total)
    normed = (normal * vec_ref[3:4] + vec_ref[4:5]).astype(bf16)
    h_ref[...] = dot(normed, one_hot(sel_ref, normed.shape[1]), 1, 1).astype(bf16)


def mlp_kernel(group, ranks, h_ref, *refs):
    f_refs, refs = refs[:group], refs[group:]
    fcb_ref, refs = refs[0], refs[1:]
    g_refs, refs = refs[:ranks], refs[ranks:]
    p_refs, refs = refs[:group], refs[group:]
    sel_ref, refs = refs[0], refs[1:]
    dh_refs, refs = refs[:ranks], refs[ranks:]
    y_ref, g_ref, hid_ref, pre_ref, wf_ref, wp_ref, dh_ref = refs
    size = y_ref.shape[1]
    planes, _, model = p_refs[0].shape
    hid_rows = wp_ref.shape[0] // (planes * group)
    rank, _, member = where_am_i(group)
    rows = wf_ref.shape[0] // group
    for slot, ref in enumerate(f_refs):
        wf_ref[slot * rows : (slot + 1) * rows] = flat_rows(ref[...])
    value = dot(h_ref[...], wf_ref[...]) + fcb_ref[0:1]
    for slot, ref in enumerate(p_refs):
        for plane in range(planes):
            at = plane * group + lax.rem(member + slot, group)
            start = pl.multiple_of(at * hid_rows, 16)
            wp_ref[pl.ds(start, hid_rows)] = ref[plane, :hid_rows]
    for k, ref in enumerate(g_refs):
        start = pl.multiple_of(lax.rem(rank + k, ranks) * size, size)
        g_ref[pl.ds(start, size)] = ref[...]
    g_ref.flush()
    grad = dot(g_ref[...], wp_ref[...], 1, 1)
    squared = value * value
    bent = jnp.tanh(gelu_root * value * (1.0 + gelu_cube * squared))
    half = 0.5 * (1.0 + bent)
    slope = half + (0.5 * gelu_root) * value * (1.0 - bent * bent) * (
        1.0 + 3.0 * gelu_cube * squared
    )
    pre_ref[...] = (grad * slope).astype(bf16)
    pre_ref.flush()
    below = dot(pre_ref[...], wf_ref[...], 1, 1).astype(bf16)
    dh_ref[...] = dot(below, one_hot(sel_ref, model)).astype(bf16).reshape(ranks, size, model)
    for k, ref in enumerate(dh_refs):
        ref[...] = dh_ref[lax.rem(rank + k, ranks)]
        ref.flush()
    hid_ref[...] = (value * half).astype(bf16)
    hid_ref.flush()
    y_ref[...] = dot(hid_ref[...], wp_ref[...]).astype(bf16).reshape(ranks, size, model)


def mlp_grad_kernel(group, planes, h_ref, pre_ref, hid_ref, g_ref, *refs):
    out_refs, fcb_ref, scr_ref = refs[:group], refs[group], refs[group + 1]
    half = scr_ref.shape[0] // group
    whole = dot(h_ref[...], pre_ref[...], 0, 0)
    for slot, ref in enumerate(out_refs):
        ref[:half] = whole[slot * half : (slot + 1) * half].astype(ref.dtype)
    scr_ref[...] = dot(hid_ref[...], g_ref[...], 0, 0)
    member = where_am_i(group)[2]
    hid_rows = half // planes
    for slot in range(group - 1, -1, -1):
        ref = out_refs[slot]
        for plane in range(planes):
            at = plane * group + lax.rem(member + slot, group)
            start = pl.multiple_of(at * hid_rows, 16)
            to = half + plane * hid_rows
            ref[to : to + hid_rows] = scr_ref[pl.ds(start, hid_rows)].astype(ref.dtype)
        ref.flush()
    fcb_ref[...] = jnp.broadcast_to(
        jnp.sum(pre_ref[...].astype(f32), 0, keepdims=True), fcb_ref.shape
    )


def add_late_kernel(group, *refs):
    parts, (fc_ref, proj_ref) = refs[:group], refs[group:]
    total = parts[0][...]
    for ref in parts[1:]:
        total = total + ref[...].astype(f32)
    half = total.shape[0] // 2
    proj_ref[...] = total[half:].reshape(proj_ref.shape).astype(bf16)
    proj_ref.flush()
    fc_ref[...] = total[:half].reshape(fc_ref.shape).astype(bf16)


def join_back_kernel(ranks, *refs):
    parts, (r_ref, g_ref, vec_ref, dr_ref, low_ref, sums_ref) = refs[:ranks], refs[ranks:]
    normal, scale = norm_parts(r_ref[...])
    upstream = g_ref[...].astype(f32)
    grad = parts[0][...].astype(f32)
    for ref in parts[1:]:
        grad = grad + ref[...].astype(f32)
    total = upstream + norm_back(normal, scale, vec_ref[3:4], grad)
    low_ref[...] = total.astype(bf16)
    low_ref.flush()
    dr_ref[...] = total
    dr_ref.flush()
    sums_ref[...] = jnp.concatenate(
        [
            jnp.sum(total, 0, keepdims=True),
            jnp.sum(grad * normal, 0, keepdims=True),
            jnp.sum(grad, 0, keepdims=True),
            jnp.sum(upstream, 0, keepdims=True),
        ]
        + [jnp.zeros((4, total.shape[1]), f32)],
        0,
    )


def layer_kernel(parts_ref, r_ref, vec_ref, out_ref):
    total = r_ref[...] + vec_ref[5:6]
    for rank in range(parts_ref.shape[0]):
        total = total + parts_ref[rank].astype(f32)
    out_ref[...] = total.astype(bf16)


def attend_back_kernel(group, low_ref, wo_ref, q_ref, *refs):
    kv_refs, refs = refs[:group], refs[group:]
    lse_ref, a_ref, refs = refs[0], refs[1], refs[2:]
    dkv_refs, dq_ref, dwo_refs, (scr_ref, wo_scr) = (
        refs[:group],
        refs[group],
        refs[group + 1 : -2],
        refs[-2:],
    )
    chunks, size, width = q_ref.shape
    heads = width // HEAD_DIM
    grad_all_rows = dot(low_ref[...], wo_ref[...], 1, 1).astype(bf16)
    for chunk in range(chunks - 1, -1, -1):
        count = (chunk + 1) * size
        keys = jnp.concatenate([r[0, : chunk + 1].reshape(count, width) for r in kv_refs], 0)
        values = jnp.concatenate([r[1, : chunk + 1].reshape(count, width) for r in kv_refs], 0)
        keys_t = keys.T
        query = by_head(q_ref[chunk])
        grad = by_head(grad_all_rows[chunk * size : (chunk + 1) * size])
        probs = jnp.exp(dot(keys, query, 1, 1) - lse_ref[chunk : chunk + 1])
        grad_probs = dot(values, grad, 1, 1)
        delta = jnp.sum(probs * grad_probs, 0, keepdims=True)
        grad_scores = (probs * (grad_probs - delta)).astype(bf16)
        turned = dot(keys_t, grad_scores)
        parts = [
            turned[head * HEAD_DIM : (head + 1) * HEAD_DIM, head * size : (head + 1) * size]
            for head in range(heads)
        ]
        dq_ref[chunk * size : (chunk + 1) * size] = (
            jnp.concatenate(parts, 0).T * score_scale
        ).astype(bf16)
        both = (dot(grad_scores, query), dot(probs.astype(bf16), grad))
        for slot in range(group):
            for k in range(2):
                value = both[k][slot * count : (slot + 1) * count].reshape(chunk + 1, size, width)
                if chunk == chunks - 1:
                    scr_ref[slot, k] = value
                else:
                    scr_ref[slot, k, : chunk + 1] = scr_ref[slot, k, : chunk + 1] + value
    for slot in range(group - 1, -1, -1):
        dkv_refs[slot][...] = scr_ref[slot].astype(dkv_refs[slot].dtype)
        dkv_refs[slot].flush()
    dq_ref.flush()
    wo_scr[...] = dot(a_ref[...], low_ref[...], 0, 0).reshape(wo_scr.shape)
    for slot in range(group - 1, -1, -1):
        owner = lax.rem(where_am_i(group)[2] + slot, group)
        for plane in range(wo_scr.shape[0]):
            dwo_refs[slot][plane] = wo_scr[plane, owner].astype(dwo_refs[slot].dtype)


def first_kernel(group, ranks, dq_ref, *refs):
    dkv_refs, refs = refs[:group], refs[group:]
    w_ref, sel_ref, refs = refs[0], refs[1], refs[2:]
    dwo_refs, refs = refs[:group], refs[group:]
    proj_ref, refs = refs[0], refs[1:]
    dh_refs, (dh_ref, mix_ref, late_ref) = refs[:ranks], refs[ranks:]
    tokens, width = dq_ref.shape
    model = sel_ref.shape[1]
    size = tokens // ranks
    low = [dq_ref[...]]
    for k in range(2):
        total = dkv_refs[0][k]
        for ref in dkv_refs[1:]:
            total = total + ref[k].astype(f32)
        low.append(total.reshape(tokens, width).astype(bf16))
    mixed = jnp.concatenate(low, 1)
    mix_ref[...] = mixed
    mix_ref.flush()
    below = dot(mixed, w_ref[:, : 3 * width], 1, 1).astype(bf16)
    dh_ref[...] = dot(below, one_hot(sel_ref, model)).astype(bf16).reshape(ranks, size, model)
    for k, ref in enumerate(dh_refs):
        ref[...] = dh_ref[lax.rem(where_am_i(group)[0] + k, ranks)]
        ref.flush()
    dh_ref.flush()
    total = dwo_refs[0][...]
    for ref in dwo_refs[1:]:
        total = total + ref[...].astype(f32)
    hid_rows = proj_ref.shape[1]
    rest = late_ref.shape[1] - hid_rows - total.shape[1]
    for plane in range(total.shape[0]):
        late_ref[plane, :hid_rows] = proj_ref[plane]
        late_ref[plane, hid_rows:] = jnp.concatenate(
            [total[plane], jnp.zeros((rest, model), f32)], 0
        ).astype(bf16)


def first_grad_kernel(
    group, h_ref, mix_ref, x_ref, dh_ref, sums_ref, fcb_ref, mask_ref, sel_ref, bsel_ref, *refs
):
    ranks, size, model = dh_ref.shape
    width = mix_ref.shape[1] // 3
    part = fcb_ref.shape[1]
    mixed = mix_ref[...]
    whole = dot(h_ref[...], mixed, 0, 0)
    normal, _ = norm_parts(x_ref[...].astype(f32))
    grad = dh_ref[...].reshape(ranks * size, model).astype(f32)
    vec = jnp.concatenate(
        [
            jnp.sum(grad * normal, 0, keepdims=True),
            jnp.sum(grad, 0, keepdims=True),
            sums_ref[0:4],
            jnp.zeros((2, model), f32),
        ],
        0,
    )
    cols = jnp.sum(mixed.astype(f32), 0, keepdims=True)
    both = jnp.concatenate([cols[:, :width], cols[:, 2 * width :]], 1)
    sums = jnp.concatenate([fcb_ref[0:1], both], 1) * mask_ref[...]
    small = dot(one_hot(sel_ref, model), vec.astype(bf16), 1, 1)
    more = dot(one_hot(bsel_ref, model), sums.astype(bf16), 1, 1)
    rest = jnp.zeros((model, SMALL - 24), f32)
    whole = jnp.concatenate([whole, small, more, rest], 1)
    rows = model // group
    for slot in range(group - 1, -1, -1):
        refs[slot][...] = whole[slot * rows : (slot + 1) * rows].astype(refs[slot].dtype)
        refs[slot].flush()


def add_early_kernel(group, *refs):
    parts, out_ref = refs[:group], refs[group]
    total = parts[0][...]
    for ref in parts[1:]:
        total = total + ref[...].astype(f32)
    out_ref[...] = total.reshape(out_ref.shape).astype(bf16)


def last_kernel(ranks, *refs):
    parts, (x_ref, vec_ref, dr_ref, out_ref) = refs[:ranks], refs[ranks:]
    normal, scale = norm_parts(x_ref[...].astype(f32))
    grad = parts[0][...].astype(f32)
    for ref in parts[1:]:
        grad = grad + ref[...].astype(f32)
    out_ref[...] = (dr_ref[...] + norm_back(normal, scale, vec_ref[0:1], grad)).astype(bf16)


def by_block(ties, parts, tie_of):
    totals = [jnp.zeros(parts[0].shape, f32) for _ in range(ties)]
    for seq, part in enumerate(parts):
        value = part.astype(f32)
        for block in range(ties):
            totals[block] = totals[block] + jnp.where(tie_of(seq) == block, value, 0.0)
    return totals


def final_late_kernel(ranks, *refs):
    tie_of = ties_of(refs[:ranks])
    fc_in, rest_in, fc_ref, proj_ref, out_ref = refs[ranks:]
    ties, _, inner = fc_ref.shape
    planes = rest_in.shape[0]
    hid_rows, rows = proj_ref.shape[1], out_ref.shape[1]
    part = inner // ranks
    for block, total in enumerate(by_block(ties, [rest_in[k] for k in range(planes)], tie_of)):
        proj_ref[block] = total[:hid_rows]
        out_ref[block] = total[hid_rows : hid_rows + rows]
    proj_ref.flush()
    for rank in range(ranks):
        parts = [fc_in[rank * planes + k] for k in range(planes)]
        for block, total in enumerate(by_block(ties, parts, tie_of)):
            fc_ref[block, :, rank * part : (rank + 1) * part] = total


def final_kernel(ranks, *refs):
    tie_of = ties_of(refs[:ranks])
    home_ref, qkv_ref, *small_refs = refs[ranks:]
    ties, rows, wide = qkv_ref.shape
    model = wide // 3
    planes = home_ref.shape[0] // ranks
    width = model // ranks
    sums = []
    for rank in range(ranks):
        parts = [home_ref[rank * planes + k] for k in range(planes)]
        sums.append(by_block(ties, parts, tie_of))
    eye = lax.broadcasted_iota(jnp.int32, (SMALL, SMALL), 0)
    eye = jnp.where(eye == lax.broadcasted_iota(jnp.int32, (SMALL, SMALL), 1), 1.0, 0.0)
    eye = eye.astype(bf16)
    for block in range(ties):
        values = [sums[rank][block] for rank in range(ranks)]
        qkv_ref[block] = jnp.concatenate(
            [value[:, k * width : (k + 1) * width] for k in range(3) for value in values], 1
        )
        small = values[0][:, 3 * width :]
        for value in values[1:]:
            small = small + value[:, 3 * width :]
        high = small.astype(bf16)
        low = (small - high.astype(f32)).astype(bf16)
        turned = dot(eye, high, 1, 1) + dot(eye, low, 1, 1)
        for k in range(6):
            small_refs[k][block : block + 1] = turned[k : k + 1]
        small_refs[6][block : block + 1] = jnp.concatenate(
            [turned[k : k + 1] for k in range(14, 16)], 1
        )
        small_refs[7][block : block + 1] = jnp.concatenate(
            [turned[k : k + 1] for k in range(16, 20)], 1
        )


def fast_device(
    n_dp,
    n_seq,
    tokens,
    tie_index,
    first_gain,
    first_shift,
    qkv_weight,
    qv_bias,
    out_weight,
    out_bias,
    second_gain,
    second_shift,
    fc_weight,
    fc_bias,
    proj_weight,
    proj_bias,
    cotangent,
):
    ranks, planes, group = n_dp, n_dp, n_seq // n_dp
    axes = ("dp", "seq")
    size, model = tokens.shape[1:]
    ties, rows = qkv_weight.shape[:2]
    hid_rows = proj_weight.shape[1]
    inner = fc_weight.shape[2]
    width = model // ranks
    part = inner // ranks
    count = ranks * size
    lanes = 3 * width + SMALL
    heads_here = width // HEAD_DIM
    squads = ranks * planes
    rank = lax.axis_index("dp")
    place = lax.axis_index("seq")
    plane, member = place // group, place % group

    def route(where):
        pairs = []
        for a in range(ranks):
            for b in range(planes):
                for c in range(group):
                    x, y, z = where(a, b, c)
                    pairs.append((a * n_seq + b * group + c, x * n_seq + y * group + z))
        return pairs

    swap = route(lambda a, b, c: (b, a, c))
    to_rank = [route(lambda a, b, c, k=k: ((a + k) % ranks, b, c)) for k in range(ranks)]
    to_plane = [route(lambda a, b, c, k=k: (a, (b + k) % planes, c)) for k in range(planes)]
    to_member = [route(lambda a, b, c, k=k: (a, b, (c + k) % group)) for k in range(group)]
    same_member = [[b * group + c for b in range(planes)] for c in range(group)]
    squad = [
        [a * n_seq + b * group + c for a in range(ranks) for b in range(planes)]
        for c in range(group)
    ]

    def send(values, pairs):
        return lax.ppermute(values, axes, pairs)

    def from_members(piece):
        return [piece] + [send(piece, to_member[group - k]) for k in range(1, group)]

    def over_members(parts):
        return [parts[0]] + [send(parts[k], to_member[k]) for k in range(1, group)]

    def over_planes(pieces):
        return lax.all_to_all(pieces, "seq", 0, 0, axis_index_groups=same_member)

    def over_squad(pieces):
        return lax.all_to_all(pieces, axes, 0, 0, axis_index_groups=squad)

    def scatter(parts):
        return [parts[0]] + [send(parts[k], to_rank[k]) for k in range(1, ranks)]

    def gate(value, *before):
        return lax.optimization_barrier((value, before))[0]

    ties_seen = [tie_index] + [send(tie_index, to_rank[ranks - k]) for k in range(1, ranks)]
    scalar_ties = tuple(range(ranks))
    tokens_own = send(tokens[0], swap)

    cols_rows = (rows + 15) // 16 * 16
    early, cols = run(
        functools.partial(pack_kernel, group, ranks),
        [((squads, rows, lanes), bf16), ((planes, cols_rows, model), bf16)],
        *ties_seen,
        qkv_weight,
        out_weight,
        first_gain,
        first_shift,
        out_bias,
        second_gain,
        second_shift,
        proj_bias,
        qv_bias,
        fc_bias,
        scalars=scalar_ties,
        scratch=[pltpu.VMEM((ties, ranks, rows, lanes), bf16)],
        us=0.1,
        name="pack",
    )
    packed = early
    early = over_squad(early)

    def arrival(owner, row):
        a, b, c = owner // n_seq, (owner % n_seq) // group, owner % group
        slot = (c + group - member) % group
        return (slot * squads + a * planes + b) * rows + row

    flat = jnp.arange(model)
    at_model = arrival(flat // rows, flat % rows)
    unit = jnp.arange(part) + rank * part
    at_fc = arrival(unit // (4 * rows), unit % rows)
    flat_qv = jnp.arange(2 * width)
    unit_qv = (flat_qv // width) * model + rank * width + flat_qv % width
    at_qv = arrival(unit_qv // (2 * rows), unit_qv % rows)
    at_bias = jnp.concatenate([at_fc, at_qv])
    lanes_of = jnp.concatenate(
        [
            (jnp.arange(part) % (4 * rows)) // rows + 8,
            (unit_qv % (2 * rows)) // rows + 6,
        ]
    )
    sel = at_model[None].astype(jnp.int32)
    bsel = at_bias[None].astype(jnp.int32)
    row_mask = (jnp.arange(16)[:, None] == lanes_of[None, :]).astype(f32)

    tokens_all = lax.all_gather(tokens_own, "dp", axis=0, tiled=True)
    early = gate(early, tokens_all, sel, bsel, row_mask)
    cols = over_planes(gate(cols, early))
    late_rows = hid_rows + cols_rows
    early = from_members(early)
    own = ((size, model), bf16)
    q, kv, h_one, vec, fcb, w_early = run(
        functools.partial(project_kernel, group),
        [
            ((ranks, size, width), bf16),
            ((2, ranks, size, width), bf16),
            ((count, model), bf16),
            ((8, model), f32),
            ((8, part), f32),
            ((model, lanes), bf16),
        ],
        tokens_all,
        *early,
        sel,
        bsel,
        row_mask,
        room=20,
        us=5.0,
        name="project",
    )
    grad_own = send(gate(cotangent[0], tokens_all), swap)
    late_fc, late_proj = run(
        functools.partial(pack_late_kernel, ranks),
        [((squads, rows, part), bf16), ((planes, hid_rows, model), bf16)],
        *ties_seen,
        gate(fc_weight, q),
        proj_weight,
        scalars=scalar_ties,
        us=2.0,
        name="pack_late",
    )
    cols = from_members(gate(cols, q, late_fc))
    late_fc = over_squad(gate(late_fc, grad_own, cols))
    kv = from_members(gate(kv, grad_own))
    grads_seen = [grad_own] + [send(grad_own, to_rank[ranks - k]) for k in range(1, ranks)]
    attended, lse, w_out, *sums = run(
        functools.partial(attend_kernel, group, rows),
        [((count, width), bf16), ((8, heads_here * size), f32), ((width, model), bf16)] + [own] * ranks,
        q,
        *kv,
        *cols,
        scratch=[pltpu.VMEM((width, model), f32), pltpu.VMEM((ranks, size, model), bf16)],
        us=6.0,
        name="attend",
    )
    sums = scatter(sums)
    late_fc = gate(late_fc, attended, grads_seen)
    late_proj = over_planes(gate(late_proj, late_fc))
    late_fc = from_members(late_fc)
    middle, h_own = run(
        functools.partial(join_kernel, ranks),
        [((size, model), f32), own],
        *sums,
        tokens_own,
        gate(vec, grads_seen),
        sel,
        room=16,
        us=2.0,
        name="join",
    )
    late_proj = from_members(gate(late_proj, h_own))
    h_two = lax.all_gather(h_own, "dp", axis=0, tiled=True)
    rest = run(
        functools.partial(mlp_kernel, group, ranks),
        [own] * ranks
        + [((ranks, size, model), bf16), ((count, model), bf16)]
        + [((count, part), bf16)] * 2,
        h_two,
        *late_fc,
        fcb,
        *grads_seen,
        *late_proj,
        sel,
        scratch=[
            pltpu.VMEM((model, part), bf16),
            pltpu.VMEM((part, model), bf16),
            pltpu.VMEM((ranks, size, model), bf16),
        ],
        us=7.0,
        name="mlp",
    )
    below, (layer_parts, grad_all, hidden, grad_pre) = rest[:ranks], rest[ranks:]
    below = scatter(below)
    half = 2 * (model // group)
    *late, fc_sums = run(
        functools.partial(mlp_grad_kernel, group, planes),
        [((half, model), f32)]
        + [((half, model), bf16)] * (group - 1)
        + [((8, part), f32)],
        h_two,
        grad_pre,
        hidden,
        grad_all,
        scratch=[pltpu.VMEM((part, model), f32)],
        us=4.0,
        name="mlp_grad",
    )
    late = over_members(late)
    grad_middle, low_own, own_sums = run(
        functools.partial(join_back_kernel, ranks),
        [((size, model), f32), own, ((8, model), f32)],
        *below,
        middle,
        grad_own,
        vec,
        room=16,
        us=30.0,
        name="join_back",
    )
    late = gate(late, low_own)
    late_fc, late_proj = run(
        functools.partial(add_late_kernel, group),
        [((squads, rows, part), bf16), ((planes, hid_rows, model), bf16)],
        *late,
        room=16,
        us=2.0,
        name="add_late",
    )
    low = lax.all_gather(gate(low_own, late_fc), "dp", axis=0, tiled=True)
    late_fc = over_squad(late_fc)
    layer_parts = lax.all_to_all(gate(layer_parts, low, late_fc), "dp", 0, 0)
    (layer_own,) = run(
        layer_kernel,
        [own],
        layer_parts,
        middle,
        vec,
        room=16,
        us=1.0,
        name="layer",
    )
    layer_out = send(layer_own, swap)
    rest = run(
        functools.partial(attend_back_kernel, group),
        [((2, ranks, size, width), f32)]
        + [((2, ranks, size, width), bf16)] * (group - 1)
        + [((count, width), bf16)]
        + [((planes, rows, model), f32)]
        + [((planes, rows, model), bf16)] * (group - 1),
        low,
        w_out,
        q,
        *kv,
        lse,
        attended,
        scratch=[
            pltpu.VMEM((group, 2, ranks, size, width), f32),
            pltpu.VMEM((planes, group, rows, model), f32),
        ],
        us=0.5,
        name="attend_back",
    )
    dkv, dq, dw_out = rest[:group], rest[group], rest[group + 1 :]
    dkv = over_members(dkv)
    dw_out = over_members(dw_out)
    rest = run(
        functools.partial(first_kernel, group, ranks),
        [own] * ranks
        + [
            ((ranks, size, model), bf16),
            ((count, 3 * width), bf16),
            ((planes, late_rows, model), bf16),
        ],
        dq,
        *dkv,
        gate(w_early, layer_own),
        sel,
        *dw_out,
        late_proj,
        us=4.0,
        name="first",
    )
    first_parts, (first_all, mixed, late_rest) = rest[:ranks], rest[ranks:]
    grad_first = scatter(first_parts)
    late_rest = over_planes(gate(late_rest, layer_parts))
    early = run(
        functools.partial(first_grad_kernel, group),
        [((model // group, lanes), f32)]
        + [((model // group, lanes), bf16)] * (group - 1),
        h_one,
        mixed,
        tokens_all,
        first_all,
        own_sums,
        fc_sums,
        row_mask,
        sel,
        bsel,
        us=5.0,
        name="first_grad",
    )
    early = over_members(early)
    (input_own,) = run(
        functools.partial(last_kernel, ranks),
        [own],
        *grad_first,
        tokens_own,
        vec,
        grad_middle,
        room=16,
        us=30.0,
        name="last",
    )
    early = gate(early, input_own, layer_out)
    (early,) = run(
        functools.partial(add_early_kernel, group),
        [((squads, rows, lanes), bf16)],
        *early,
        room=16,
        us=1.0,
        name="add_early",
    )
    input_grad = send(input_own, swap)
    early = over_squad(early)
    grad_fc_weight, grad_proj_weight, grad_out_weight = run(
        functools.partial(final_late_kernel, ranks),
        [((ties, rows, inner), f32), ((ties, hid_rows, model), f32), ((ties, rows, model), f32)],
        *ties_seen,
        late_fc,
        gate(late_rest, input_own),
        scalars=scalar_ties,
        us=60.0,
        name="final_late",
    )
    early = gate(early, grad_fc_weight)
    grad_qkv_weight, *small = run(
        functools.partial(final_kernel, ranks),
        [((ties, rows, 3 * model), f32)]
        + [((ties, rows), f32)] * 6
        + [((ties, 2 * rows), f32), ((ties, 4 * rows), f32)],
        *ties_seen,
        early,
        scalars=scalar_ties,
        room=16,
        us=1.0,
        name="final",
    )
    layer_out, input_grad = gate((layer_out, input_grad), grad_qkv_weight)
    return (
        layer_out[None],
        input_grad[None],
        small[0],
        small[1],
        grad_qkv_weight,
        small[6],
        grad_out_weight,
        small[2],
        small[3],
        small[4],
        grad_fc_weight,
        small[7],
        grad_proj_weight,
        small[5],
    )


def pick_device(n_dp, n_seq, *args):
    tokens, qkv_weight, proj_weight = args[0], args[4], args[12]
    size, rows, hid_rows = tokens.shape[1], qkv_weight.shape[1], proj_weight.shape[1]
    group = n_seq // n_dp
    whole_tiles = rows % 8 == 0 and (group * rows) % 16 == 0 and hid_rows % 16 == 0
    one_block = tokens.shape[0] == 1 and group == 2 and size * group == BLOCK
    if whole_tiles and one_block:
        return fast_device(n_dp, n_seq, *args)
    return per_device(*args)


def solution(mesh):
    in_specs = (
        P("dp", "seq", None),
        P("dp"),
        P(None, ("dp", "seq")),
        P(None, ("dp", "seq")),
        P(None, ("dp", "seq"), None),
        P(None, ("dp", "seq")),
        P(None, ("dp", "seq"), None),
        P(None, ("dp", "seq")),
        P(None, ("dp", "seq")),
        P(None, ("dp", "seq")),
        P(None, ("dp", "seq"), None),
        P(None, ("dp", "seq")),
        P(None, ("dp", "seq"), None),
        P(None, ("dp", "seq")),
        P("dp", "seq", None),
    )
    out_specs = (
        P("dp", "seq", None),
        P("dp", "seq", None),
        P(None, ("dp", "seq")),
        P(None, ("dp", "seq")),
        P(None, ("dp", "seq"), None),
        P(None, ("dp", "seq")),
        P(None, ("dp", "seq"), None),
        P(None, ("dp", "seq")),
        P(None, ("dp", "seq")),
        P(None, ("dp", "seq")),
        P(None, ("dp", "seq"), None),
        P(None, ("dp", "seq")),
        P(None, ("dp", "seq"), None),
        P(None, ("dp", "seq")),
    )
    return jax.shard_map(
        functools.partial(pick_device, mesh.shape["dp"], mesh.shape["seq"]),
        mesh=mesh,
        in_specs=in_specs,
        out_specs=out_specs,
        check_vma=False,
    )
```

```python
import functools
import math

import jax
import jax.numpy as jnp
from jax import lax
from jax.experimental import pallas as pl
from jax.experimental.pallas import tpu as pltpu
from jax.sharding import PartitionSpec as P

HEADS = 12
HEAD_DIM = 64
BLOCK = 256


epsilon = 1e-05
neg_large = -1e30


def norm_apply(values, norm_gain, norm_shift):
    row_mean = jnp.mean(values, -1, keepdims=True)
    centred = values - row_mean
    row_var = jnp.mean(centred * centred, -1, keepdims=True)
    return centred * lax.rsqrt(row_var + epsilon) * norm_gain + norm_shift


def gelu_tanh(values):
    return jax.nn.gelu(values, approximate=True)


def select_all(gathered, chosen):
    return tuple(
        (lax.dynamic_index_in_dim(stacked, chosen, 0, keepdims=False) for stacked in gathered)
    )


def add_block(totals, update, chosen):
    current = lax.dynamic_index_in_dim(totals, chosen, 0, keepdims=True)
    return lax.dynamic_update_index_in_dim(totals, current + update[None], chosen, 0)


def split_three(values):
    upper_part = values.astype(jnp.bfloat16)
    rest_one = values - lax.optimization_barrier(upper_part).astype(jnp.float32)
    middle_part = rest_one.astype(jnp.bfloat16)
    lower_part = (rest_one - lax.optimization_barrier(middle_part).astype(jnp.float32)).astype(
        jnp.bfloat16
    )
    return (upper_part, middle_part, lower_part)


def to_heads(flat_rows, head_count):
    return flat_rows.reshape(
        flat_rows.shape[0], flat_rows.shape[1], head_count, flat_rows.shape[2] // head_count
    )


def allowed_mask(query_pos, key_pos, block_len):
    return (key_pos[None, :] // block_len <= query_pos[:, None] // block_len)[None, :, None, :]


def make_forward_step(query_heads, positions, block_len, score_scale):
    last_block = positions[-1] // block_len
    head_count = query_heads.shape[2]

    def fold_step(carried, shard_piece, start_row):
        key_piece, value_piece = shard_piece
        key_count = key_piece.shape[1]
        step_len = math.gcd(key_count, 512)

        def one_part(fold_state, offset):
            key_heads = to_heads(
                lax.dynamic_slice_in_dim(key_piece, offset, step_len, 1), head_count
            )
            value_heads = to_heads(
                lax.dynamic_slice_in_dim(value_piece, offset, step_len, 1), head_count
            )
            key_pos = offset + jnp.arange(step_len, dtype=jnp.int32)

            def update(state_in):
                top_old, total_old, sum_old = state_in
                scores = (
                    jnp.einsum(
                        "sqhe,skhe->sqhk",
                        query_heads,
                        key_heads,
                        preferred_element_type=jnp.float32,
                    )
                    * score_scale
                )
                allowed = allowed_mask(positions, key_pos, block_len)
                top_new = jnp.maximum(top_old, jnp.max(jnp.where(allowed, scores, neg_large), -1))
                exp_scores = jnp.where(allowed, jnp.exp(scores - top_new[..., None]), 0.0)
                rescale = jnp.exp(top_old - top_new)
                total_new = total_old * rescale + jnp.sum(exp_scores, -1)
                sum_new = sum_old * rescale[..., None] + jnp.einsum(
                    "sqhk,skhe->sqhe",
                    exp_scores.astype(jnp.bfloat16),
                    value_heads,
                    preferred_element_type=jnp.float32,
                )
                return (top_new, total_new, sum_new)

            return (
                lax.cond(
                    offset // block_len <= last_block, update, lambda state_in: state_in, fold_state
                ),
                None,
            )

        offsets = jnp.arange(key_count // step_len, dtype=jnp.int32) * step_len
        return lax.scan(one_part, carried, offsets)[0]

    return fold_step


def make_query_step(
    query_heads, grad_heads, log_total, delta_rows, positions, block_len, score_scale
):
    last_block = positions[-1] // block_len
    head_count = query_heads.shape[2]

    def fold_step(carried, shard_piece, start_row):
        key_piece, value_piece = shard_piece
        key_count = key_piece.shape[1]
        step_len = math.gcd(key_count, 512)

        def one_part(fold_state, offset):
            key_heads = to_heads(
                lax.dynamic_slice_in_dim(key_piece, offset, step_len, 1), head_count
            )
            value_heads = to_heads(
                lax.dynamic_slice_in_dim(value_piece, offset, step_len, 1), head_count
            )
            key_pos = offset + jnp.arange(step_len, dtype=jnp.int32)

            def update(state_in):
                scores = (
                    jnp.einsum(
                        "sqhe,skhe->sqhk",
                        query_heads,
                        key_heads,
                        preferred_element_type=jnp.float32,
                    )
                    * score_scale
                )
                allowed = allowed_mask(positions, key_pos, block_len)
                probs_all = jnp.where(allowed, jnp.exp(scores - log_total[..., None]), 0.0)
                grad_probs = jnp.einsum(
                    "sqhe,skhe->sqhk", grad_heads, value_heads, preferred_element_type=jnp.float32
                )
                grad_scores = (probs_all * (grad_probs - delta_rows[..., None])).astype(
                    jnp.bfloat16
                )
                return state_in + jnp.einsum(
                    "sqhk,skhe->sqhe", grad_scores, key_heads, preferred_element_type=jnp.float32
                )

            return (
                lax.cond(
                    offset // block_len <= last_block, update, lambda state_in: state_in, fold_state
                ),
                None,
            )

        offsets = jnp.arange(key_count // step_len, dtype=jnp.int32) * step_len
        return lax.scan(one_part, carried, offsets)[0]

    return fold_step


def make_key_step(key_heads, value_heads, positions, block_len, score_scale):
    first_block = positions[0] // block_len
    head_count = key_heads.shape[2]

    def fold_step(carried, shard_piece, start_row):
        query_piece, grad_piece, stats_piece = shard_piece
        seq_count, query_count, model_width = query_piece.shape
        step_len = math.gcd(query_count, 512)

        def one_part(fold_state, offset):
            query_part = to_heads(
                lax.dynamic_slice_in_dim(query_piece, offset, step_len, 1), head_count
            )
            grad_part = to_heads(
                lax.dynamic_slice_in_dim(grad_piece, offset, step_len, 1), head_count
            )
            stats_part = lax.dynamic_slice_in_dim(stats_piece, offset, step_len, 1).astype(
                jnp.float32
            )
            stats_part = stats_part.reshape(seq_count, step_len, 6, head_count)
            log_total = stats_part[:, :, 0] + stats_part[:, :, 1] + stats_part[:, :, 2]
            delta_rows = stats_part[:, :, 3] + stats_part[:, :, 4] + stats_part[:, :, 5]
            query_pos = offset + jnp.arange(step_len, dtype=jnp.int32)

            def update(state_in):
                key_grad, value_grad = state_in
                scores = (
                    jnp.einsum(
                        "sqhe,skhe->sqhk", query_part, key_heads, preferred_element_type=jnp.float32
                    )
                    * score_scale
                )
                allowed = allowed_mask(query_pos, positions, block_len)
                probs_all = jnp.where(allowed, jnp.exp(scores - log_total[..., None]), 0.0)
                grad_probs = jnp.einsum(
                    "sqhe,skhe->sqhk", grad_part, value_heads, preferred_element_type=jnp.float32
                )
                grad_scores = (probs_all * (grad_probs - delta_rows[..., None])).astype(
                    jnp.bfloat16
                )
                value_grad = value_grad + jnp.einsum(
                    "sqhk,sqhe->skhe",
                    probs_all.astype(jnp.bfloat16),
                    grad_part,
                    preferred_element_type=jnp.float32,
                )
                key_grad = key_grad + jnp.einsum(
                    "sqhk,sqhe->skhe", grad_scores, query_part, preferred_element_type=jnp.float32
                )
                return (key_grad, value_grad)

            last_query = (offset + step_len - 1) // block_len
            return (
                lax.cond(last_query >= first_block, update, lambda state_in: state_in, fold_state),
                None,
            )

        offsets = jnp.arange(query_count // step_len, dtype=jnp.int32) * step_len
        return lax.scan(one_part, carried, offsets)[0]

    return fold_step


def per_device(
    tokens,
    tie_index,
    first_gain,
    first_shift,
    qkv_weight,
    qv_bias,
    out_weight,
    out_bias,
    second_gain,
    second_shift,
    fc_weight,
    fc_bias,
    proj_weight,
    proj_bias,
    cotangent,
):
    gathered = (
        lax.all_gather(first_gain, ("dp", "seq"), axis=1, tiled=True),
        lax.all_gather(first_shift, ("dp", "seq"), axis=1, tiled=True),
        lax.all_gather(qkv_weight, ("dp", "seq"), axis=1, tiled=True),
        lax.all_gather(qv_bias, ("dp", "seq"), axis=1, tiled=True),
        lax.all_gather(out_weight, ("dp", "seq"), axis=1, tiled=True),
        lax.all_gather(out_bias, ("dp", "seq"), axis=1, tiled=True),
        lax.all_gather(second_gain, ("dp", "seq"), axis=1, tiled=True),
        lax.all_gather(second_shift, ("dp", "seq"), axis=1, tiled=True),
        lax.all_gather(fc_weight, ("dp", "seq"), axis=1, tiled=True),
        lax.all_gather(fc_bias, ("dp", "seq"), axis=1, tiled=True),
        lax.all_gather(proj_weight, ("dp", "seq"), axis=1, tiled=True),
        lax.all_gather(proj_bias, ("dp", "seq"), axis=1, tiled=True),
    )
    seq_count, tok_count, model_width = tokens.shape
    head_count = HEADS
    block_len = BLOCK
    score_scale = 1.0 / math.sqrt(HEAD_DIM)
    positions = lax.axis_index("seq") * tok_count + jnp.arange(tok_count, dtype=jnp.int32)
    member = 0
    gain_one, shift_one, w_qkv, bias_qv = select_all(gathered[0:4], tie_index[member])
    inputs = tokens[member].astype(jnp.float32)
    normed = norm_apply(inputs, gain_one, shift_one).astype(jnp.bfloat16)
    qkv_rows = jnp.dot(normed, w_qkv, preferred_element_type=jnp.float32)
    normed_list = [normed]
    query_list = [(qkv_rows[:, :model_width] + bias_qv[:model_width]).astype(jnp.bfloat16)]
    key_list = [qkv_rows[:, model_width : 2 * model_width].astype(jnp.bfloat16)]
    value_list = [(qkv_rows[:, 2 * model_width :] + bias_qv[model_width:]).astype(jnp.bfloat16)]
    query_all = jnp.stack(query_list)
    key_all = jnp.stack(key_list)
    value_all = jnp.stack(value_list)
    query_heads = to_heads(query_all, head_count)
    head_dim = query_heads.shape[3]
    stat_shape = (seq_count, tok_count, head_count)
    start_state = (
        jnp.full(stat_shape, neg_large, jnp.float32),
        jnp.zeros(stat_shape, jnp.float32),
        jnp.zeros(stat_shape + (head_dim,), jnp.float32),
    )
    forward_step = make_forward_step(query_heads, positions, block_len, score_scale)
    top_score, total_weight, weighted_sum = forward_step(
        start_state,
        (
            lax.all_gather(key_all, "seq", axis=1, tiled=True),
            lax.all_gather(value_all, "seq", axis=1, tiled=True),
        ),
        jnp.int32(0),
    )
    attn_heads = weighted_sum / total_weight[..., None]
    log_total = top_score + jnp.log(total_weight)
    attended = attn_heads.reshape(seq_count, tok_count, model_width).astype(jnp.bfloat16)
    member = 0
    w_out, bias_out, gain_two, shift_two, w_fc, bias_fc, w_proj, bias_proj = select_all(
        gathered[4:12], tie_index[member]
    )
    inputs = tokens[member].astype(jnp.float32)
    middle = (
        inputs + jnp.dot(attended[member], w_out, preferred_element_type=jnp.float32) + bias_out
    )
    normed_two = norm_apply(middle, gain_two, shift_two).astype(jnp.bfloat16)
    hidden_pre = jnp.dot(normed_two, w_fc, preferred_element_type=jnp.float32) + bias_fc
    hidden = gelu_tanh(hidden_pre).astype(jnp.bfloat16)
    layer_rows = [
        (middle + jnp.dot(hidden, w_proj, preferred_element_type=jnp.float32) + bias_proj).astype(
            jnp.bfloat16
        )
    ]
    saved_mlp = [(middle, normed_two, hidden_pre, hidden)]
    layer_out = jnp.stack(layer_rows)
    whole_back = (
        lax.all_gather(first_gain, ("dp", "seq"), axis=1, tiled=True),
        lax.all_gather(first_shift, ("dp", "seq"), axis=1, tiled=True),
        lax.all_gather(qkv_weight, ("dp", "seq"), axis=1, tiled=True),
        lax.all_gather(qv_bias, ("dp", "seq"), axis=1, tiled=True),
        lax.all_gather(out_weight, ("dp", "seq"), axis=1, tiled=True),
        lax.all_gather(out_bias, ("dp", "seq"), axis=1, tiled=True),
        lax.all_gather(second_gain, ("dp", "seq"), axis=1, tiled=True),
        lax.all_gather(second_shift, ("dp", "seq"), axis=1, tiled=True),
        lax.all_gather(fc_weight, ("dp", "seq"), axis=1, tiled=True),
        lax.all_gather(fc_bias, ("dp", "seq"), axis=1, tiled=True),
        lax.all_gather(proj_weight, ("dp", "seq"), axis=1, tiled=True),
        lax.all_gather(proj_bias, ("dp", "seq"), axis=1, tiled=True),
    )
    grad_totals = [jnp.zeros(stacked.shape, jnp.float32) for stacked in whole_back]
    member = 0
    chosen = tie_index[member]
    w_out, bias_out, gain_two, shift_two, w_fc, bias_fc, w_proj, bias_proj = select_all(
        whole_back[4:12], chosen
    )
    middle, normed_two, hidden_pre, hidden = saved_mlp[member]
    upstream = cotangent[member].astype(jnp.float32)
    upstream_low = upstream.astype(jnp.bfloat16)
    grad_hidden = jnp.einsum("td,fd->tf", upstream_low, w_proj, preferred_element_type=jnp.float32)
    gelu_pull = jax.vjp(gelu_tanh, hidden_pre)[1]
    grad_pre = gelu_pull(grad_hidden)[0].astype(jnp.bfloat16)
    grad_normed = jnp.einsum("tf,df->td", grad_pre, w_fc, preferred_element_type=jnp.float32)
    norm_pull = jax.vjp(
        norm_apply, middle, gain_two.astype(jnp.float32), shift_two.astype(jnp.float32)
    )[1]
    grad_middle, grad_gain, grad_shift = norm_pull(grad_normed)
    grad_middle = grad_middle + upstream
    middle_low = grad_middle.astype(jnp.bfloat16)
    attn_grads = [
        jnp.einsum("te,de->td", middle_low, w_out, preferred_element_type=jnp.float32).astype(
            jnp.bfloat16
        )
    ]
    middle_grads = [grad_middle]
    updates = (
        jnp.einsum("td,te->de", attended[member], middle_low, preferred_element_type=jnp.float32),
        jnp.sum(grad_middle, 0),
        grad_gain,
        grad_shift,
        jnp.einsum("td,tf->df", normed_two, grad_pre, preferred_element_type=jnp.float32),
        jnp.sum(grad_pre.astype(jnp.float32), 0),
        jnp.einsum("tf,td->fd", hidden, upstream_low, preferred_element_type=jnp.float32),
        jnp.sum(upstream, 0),
    )
    for slot_index, update in enumerate(updates):
        grad_totals[4 + slot_index] = add_block(grad_totals[4 + slot_index], update, chosen)
    grad_attn_all = jnp.stack(attn_grads)
    grad_heads = to_heads(grad_attn_all, head_count)
    delta_rows = jnp.sum(grad_heads.astype(jnp.float32) * attn_heads, -1)
    query_step = make_query_step(
        query_heads, grad_heads, log_total, delta_rows, positions, block_len, score_scale
    )
    zero_heads = jnp.zeros(stat_shape + (head_dim,), jnp.float32)
    grad_query = query_step(
        zero_heads,
        (
            lax.all_gather(key_all, "seq", axis=1, tiled=True),
            lax.all_gather(value_all, "seq", axis=1, tiled=True),
        ),
        jnp.int32(0),
    )
    row_stats = jnp.stack(split_three(log_total) + split_three(delta_rows), 2).reshape(
        seq_count, tok_count, 6 * head_count
    )
    key_step = make_key_step(
        to_heads(key_all, head_count),
        to_heads(value_all, head_count),
        positions,
        block_len,
        score_scale,
    )
    grad_key, grad_value = key_step(
        (zero_heads, zero_heads),
        (
            lax.all_gather(query_all, "seq", axis=1, tiled=True),
            lax.all_gather(grad_attn_all, "seq", axis=1, tiled=True),
            lax.all_gather(row_stats, "seq", axis=1, tiled=True),
        ),
        jnp.int32(0),
    )
    flat_shape = (seq_count, tok_count, model_width)
    grad_query = (grad_query * score_scale).reshape(flat_shape).astype(jnp.bfloat16)
    grad_key = (grad_key * score_scale).reshape(flat_shape).astype(jnp.bfloat16)
    grad_value = grad_value.reshape(flat_shape).astype(jnp.bfloat16)
    member = 0
    chosen = tie_index[member]
    gain_one, shift_one, w_qkv, bias_qv = select_all(whole_back[0:4], chosen)
    grad_mixed = jnp.concatenate([grad_query[member], grad_key[member], grad_value[member]], 1)
    grad_normed = jnp.einsum("te,de->td", grad_mixed, w_qkv, preferred_element_type=jnp.float32)
    norm_pull = jax.vjp(
        norm_apply,
        tokens[member].astype(jnp.float32),
        gain_one.astype(jnp.float32),
        shift_one.astype(jnp.float32),
    )[1]
    grad_inputs, grad_gain, grad_shift = norm_pull(grad_normed)
    input_rows = [(grad_inputs + middle_grads[member]).astype(jnp.bfloat16)]
    updates = (
        grad_gain,
        grad_shift,
        jnp.einsum(
            "td,te->de", normed_list[member], grad_mixed, preferred_element_type=jnp.float32
        ),
        jnp.concatenate(
            [
                jnp.sum(grad_query[member].astype(jnp.float32), 0),
                jnp.sum(grad_value[member].astype(jnp.float32), 0),
            ]
        ),
    )
    for slot_index, update in enumerate(updates):
        grad_totals[slot_index] = add_block(grad_totals[slot_index], update, chosen)
    input_grad = jnp.stack(input_rows)
    shard_grads = tuple(
        (
            lax.psum_scatter(grad_totals[0], ("dp", "seq"), scatter_dimension=1, tiled=True),
            lax.psum_scatter(grad_totals[1], ("dp", "seq"), scatter_dimension=1, tiled=True),
            lax.psum_scatter(grad_totals[2], ("dp", "seq"), scatter_dimension=1, tiled=True),
            lax.psum_scatter(grad_totals[3], ("dp", "seq"), scatter_dimension=1, tiled=True),
            lax.psum_scatter(grad_totals[4], ("dp", "seq"), scatter_dimension=1, tiled=True),
            lax.psum_scatter(grad_totals[5], ("dp", "seq"), scatter_dimension=1, tiled=True),
            lax.psum_scatter(grad_totals[6], ("dp", "seq"), scatter_dimension=1, tiled=True),
            lax.psum_scatter(grad_totals[7], ("dp", "seq"), scatter_dimension=1, tiled=True),
            lax.psum_scatter(grad_totals[8], ("dp", "seq"), scatter_dimension=1, tiled=True),
            lax.psum_scatter(grad_totals[9], ("dp", "seq"), scatter_dimension=1, tiled=True),
            lax.psum_scatter(grad_totals[10], ("dp", "seq"), scatter_dimension=1, tiled=True),
            lax.psum_scatter(grad_totals[11], ("dp", "seq"), scatter_dimension=1, tiled=True),
        )
    )
    return (layer_out, input_grad) + shard_grads


bf16 = jnp.bfloat16
f32 = jnp.float32
SMALL = 64
score_scale = 1.0 / math.sqrt(HEAD_DIM)
gelu_root = math.sqrt(2.0 / math.pi)
gelu_cube = 0.044715
SMEM = pl.BlockSpec(memory_space=pltpu.SMEM)
VMEM = pl.BlockSpec(memory_space=pltpu.VMEM)


def dot(a, b, ca=1, cb=0):
    return lax.dot_general(a, b, (((ca,), (cb,)), ((), ())), preferred_element_type=f32)


def norm_parts(values):
    row_mean = jnp.mean(values, -1, keepdims=True)
    centred = values - row_mean
    row_var = jnp.mean(centred * centred, -1, keepdims=True)
    scale = lax.rsqrt(row_var + epsilon)
    return centred * scale, scale


def norm_back(normal, scale, gain, grad):
    scaled = grad * gain
    return scale * (
        scaled
        - jnp.mean(scaled, -1, keepdims=True)
        - normal * jnp.mean(scaled * normal, -1, keepdims=True)
    )


def head_mask(rows, width, head):
    lane = lax.broadcasted_iota(jnp.int32, (rows, width), 1)
    return (lane >= head * HEAD_DIM) & (lane < (head + 1) * HEAD_DIM)


class Held:
    def __init__(self, ref, copy):
        self.ref, self.copy = ref, copy
        self.shape, self.dtype = ref.shape, ref.dtype

    def __getitem__(self, at):
        if self.copy is not None:
            self.copy.wait()
            self.copy = None
        return self.ref[at]


class Made:
    def __init__(self, ref, copy):
        self.ref, self.copy = ref, copy
        self.shape, self.dtype = ref.shape, ref.dtype
        self.flushed = False

    def __getitem__(self, at):
        return self.ref[at]

    def __setitem__(self, at, value):
        self.ref[at] = value

    def flush(self):
        if not self.flushed:
            self.copy.start()
            self.flushed = True


COST = 1.0


def run(kernel, outs, *args, scalars=(), scalar_out=False, scratch=(), us=1.0, room=60, name=None):
    shapes = [jax.ShapeDtypeStruct(shape, dtype) for shape, dtype in outs]
    far = [k for k in range(len(args)) if k not in scalars]
    made_count = len(outs) - scalar_out

    def body(*refs):
        ins, refs = list(refs[: len(args)]), refs[len(args) :]
        targets, refs = refs[: len(outs)], refs[len(outs) :]
        own, refs = refs[: len(scratch)], refs[len(scratch) :]
        held, refs = refs[: len(far)], refs[len(far) :]
        made, (in_sems, out_sems) = refs[:made_count], refs[made_count:]
        for n, k in enumerate(far):
            copy = pltpu.make_async_copy(ins[k], held[n], in_sems.at[n])
            copy.start()
            ins[k] = Held(held[n], copy)
        results = [
            Made(made[n], pltpu.make_async_copy(made[n], targets[n], out_sems.at[n]))
            for n in range(made_count)
        ]
        kernel(*ins, *results, *targets[made_count:], *own)
        for k in far:
            if ins[k].copy is not None:
                ins[k].copy.wait()
        for result in results:
            result.flush()
        for result in results:
            result.copy.wait()

    hbm = pl.BlockSpec(memory_space=pl.ANY)
    return pl.pallas_call(
        body,
        out_shape=shapes,
        in_specs=[SMEM if k in scalars else hbm for k in range(len(args))],
        out_specs=[hbm] * made_count + [SMEM] * (len(outs) - made_count),
        scratch_shapes=list(scratch)
        + [pltpu.VMEM(args[k].shape, args[k].dtype) for k in far]
        + [pltpu.VMEM(out.shape, out.dtype) for out in shapes[:made_count]]
        + [
            pltpu.SemaphoreType.DMA((max(len(far), 1),)),
            pltpu.SemaphoreType.DMA((made_count,)),
        ],
        compiler_params=pltpu.CompilerParams(vmem_limit_bytes=room * 1024 * 1024),
        cost_estimate=pl.CostEstimate(
            flops=int(us * COST * 1e9), bytes_accessed=int(us * COST * 3.5e6), transcendentals=0
        ),
        name=name,
    )(*args)


def by_head(values):
    size, width = values.shape
    blank = jnp.zeros_like(values)
    return jnp.concatenate(
        [
            jnp.where(head_mask(size, width, head), values, blank)
            for head in range(width // HEAD_DIM)
        ],
        0,
    )


def where_am_i(group):
    place = lax.axis_index("seq")
    return lax.axis_index("dp"), place // group, place % group


def ties_of(tie_refs):
    ranks = len(tie_refs)
    rank = lax.axis_index("dp")

    def tie_of(seq):
        step = lax.rem(seq + ranks - rank, ranks)
        tie = tie_refs[0][0]
        for k in range(1, ranks):
            tie = jnp.where(step == k, tie_refs[k][0], tie)
        return tie

    return tie_of


def one_hot(at_ref, rows):
    at = at_ref[...]
    row = lax.broadcasted_iota(jnp.int32, (rows, at.shape[1]), 0)
    return jnp.where(row == at, 1.0, 0.0).astype(bf16)


def flat_rows(value):
    return value.astype(f32).reshape(-1, value.shape[-1]).astype(value.dtype)


def pack_kernel(group, ranks, *refs):
    refs, scr_ref = refs[:-1], refs[-1]
    tie_of, refs = ties_of(refs[:ranks]), refs[ranks:]
    qkv_ref, out_w_ref, vectors, out_ref, cols_ref = refs[0], refs[1], refs[2:10], refs[10], refs[11]
    ties_ref = refs[12]
    ties, rows, _ = qkv_ref.shape
    planes = ranks
    model = qkv_ref.shape[2] // 3
    width = model // ranks
    shape = (16, SMALL)
    eye = lax.broadcasted_iota(jnp.int32, shape, 0) == lax.broadcasted_iota(jnp.int32, shape, 1)
    eye = jnp.where(eye, 1.0, 0.0).astype(bf16)
    for tie in range(ties):
        lines = []
        for ref in vectors:
            line = ref[tie : tie + 1].astype(f32)
            for at in range(line.shape[1] // rows):
                lines.append(line[:, at * rows : (at + 1) * rows])
        lines.append(jnp.zeros((16 - len(lines), rows), f32))
        small = dot(jnp.concatenate(lines, 0).astype(bf16), eye, 0, 0).astype(bf16)
        qkv = qkv_ref[tie]
        for to in range(ranks):
            cols = [
                qkv[:, k * model + to * width : k * model + (to + 1) * width] for k in range(3)
            ]
            scr_ref[tie, to] = jnp.concatenate(cols + [small], 1)
    for seq in range(planes):
        tie = tie_of(seq)
        ties_ref[seq] = tie
        for to in range(ranks):
            out_ref[to * planes + seq] = scr_ref[tie, to]
    out_ref.flush()
    blank = jnp.zeros((cols_ref.shape[1] - rows, model), f32)
    for seq in range(planes):
        cols = jnp.concatenate([out_w_ref[tie_of(seq)].astype(f32), blank], 0)
        cols_ref[seq] = cols.astype(bf16)


def pack_late_kernel(ranks, *refs):
    tie_of = lambda seq: refs[0][seq]
    fc_ref, proj_ref, fc_out_ref, proj_out_ref = refs[1:]
    planes = proj_out_ref.shape[0]
    part = fc_ref.shape[2] // ranks
    for seq in range(planes):
        fc = fc_ref[tie_of(seq)]
        for to in range(ranks):
            fc_out_ref[to * planes + seq] = fc[:, to * part : (to + 1) * part]
    fc_out_ref.flush()
    for seq in range(planes):
        proj_out_ref[seq] = proj_ref[tie_of(seq)]


def project_kernel(group, x_ref, *refs):
    w_refs, refs = refs[:group], refs[group:]
    sel_ref, bsel_ref, mask_ref, q_ref, kv_ref, h_ref, vec_ref, fcb_ref, w_ref = refs
    ranks, size, width = q_ref.shape
    part = fcb_ref.shape[1]
    model = x_ref.shape[1]
    sel = one_hot(sel_ref, model)
    bsel = one_hot(bsel_ref, model)
    normal, _ = norm_parts(x_ref[...].astype(f32))
    rows = w_ref.shape[0] // group
    for slot, ref in enumerate(w_refs):
        w_ref[slot * rows : (slot + 1) * rows] = flat_rows(ref[...])
    w_ref.flush()
    small = w_ref[:, 3 * width :]
    spread = dot(small, sel, 0, 0)[:16]
    normed = (normal * spread[0:1] + spread[1:2]).astype(bf16)
    normed = dot(normed, sel, 1, 1).astype(bf16)
    mixed = dot(normed, w_ref[:, : 3 * width])
    biases = jnp.sum(dot(small, bsel, 0, 0)[:16] * mask_ref[...], 0, keepdims=True)
    bias = biases[:, part:]
    kv_ref[0] = mixed[:, width : 2 * width].astype(bf16).reshape(ranks, size, width)
    value = (mixed[:, 2 * width :] + bias[:, width:]).astype(bf16)
    kv_ref[1] = value.reshape(ranks, size, width)
    kv_ref.flush()
    query = (mixed[:, :width] + bias[:, :width]).astype(bf16) * jnp.asarray(score_scale, bf16)
    q_ref[...] = query.reshape(ranks, size, width)
    h_ref[...] = normed
    vec_ref[...] = spread[:8]
    fcb_ref[...] = jnp.broadcast_to(biases[:, :part], fcb_ref.shape)


def attend_kernel(group, rows, q_ref, *refs):
    kv_refs, refs = refs[:group], refs[group:]
    cols_refs, refs = refs[:group], refs[group:]
    a_ref, lse_ref, w_ref, sums_refs, (whole_ref, sums_ref) = *refs[:3], refs[3:-2], refs[-2:]
    rank, _, member = where_am_i(group)
    chunks, size, width = q_ref.shape
    for chunk in range(chunks):
        count = (chunk + 1) * size
        keys = jnp.concatenate([r[0, : chunk + 1].reshape(count, width) for r in kv_refs], 0)
        values = jnp.concatenate([r[1, : chunk + 1].reshape(count, width) for r in kv_refs], 0)
        values_t = values.T
        scores = dot(keys, by_head(q_ref[chunk]), 1, 1)
        top = jnp.max(scores, 0, keepdims=True)
        raised = jnp.exp(scores - top)
        total = jnp.sum(raised, 0, keepdims=True)
        lse_ref[chunk : chunk + 1] = top + jnp.log(total)
        mixed = dot(values_t, raised.astype(bf16)) / total
        parts = [
            mixed[head * HEAD_DIM : (head + 1) * HEAD_DIM, head * size : (head + 1) * size]
            for head in range(width // HEAD_DIM)
        ]
        a_ref[chunk * size : (chunk + 1) * size] = jnp.concatenate(parts, 0).T.astype(bf16)
    a_ref.flush()
    lse_ref.flush()
    for plane in range(cols_refs[0].shape[0]):
        pieces = [ref[plane].astype(f32)[:rows] for ref in cols_refs]
        for owner in range(group):
            piece = pieces[0]
            for slot in range(1, group):
                here = lax.rem(member + slot, group) == owner
                piece = jnp.where(here, pieces[slot], piece)
            at = (plane * group + owner) * rows
            whole_ref[at : at + rows] = piece
    w_ref[...] = whole_ref[...].astype(bf16)
    sums_ref[...] = dot(a_ref[...], w_ref[...]).astype(bf16).reshape(sums_ref.shape)
    for k, ref in enumerate(sums_refs):
        ref[...] = sums_ref[lax.rem(rank + k, chunks)]
        ref.flush()


def join_kernel(ranks, *refs):
    parts, (x_ref, vec_ref, sel_ref, r_ref, h_ref) = refs[:ranks], refs[ranks:]
    total = x_ref[...].astype(f32) + vec_ref[2:3]
    for ref in parts:
        total = total + ref[...].astype(f32)
    r_ref[...] = total
    r_ref.flush()
    normal, _ = norm_parts(total)
    normed = (normal * vec_ref[3:4] + vec_ref[4:5]).astype(bf16)
    h_ref[...] = dot(normed, one_hot(sel_ref, normed.shape[1]), 1, 1).astype(bf16)


def mlp_kernel(group, ranks, h_ref, *refs):
    f_refs, refs = refs[:group], refs[group:]
    fcb_ref, refs = refs[0], refs[1:]
    g_refs, refs = refs[:ranks], refs[ranks:]
    p_refs, refs = refs[:group], refs[group:]
    sel_ref, refs = refs[0], refs[1:]
    dh_refs, refs = refs[:ranks], refs[ranks:]
    y_ref, g_ref, hid_ref, pre_ref, wf_ref, wp_ref, dh_ref = refs
    size = y_ref.shape[1]
    planes, _, model = p_refs[0].shape
    hid_rows = wp_ref.shape[0] // (planes * group)
    rank, _, member = where_am_i(group)
    rows = wf_ref.shape[0] // group
    for slot, ref in enumerate(f_refs):
        wf_ref[slot * rows : (slot + 1) * rows] = flat_rows(ref[...])
    value = dot(h_ref[...], wf_ref[...]) + fcb_ref[0:1]
    for slot, ref in enumerate(p_refs):
        for plane in range(planes):
            at = plane * group + lax.rem(member + slot, group)
            start = pl.multiple_of(at * hid_rows, 16)
            wp_ref[pl.ds(start, hid_rows)] = ref[plane, :hid_rows]
    for k, ref in enumerate(g_refs):
        start = pl.multiple_of(lax.rem(rank + k, ranks) * size, size)
        g_ref[pl.ds(start, size)] = ref[...]
    g_ref.flush()
    grad = dot(g_ref[...], wp_ref[...], 1, 1)
    squared = value * value
    bent = jnp.tanh(gelu_root * value * (1.0 + gelu_cube * squared))
    half = 0.5 * (1.0 + bent)
    slope = half + (0.5 * gelu_root) * value * (1.0 - bent * bent) * (
        1.0 + 3.0 * gelu_cube * squared
    )
    pre_ref[...] = (grad * slope).astype(bf16)
    pre_ref.flush()
    below = dot(pre_ref[...], wf_ref[...], 1, 1).astype(bf16)
    dh_ref[...] = dot(below, one_hot(sel_ref, model)).astype(bf16).reshape(ranks, size, model)
    for k, ref in enumerate(dh_refs):
        ref[...] = dh_ref[lax.rem(rank + k, ranks)]
        ref.flush()
    hid_ref[...] = (value * half).astype(bf16)
    hid_ref.flush()
    y_ref[...] = dot(hid_ref[...], wp_ref[...]).astype(bf16).reshape(ranks, size, model)


def mlp_grad_kernel(group, planes, h_ref, pre_ref, hid_ref, g_ref, *refs):
    out_refs, fcb_ref, scr_ref = refs[:group], refs[group], refs[group + 1]
    half = scr_ref.shape[0] // group
    whole = dot(h_ref[...], pre_ref[...], 0, 0)
    for slot, ref in enumerate(out_refs):
        ref[:half] = whole[slot * half : (slot + 1) * half].astype(ref.dtype)
    scr_ref[...] = dot(hid_ref[...], g_ref[...], 0, 0)
    member = where_am_i(group)[2]
    hid_rows = half // planes
    for slot in range(group - 1, -1, -1):
        ref = out_refs[slot]
        for plane in range(planes):
            at = plane * group + lax.rem(member + slot, group)
            start = pl.multiple_of(at * hid_rows, 16)
            to = half + plane * hid_rows
            ref[to : to + hid_rows] = scr_ref[pl.ds(start, hid_rows)].astype(ref.dtype)
        ref.flush()
    fcb_ref[...] = jnp.broadcast_to(
        jnp.sum(pre_ref[...].astype(f32), 0, keepdims=True), fcb_ref.shape
    )


def add_late_kernel(group, *refs):
    parts, (fc_ref, proj_ref) = refs[:group], refs[group:]
    total = parts[0][...]
    for ref in parts[1:]:
        total = total + ref[...].astype(f32)
    half = total.shape[0] // 2
    proj_ref[...] = total[half:].reshape(proj_ref.shape).astype(bf16)
    proj_ref.flush()
    fc_ref[...] = total[:half].reshape(fc_ref.shape).astype(bf16)


def join_back_kernel(ranks, *refs):
    parts, (r_ref, g_ref, vec_ref, dr_ref, low_ref, sums_ref) = refs[:ranks], refs[ranks:]
    normal, scale = norm_parts(r_ref[...])
    upstream = g_ref[...].astype(f32)
    grad = parts[0][...].astype(f32)
    for ref in parts[1:]:
        grad = grad + ref[...].astype(f32)
    total = upstream + norm_back(normal, scale, vec_ref[3:4], grad)
    low_ref[...] = total.astype(bf16)
    low_ref.flush()
    dr_ref[...] = total
    dr_ref.flush()
    sums_ref[...] = jnp.concatenate(
        [
            jnp.sum(total, 0, keepdims=True),
            jnp.sum(grad * normal, 0, keepdims=True),
            jnp.sum(grad, 0, keepdims=True),
            jnp.sum(upstream, 0, keepdims=True),
        ]
        + [jnp.zeros((4, total.shape[1]), f32)],
        0,
    )


def layer_kernel(parts_ref, r_ref, vec_ref, out_ref):
    total = r_ref[...] + vec_ref[5:6]
    for rank in range(parts_ref.shape[0]):
        total = total + parts_ref[rank].astype(f32)
    out_ref[...] = total.astype(bf16)


def attend_back_kernel(group, low_ref, wo_ref, q_ref, *refs):
    kv_refs, refs = refs[:group], refs[group:]
    lse_ref, a_ref, refs = refs[0], refs[1], refs[2:]
    dkv_refs, dq_ref, dwo_refs, (scr_ref, wo_scr) = (
        refs[:group],
        refs[group],
        refs[group + 1 : -2],
        refs[-2:],
    )
    chunks, size, width = q_ref.shape
    heads = width // HEAD_DIM
    grad_all_rows = dot(low_ref[...], wo_ref[...], 1, 1).astype(bf16)
    for chunk in range(chunks - 1, -1, -1):
        count = (chunk + 1) * size
        keys = jnp.concatenate([r[0, : chunk + 1].reshape(count, width) for r in kv_refs], 0)
        values = jnp.concatenate([r[1, : chunk + 1].reshape(count, width) for r in kv_refs], 0)
        keys_t = keys.T
        query = by_head(q_ref[chunk])
        grad = by_head(grad_all_rows[chunk * size : (chunk + 1) * size])
        probs = jnp.exp(dot(keys, query, 1, 1) - lse_ref[chunk : chunk + 1])
        grad_probs = dot(values, grad, 1, 1)
        delta = jnp.sum(probs * grad_probs, 0, keepdims=True)
        grad_scores = (probs * (grad_probs - delta)).astype(bf16)
        turned = dot(keys_t, grad_scores)
        parts = [
            turned[head * HEAD_DIM : (head + 1) * HEAD_DIM, head * size : (head + 1) * size]
            for head in range(heads)
        ]
        dq_ref[chunk * size : (chunk + 1) * size] = (
            jnp.concatenate(parts, 0).T * score_scale
        ).astype(bf16)
        both = (dot(grad_scores, query), dot(probs.astype(bf16), grad))
        for slot in range(group):
            for k in range(2):
                value = both[k][slot * count : (slot + 1) * count].reshape(chunk + 1, size, width)
                if chunk == chunks - 1:
                    scr_ref[slot, k] = value
                else:
                    scr_ref[slot, k, : chunk + 1] = scr_ref[slot, k, : chunk + 1] + value
    for slot in range(group - 1, -1, -1):
        dkv_refs[slot][...] = scr_ref[slot].astype(dkv_refs[slot].dtype)
        dkv_refs[slot].flush()
    dq_ref.flush()
    wo_scr[...] = dot(a_ref[...], low_ref[...], 0, 0).reshape(wo_scr.shape)
    for slot in range(group - 1, -1, -1):
        owner = lax.rem(where_am_i(group)[2] + slot, group)
        for plane in range(wo_scr.shape[0]):
            dwo_refs[slot][plane] = wo_scr[plane, owner].astype(dwo_refs[slot].dtype)


def first_kernel(group, ranks, dq_ref, *refs):
    dkv_refs, refs = refs[:group], refs[group:]
    w_ref, sel_ref, refs = refs[0], refs[1], refs[2:]
    dwo_refs, refs = refs[:group], refs[group:]
    proj_ref, refs = refs[0], refs[1:]
    dh_refs, (dh_ref, mix_ref, late_ref) = refs[:ranks], refs[ranks:]
    tokens, width = dq_ref.shape
    model = sel_ref.shape[1]
    size = tokens // ranks
    low = [dq_ref[...]]
    for k in range(2):
        total = dkv_refs[0][k]
        for ref in dkv_refs[1:]:
            total = total + ref[k].astype(f32)
        low.append(total.reshape(tokens, width).astype(bf16))
    mixed = jnp.concatenate(low, 1)
    mix_ref[...] = mixed
    mix_ref.flush()
    below = dot(mixed, w_ref[:, : 3 * width], 1, 1).astype(bf16)
    dh_ref[...] = dot(below, one_hot(sel_ref, model)).astype(bf16).reshape(ranks, size, model)
    for k, ref in enumerate(dh_refs):
        ref[...] = dh_ref[lax.rem(where_am_i(group)[0] + k, ranks)]
        ref.flush()
    dh_ref.flush()
    total = dwo_refs[0][...]
    for ref in dwo_refs[1:]:
        total = total + ref[...].astype(f32)
    hid_rows = proj_ref.shape[1]
    rest = late_ref.shape[1] - hid_rows - total.shape[1]
    for plane in range(total.shape[0]):
        late_ref[plane, :hid_rows] = proj_ref[plane]
        late_ref[plane, hid_rows:] = jnp.concatenate(
            [total[plane], jnp.zeros((rest, model), f32)], 0
        ).astype(bf16)


def first_grad_kernel(
    group, h_ref, mix_ref, x_ref, dh_ref, sums_ref, fcb_ref, mask_ref, sel_ref, bsel_ref, *refs
):
    ranks, size, model = dh_ref.shape
    width = mix_ref.shape[1] // 3
    part = fcb_ref.shape[1]
    mixed = mix_ref[...]
    whole = dot(h_ref[...], mixed, 0, 0)
    normal, _ = norm_parts(x_ref[...].astype(f32))
    grad = dh_ref[...].reshape(ranks * size, model).astype(f32)
    vec = jnp.concatenate(
        [
            jnp.sum(grad * normal, 0, keepdims=True),
            jnp.sum(grad, 0, keepdims=True),
            sums_ref[0:4],
            jnp.zeros((2, model), f32),
        ],
        0,
    )
    cols = jnp.sum(mixed.astype(f32), 0, keepdims=True)
    both = jnp.concatenate([cols[:, :width], cols[:, 2 * width :]], 1)
    sums = jnp.concatenate([fcb_ref[0:1], both], 1) * mask_ref[...]
    small = dot(one_hot(sel_ref, model), vec.astype(bf16), 1, 1)
    more = dot(one_hot(bsel_ref, model), sums.astype(bf16), 1, 1)
    rest = jnp.zeros((model, SMALL - 24), f32)
    whole = jnp.concatenate([whole, small, more, rest], 1)
    rows = model // group
    for slot in range(group - 1, -1, -1):
        refs[slot][...] = whole[slot * rows : (slot + 1) * rows].astype(refs[slot].dtype)
        refs[slot].flush()


def add_early_kernel(group, *refs):
    parts, out_ref = refs[:group], refs[group]
    total = parts[0][...]
    for ref in parts[1:]:
        total = total + ref[...].astype(f32)
    out_ref[...] = total.reshape(out_ref.shape).astype(bf16)


def last_kernel(ranks, *refs):
    parts, (x_ref, vec_ref, dr_ref, out_ref) = refs[:ranks], refs[ranks:]
    normal, scale = norm_parts(x_ref[...].astype(f32))
    grad = parts[0][...].astype(f32)
    for ref in parts[1:]:
        grad = grad + ref[...].astype(f32)
    out_ref[...] = (dr_ref[...] + norm_back(normal, scale, vec_ref[0:1], grad)).astype(bf16)


def by_block(ties, parts, tie_of):
    totals = [jnp.zeros(parts[0].shape, f32) for _ in range(ties)]
    for seq, part in enumerate(parts):
        value = part.astype(f32)
        for block in range(ties):
            totals[block] = totals[block] + jnp.where(tie_of(seq) == block, value, 0.0)
    return totals


def final_late_kernel(ranks, *refs):
    tie_of = lambda seq: refs[0][seq]
    fc_in, rest_in, fc_ref, proj_ref, out_ref = refs[1:]
    ties, _, inner = fc_ref.shape
    planes = rest_in.shape[0]
    hid_rows, rows = proj_ref.shape[1], out_ref.shape[1]
    part = inner // ranks
    for block, total in enumerate(by_block(ties, [rest_in[k] for k in range(planes)], tie_of)):
        proj_ref[block] = total[:hid_rows]
        out_ref[block] = total[hid_rows : hid_rows + rows]
    proj_ref.flush()
    for rank in range(ranks):
        parts = [fc_in[rank * planes + k] for k in range(planes)]
        for block, total in enumerate(by_block(ties, parts, tie_of)):
            fc_ref[block, :, rank * part : (rank + 1) * part] = total


def final_kernel(ranks, *refs):
    tie_of = lambda seq: refs[0][seq]
    home_ref, qkv_ref, *small_refs = refs[1:]
    ties, rows, wide = qkv_ref.shape
    model = wide // 3
    planes = home_ref.shape[0] // ranks
    width = model // ranks
    sums = []
    for rank in range(ranks):
        parts = [home_ref[rank * planes + k] for k in range(planes)]
        sums.append(by_block(ties, parts, tie_of))
    eye = lax.broadcasted_iota(jnp.int32, (SMALL, SMALL), 0)
    eye = jnp.where(eye == lax.broadcasted_iota(jnp.int32, (SMALL, SMALL), 1), 1.0, 0.0)
    eye = eye.astype(bf16)
    for block in range(ties):
        values = [sums[rank][block] for rank in range(ranks)]
        qkv_ref[block] = jnp.concatenate(
            [value[:, k * width : (k + 1) * width] for k in range(3) for value in values], 1
        )
        small = values[0][:, 3 * width :]
        for value in values[1:]:
            small = small + value[:, 3 * width :]
        high = small.astype(bf16)
        low = (small - high.astype(f32)).astype(bf16)
        turned = dot(eye, high, 1, 1) + dot(eye, low, 1, 1)
        for k in range(6):
            small_refs[k][block : block + 1] = turned[k : k + 1]
        small_refs[6][block : block + 1] = jnp.concatenate(
            [turned[k : k + 1] for k in range(14, 16)], 1
        )
        small_refs[7][block : block + 1] = jnp.concatenate(
            [turned[k : k + 1] for k in range(16, 20)], 1
        )


def fast_device(
    n_dp,
    n_seq,
    tokens,
    tie_index,
    first_gain,
    first_shift,
    qkv_weight,
    qv_bias,
    out_weight,
    out_bias,
    second_gain,
    second_shift,
    fc_weight,
    fc_bias,
    proj_weight,
    proj_bias,
    cotangent,
):
    ranks, planes, group = n_dp, n_dp, n_seq // n_dp
    axes = ("dp", "seq")
    size, model = tokens.shape[1:]
    ties, rows = qkv_weight.shape[:2]
    hid_rows = proj_weight.shape[1]
    inner = fc_weight.shape[2]
    width = model // ranks
    part = inner // ranks
    count = ranks * size
    lanes = 3 * width + SMALL
    heads_here = width // HEAD_DIM
    squads = ranks * planes
    rank = lax.axis_index("dp")
    place = lax.axis_index("seq")
    plane, member = place // group, place % group

    def route(where):
        pairs = []
        for a in range(ranks):
            for b in range(planes):
                for c in range(group):
                    x, y, z = where(a, b, c)
                    pairs.append((a * n_seq + b * group + c, x * n_seq + y * group + z))
        return pairs

    swap = route(lambda a, b, c: (b, a, c))
    to_rank = [route(lambda a, b, c, k=k: ((a + k) % ranks, b, c)) for k in range(ranks)]
    to_plane = [route(lambda a, b, c, k=k: (a, (b + k) % planes, c)) for k in range(planes)]
    to_member = [route(lambda a, b, c, k=k: (a, b, (c + k) % group)) for k in range(group)]
    same_member = [[b * group + c for b in range(planes)] for c in range(group)]
    squad = [
        [a * n_seq + b * group + c for a in range(ranks) for b in range(planes)]
        for c in range(group)
    ]

    def send(values, pairs):
        return lax.ppermute(values, axes, pairs)

    def from_members(piece):
        return [piece] + [send(piece, to_member[group - k]) for k in range(1, group)]

    def over_members(parts):
        return [parts[0]] + [send(parts[k], to_member[k]) for k in range(1, group)]

    def over_planes(pieces):
        return lax.all_to_all(pieces, "seq", 0, 0, axis_index_groups=same_member)

    def over_squad(pieces):
        return lax.all_to_all(pieces, axes, 0, 0, axis_index_groups=squad)

    def scatter(parts):
        return [parts[0]] + [send(parts[k], to_rank[k]) for k in range(1, ranks)]

    def gate(value, *before):
        return lax.optimization_barrier((value, before))[0]

    ties_seen = [tie_index] + [send(tie_index, to_rank[ranks - k]) for k in range(1, ranks)]
    scalar_ties = tuple(range(ranks))
    tokens_own = send(tokens[0], swap)

    cols_rows = (rows + 15) // 16 * 16
    early, cols, all_ties = run(
        functools.partial(pack_kernel, group, ranks),
        [
            ((squads, rows, lanes), bf16),
            ((planes, cols_rows, model), bf16),
            ((planes,), jnp.int32),
        ],
        *ties_seen,
        qkv_weight,
        out_weight,
        first_gain,
        first_shift,
        out_bias,
        second_gain,
        second_shift,
        proj_bias,
        qv_bias,
        fc_bias,
        scalars=scalar_ties,
        scalar_out=True,
        scratch=[pltpu.VMEM((ties, ranks, rows, lanes), bf16)],
        us=0.1,
        name="pack",
    )
    packed = early
    early = over_squad(early)

    def arrival(owner, row):
        a, b, c = owner // n_seq, (owner % n_seq) // group, owner % group
        slot = (c + group - member) % group
        return (slot * squads + a * planes + b) * rows + row

    flat = jnp.arange(model)
    at_model = arrival(flat // rows, flat % rows)
    unit = jnp.arange(part) + rank * part
    at_fc = arrival(unit // (4 * rows), unit % rows)
    flat_qv = jnp.arange(2 * width)
    unit_qv = (flat_qv // width) * model + rank * width + flat_qv % width
    at_qv = arrival(unit_qv // (2 * rows), unit_qv % rows)
    at_bias = jnp.concatenate([at_fc, at_qv])
    lanes_of = jnp.concatenate(
        [
            (jnp.arange(part) % (4 * rows)) // rows + 8,
            (unit_qv % (2 * rows)) // rows + 6,
        ]
    )
    sel = at_model[None].astype(jnp.int32)
    bsel = at_bias[None].astype(jnp.int32)
    row_mask = (jnp.arange(16)[:, None] == lanes_of[None, :]).astype(f32)

    tokens_all = lax.all_gather(tokens_own, "dp", axis=0, tiled=True)
    early = gate(early, tokens_all, sel, bsel, row_mask)
    cols = over_planes(gate(cols, early))
    late_rows = hid_rows + cols_rows
    early = from_members(early)
    own = ((size, model), bf16)
    q, kv, h_one, vec, fcb, w_early = run(
        functools.partial(project_kernel, group),
        [
            ((ranks, size, width), bf16),
            ((2, ranks, size, width), bf16),
            ((count, model), bf16),
            ((8, model), f32),
            ((8, part), f32),
            ((model, lanes), bf16),
        ],
        tokens_all,
        *early,
        sel,
        bsel,
        row_mask,
        room=20,
        us=5.0,
        name="project",
    )
    grad_own = send(gate(cotangent[0], tokens_all), swap)
    late_fc, late_proj = run(
        functools.partial(pack_late_kernel, ranks),
        [((squads, rows, part), bf16), ((planes, hid_rows, model), bf16)],
        all_ties,
        gate(fc_weight, q),
        proj_weight,
        scalars=(0,),
        us=2.0,
        name="pack_late",
    )
    cols = from_members(gate(cols, q, late_fc))
    late_fc = over_squad(gate(late_fc, grad_own, cols))
    kv = from_members(gate(kv, grad_own))
    grads_seen = [grad_own] + [send(grad_own, to_rank[ranks - k]) for k in range(1, ranks)]
    attended, lse, w_out, *sums = run(
        functools.partial(attend_kernel, group, rows),
        [((count, width), bf16), ((8, heads_here * size), f32), ((width, model), bf16)] + [own] * ranks,
        q,
        *kv,
        *cols,
        scratch=[pltpu.VMEM((width, model), f32), pltpu.VMEM((ranks, size, model), bf16)],
        us=6.0,
        name="attend",
    )
    sums = scatter(sums)
    late_fc = gate(late_fc, attended, grads_seen)
    late_proj = over_planes(gate(late_proj, late_fc))
    late_fc = from_members(late_fc)
    middle, h_own = run(
        functools.partial(join_kernel, ranks),
        [((size, model), f32), own],
        *sums,
        tokens_own,
        gate(vec, grads_seen),
        sel,
        room=16,
        us=2.0,
        name="join",
    )
    late_proj = from_members(gate(late_proj, h_own))
    h_two = lax.all_gather(h_own, "dp", axis=0, tiled=True)
    rest = run(
        functools.partial(mlp_kernel, group, ranks),
        [own] * ranks
        + [((ranks, size, model), bf16), ((count, model), bf16)]
        + [((count, part), bf16)] * 2,
        h_two,
        *late_fc,
        fcb,
        *grads_seen,
        *late_proj,
        sel,
        scratch=[
            pltpu.VMEM((model, part), bf16),
            pltpu.VMEM((part, model), bf16),
            pltpu.VMEM((ranks, size, model), bf16),
        ],
        us=7.0,
        name="mlp",
    )
    below, (layer_parts, grad_all, hidden, grad_pre) = rest[:ranks], rest[ranks:]
    below = scatter(below)
    half = 2 * (model // group)
    *late, fc_sums = run(
        functools.partial(mlp_grad_kernel, group, planes),
        [((half, model), f32)]
        + [((half, model), bf16)] * (group - 1)
        + [((8, part), f32)],
        h_two,
        grad_pre,
        hidden,
        grad_all,
        scratch=[pltpu.VMEM((part, model), f32)],
        us=4.0,
        name="mlp_grad",
    )
    late = over_members(late)
    grad_middle, low_own, own_sums = run(
        functools.partial(join_back_kernel, ranks),
        [((size, model), f32), own, ((8, model), f32)],
        *below,
        middle,
        grad_own,
        vec,
        room=16,
        us=30.0,
        name="join_back",
    )
    late = gate(late, low_own)
    late_fc, late_proj = run(
        functools.partial(add_late_kernel, group),
        [((squads, rows, part), bf16), ((planes, hid_rows, model), bf16)],
        *late,
        room=16,
        us=2.0,
        name="add_late",
    )
    low = lax.all_gather(gate(low_own, late_fc), "dp", axis=0, tiled=True)
    late_fc = over_squad(late_fc)
    layer_parts = lax.all_to_all(gate(layer_parts, low, late_fc), "dp", 0, 0)
    (layer_own,) = run(
        layer_kernel,
        [own],
        layer_parts,
        middle,
        vec,
        room=16,
        us=1.0,
        name="layer",
    )
    layer_out = send(layer_own, swap)
    rest = run(
        functools.partial(attend_back_kernel, group),
        [((2, ranks, size, width), f32)]
        + [((2, ranks, size, width), bf16)] * (group - 1)
        + [((count, width), bf16)]
        + [((planes, rows, model), f32)]
        + [((planes, rows, model), bf16)] * (group - 1),
        low,
        w_out,
        q,
        *kv,
        lse,
        attended,
        scratch=[
            pltpu.VMEM((group, 2, ranks, size, width), f32),
            pltpu.VMEM((planes, group, rows, model), f32),
        ],
        us=0.5,
        name="attend_back",
    )
    dkv, dq, dw_out = rest[:group], rest[group], rest[group + 1 :]
    dkv = over_members(dkv)
    dw_out = over_members(dw_out)
    rest = run(
        functools.partial(first_kernel, group, ranks),
        [own] * ranks
        + [
            ((ranks, size, model), bf16),
            ((count, 3 * width), bf16),
            ((planes, late_rows, model), bf16),
        ],
        dq,
        *dkv,
        gate(w_early, layer_own),
        sel,
        *dw_out,
        late_proj,
        us=4.0,
        name="first",
    )
    first_parts, (first_all, mixed, late_rest) = rest[:ranks], rest[ranks:]
    grad_first = scatter(first_parts)
    late_rest = over_planes(gate(late_rest, layer_parts))
    early = run(
        functools.partial(first_grad_kernel, group),
        [((model // group, lanes), f32)]
        + [((model // group, lanes), bf16)] * (group - 1),
        h_one,
        mixed,
        tokens_all,
        first_all,
        own_sums,
        fc_sums,
        row_mask,
        sel,
        bsel,
        us=5.0,
        name="first_grad",
    )
    early = over_members(early)
    (input_own,) = run(
        functools.partial(last_kernel, ranks),
        [own],
        *grad_first,
        tokens_own,
        vec,
        grad_middle,
        room=16,
        us=30.0,
        name="last",
    )
    early = gate(early, input_own, layer_out)
    (early,) = run(
        functools.partial(add_early_kernel, group),
        [((squads, rows, lanes), bf16)],
        *early,
        room=16,
        us=1.0,
        name="add_early",
    )
    input_grad = send(input_own, swap)
    early = over_squad(early)
    grad_fc_weight, grad_proj_weight, grad_out_weight = run(
        functools.partial(final_late_kernel, ranks),
        [((ties, rows, inner), f32), ((ties, hid_rows, model), f32), ((ties, rows, model), f32)],
        all_ties,
        late_fc,
        gate(late_rest, input_own),
        scalars=(0,),
        us=60.0,
        name="final_late",
    )
    early = gate(early, grad_fc_weight)
    grad_qkv_weight, *small = run(
        functools.partial(final_kernel, ranks),
        [((ties, rows, 3 * model), f32)]
        + [((ties, rows), f32)] * 6
        + [((ties, 2 * rows), f32), ((ties, 4 * rows), f32)],
        all_ties,
        early,
        scalars=(0,),
        room=16,
        us=1.0,
        name="final",
    )
    layer_out, input_grad = gate((layer_out, input_grad), grad_qkv_weight)
    return (
        layer_out[None],
        input_grad[None],
        small[0],
        small[1],
        grad_qkv_weight,
        small[6],
        grad_out_weight,
        small[2],
        small[3],
        small[4],
        grad_fc_weight,
        small[7],
        grad_proj_weight,
        small[5],
    )


def pick_device(n_dp, n_seq, *args):
    tokens, qkv_weight, proj_weight = args[0], args[4], args[12]
    size, rows, hid_rows = tokens.shape[1], qkv_weight.shape[1], proj_weight.shape[1]
    group = n_seq // n_dp
    whole_tiles = rows % 8 == 0 and (group * rows) % 16 == 0 and hid_rows % 16 == 0
    one_block = tokens.shape[0] == 1 and group == 2 and size * group == BLOCK
    if whole_tiles and one_block:
        return fast_device(n_dp, n_seq, *args)
    return per_device(*args)


def solution(mesh):
    in_specs = (
        P("dp", "seq", None),
        P("dp"),
        P(None, ("dp", "seq")),
        P(None, ("dp", "seq")),
        P(None, ("dp", "seq"), None),
        P(None, ("dp", "seq")),
        P(None, ("dp", "seq"), None),
        P(None, ("dp", "seq")),
        P(None, ("dp", "seq")),
        P(None, ("dp", "seq")),
        P(None, ("dp", "seq"), None),
        P(None, ("dp", "seq")),
        P(None, ("dp", "seq"), None),
        P(None, ("dp", "seq")),
        P("dp", "seq", None),
    )
    out_specs = (
        P("dp", "seq", None),
        P("dp", "seq", None),
        P(None, ("dp", "seq")),
        P(None, ("dp", "seq")),
        P(None, ("dp", "seq"), None),
        P(None, ("dp", "seq")),
        P(None, ("dp", "seq"), None),
        P(None, ("dp", "seq")),
        P(None, ("dp", "seq")),
        P(None, ("dp", "seq")),
        P(None, ("dp", "seq"), None),
        P(None, ("dp", "seq")),
        P(None, ("dp", "seq"), None),
        P(None, ("dp", "seq")),
    )
    return jax.shard_map(
        functools.partial(pick_device, mesh.shape["dp"], mesh.shape["seq"]),
        mesh=mesh,
        in_specs=in_specs,
        out_specs=out_specs,
        check_vma=False,
    )
```
